128 devices in a mesh: expert: 32 (over x, z, core), tensor: 4 (over y).
Axes of the slice: x: 4, y: 4, z: 4, core: 2. Of those that a mesh axis runs over, the one named last changes fastest.
Arguments:
- hidden_in: bfloat16 [4096, 2048], P('expert'), may hold values from -6 to 6
- cotangent: bfloat16 [4096, 2048], P('expert'), may hold values from -6 to 6
- segments: int32 [4096], replicated, may hold values from 0 to 3, never falling along the last dimension, each value on 1 to 2048 neighbouring positions
- routes: int32 [4096, 6], P('expert'), may hold values from 0 to 63, all different within a row; in each aligned block of 128 rows (0 to 127, 128 to 255, ...) at most 24 rows name the same one
- attn_norm: float32 [2048], P('expert'), may hold values from 0.5 to 1.5
- w_query: float32 [2048, 3072], P('expert', 'tensor'), may hold values from -0.125 to 0.125
- w_latent: float32 [2048, 576], P('expert'), may hold values from -0.125 to 0.125
- latent_norm: float32 [512], P('expert'), may hold values from 0.5 to 1.5
- w_expand: float32 [512, 4096], P('expert', 'tensor'), may hold values from -0.25 to 0.25
- w_output: float32 [2048, 2048], P('tensor', 'expert'), may hold values from -0.5 to 0.5
- ffn_norm: float32 [2048], P('expert'), may hold values from 0.5 to 1.5
- w_router: float32 [2048, 64], P('expert'), may hold values from -0.0625 to 0.0625
- shared_gate: float32 [2048, 2816], P('expert', 'tensor'), may hold values from -0.125 to 0.125
- shared_up: float32 [2048, 2816], P('expert', 'tensor'), may hold values from -0.125 to 0.125
- shared_down: float32 [2816, 2048], P('tensor', 'expert'), may hold values from -0.109375 to 0.109375
- expert_gate: float32 [64, 2048, 1408], P('expert', None, 'tensor'), may hold values from -0.125 to 0.125
- routed_expert_up: float32 [64, 2048, 1408], P('expert', None, 'tensor'), may hold values from -0.125 to 0.125
- expert_down: float32 [64, 1408, 2048], P('expert', 'tensor'), may hold values from -0.3125 to 0.3125
Outputs:
- layer_out: bfloat16 [4096, 2048], P('expert')
- grad_in: bfloat16 [4096, 2048], P('expert')
- grad_attn_norm: float32 [2048], P('expert')
- grad_query: float32 [2048, 3072], P('expert', 'tensor')
- grad_latent: float32 [2048, 576], P('expert')
- grad_latent_norm: float32 [512], P('expert')
- grad_expand: float32 [512, 4096], P('expert', 'tensor')
- grad_output: float32 [2048, 2048], P('tensor', 'expert')
- grad_ffn_norm: float32 [2048], P('expert')
- grad_router: float32 [2048, 64], P('expert')
- grad_shared_gate: float32 [2048, 2816], P('expert', 'tensor')
- grad_shared_up: float32 [2048, 2816], P('expert', 'tensor')
- grad_shared_down: float32 [2816, 2048], P('tensor', 'expert')
- grad_expert_gate: float32 [64, 2048, 1408], P('expert', None, 'tensor')
- grad_expert_up: float32 [64, 2048, 1408], P('expert', None, 'tensor')
- grad_expert_down: float32 [64, 1408, 2048], P('expert', 'tensor')
The draws below stay inside these ranges and needn't reach their ends.
Inputs may be any that keep to these rules, and one draw needn't show every extreme that they name: `segments`: document numbers never fall along the tokens; a document has 1 to 2048 tokens, and one has exactly 2048. `routes`: the 6 experts of a token differ. Among the rows of one device (aligned blocks of 128 tokens) no expert is named more than 24 times, a bound that some block reaches.
All inputs are finite; a program needn't handle non-finite values.
Results may differ from the reference program's by a relative error of at most 0.035.
Values may be sent and summed in bfloat16 or wider, within the bound.
A program may use at most 256 MiB of HBM per device.

```python
import math
from functools import partial
import jax
import jax.numpy as jnp
import numpy as np
from jax import lax

D = 2048
H = 16
NOPE = 128
ROPE = 64
VH = 128
RANK = 512
FF = 1408
SHARED = 2816
TOP = 6
WINDOW = 1024
DOC_MAX = 2048
TOK_DEV = 128
TOKENS = 4096
EXPERTS = 64
DOCS = 4
CAP = 24
N_EXPERT = 32


def levels(own_key, dims, split, least, largest):
    def one(axis_at, blocks):
        steps = jax.random.uniform(jax.random.fold_in(jax.random.fold_in(own_key, 6), axis_at), (blocks,), jnp.float32, least / len(split), largest / len(split))
        return jnp.repeat(jnp.exp(steps), dims[axis_at] // blocks).reshape((-1,) + (1,) * (len(dims) - axis_at - 1))

    factor_of = one(*split[0])
    for cut in split[1:]:
        factor_of = factor_of * one(*cut)
    return factor_of


def profile(number_of, total, reach, skew):
    loads = [(1 << 20) // math.isqrt(rank ** skew) + 1 for rank in range(2, number_of + 1)]
    rest, holding = total - reach - (number_of - 1), [1] * (number_of - 1)
    while rest > 0:
        movable = [i for i in range(number_of - 1) if holding[i] < reach]
        pool, left = sum([loads[i] for i in movable]), rest
        for i in movable:
            extra = min(reach - holding[i], max(1, left * loads[i] // pool), rest)
            holding[i] = holding[i] + extra
            rest = rest - extra
    return np.array([reach] + holding)


def uneven(rng, amount, total, most, lean):
    if amount == 2:
        one = jax.random.randint(rng, (), max(1, total - most), min(most, total - 1) + 1)
        return jnp.stack([one, total - one])
    sizes = jnp.asarray(profile(amount, total, most, lean), jnp.int32)
    couples = (amount - 1) // 2
    giver, receiver = sizes[1:1 + 2 * couples:2], sizes[2:2 + 2 * couples:2]
    margin = jnp.minimum(giver - 1, most - receiver)
    shifted = jax.random.randint(jax.random.fold_in(rng, 1), (couples,), 0, 1 << 20) % (margin + 1)
    sizes = sizes.at[1:1 + 2 * couples:2].set(giver - shifted).at[2:2 + 2 * couples:2].set(receiver + shifted)
    return sizes[jax.random.permutation(jax.random.fold_in(rng, 2), amount)]


def routed_block(key, own, number, rows, count, top, limit, skew):
    sequence = jax.random.permutation(key, count)
    heavy_load, usual = shares(count, rows * top, limit, skew, True), shares(count, rows * top, limit, skew, False)
    places = jnp.arange(count)

    def named(tallies, rotation):
        used = int((tallies > 0).sum())
        fixed = max(1, used // 4)
        moved = fixed + (places - fixed + rotation * (used - fixed)) % max(1, count - fixed)
        return jnp.zeros((count,), jnp.int32).at[sequence[jnp.where(places < fixed, places, moved)]].set(jnp.asarray(tallies, jnp.int32))

    tallies = jnp.where(number % 4 == 0, named(heavy_load, number // 4), named(usual, number - number // 4 - 1))
    mixed = jax.random.permutation(jax.random.fold_in(own, 3), count)
    donor, taker = mixed[0:count // 2 * 2:2], mixed[1:count // 2 * 2:2]
    margin = jnp.minimum(tallies[donor] - 1, limit - tallies[taker]) // 2
    margin = jnp.where((donor == sequence[0]) | (taker == sequence[0]) | (tallies[taker] == 0), 0, jnp.maximum(margin, 0))
    moved = jax.random.randint(jax.random.fold_in(own, 4), (count // 2,), 0, 1 << 20) % (margin + 1)
    tallies = tallies.at[donor].add(-moved).at[taker].add(moved)
    labels = jnp.searchsorted(jnp.cumsum(tallies), jnp.arange(rows * top), side="right").astype(jnp.int32)
    listing = labels.reshape(top, rows).T
    listing = listing[jax.random.permutation(jax.random.fold_in(own, 1), rows)]
    rotation = jax.random.randint(jax.random.fold_in(own, 2), (rows, 1), 0, top)
    return jnp.take_along_axis(listing, (jnp.arange(top)[None, :] + rotation) % top, axis=1)


def shares(count, total, bound, slope, full):
    weights = [(1 << 20) // math.isqrt(rank ** slope) + 1 for rank in range(1, count + 1)]
    largest = bound if full else min(bound, max(-(-total // count), total * weights[0] // sum(weights)))
    least = 1 if total - largest >= count - 1 else 0
    holding, surplus = [largest] + [least] * (count - 1), total - largest - least * (count - 1)
    while surplus > 0:
        movable = [i for i in range(1, count) if holding[i] < largest] or [i for i in range(1, count) if holding[i] < bound]
        pool, left = sum([weights[i] for i in movable]), surplus
        for i in movable:
            more = min(bound - holding[i], max(1, left * weights[i] // pool), surplus)
            holding[i] = holding[i] + more
            surplus = surplus - more
    return np.array(holding)


def scatter_about(stream_key, extent, spread, reach, cuts=(), kind=jnp.bfloat16):
    level = levels(stream_key, extent, cuts, -0.22, 0.18) if cuts else 1.0
    drawn = jax.random.normal(stream_key, extent, jnp.float32) * spread * level
    return jnp.minimum(jnp.maximum(drawn, -reach), reach).astype(kind)


def setup_inputs(seed: int = 0) -> dict:
    key_of = jax.random.split(jax.random.key(seed), 19)
    hidden_in = scatter_about(key_of[0], (TOKENS, D), 1.0, 6.0, ((0, 32),))
    cotangent = scatter_about(key_of[1], (TOKENS, D), 1.0, 6.0, ((0, 32),))
    segments = jnp.searchsorted(jnp.cumsum(uneven(key_of[2], DOCS, TOKENS, DOC_MAX, 0)), jnp.arange(TOKENS), side="right").astype(jnp.int32)
    routes_keys = jax.random.split(jax.random.fold_in(key_of[3], 1), TOKENS // TOK_DEV)
    routes_turns = jax.random.permutation(jax.random.fold_in(key_of[3], 3), TOKENS // TOK_DEV)
    routes = jax.vmap(lambda own, number: routed_block(jax.random.fold_in(key_of[3], 2), own, number, TOK_DEV, EXPERTS, TOP, CAP, 2))(routes_keys, routes_turns).reshape((TOKENS, TOP))
    attn_norm = jnp.clip(1.0 + 0.1 * jax.random.normal(key_of[4], (D,), jnp.float32), 0.5, 1.5)
    w_query = scatter_about(key_of[5], (D, H * (NOPE + ROPE)), D ** -0.5, 0.125, ((0, 32), (1, 4)), jnp.float32)
    w_latent = scatter_about(key_of[6], (D, RANK + ROPE), D ** -0.5, 0.125, ((0, 32),), jnp.float32)
    latent_norm = jnp.clip(1.0 + 0.1 * jax.random.normal(key_of[7], (RANK,), jnp.float32), 0.5, 1.5)
    w_expand = scatter_about(key_of[8], (RANK, H * (NOPE + VH)), RANK ** -0.5, 0.25, ((0, 32), (1, 4)), jnp.float32)
    w_output = scatter_about(key_of[9], (H * VH, D), VH ** -0.5, 0.5, ((0, 4), (1, 32)), jnp.float32)
    ffn_norm = jnp.clip(1.0 + 0.1 * jax.random.normal(key_of[10], (D,), jnp.float32), 0.5, 1.5)
    w_router = scatter_about(key_of[11], (D, EXPERTS), (4 * D) ** -0.5, 0.0625, ((0, 32),), jnp.float32)
    shared_gate = scatter_about(key_of[12], (D, SHARED), D ** -0.5, 0.125, ((0, 32), (1, 4)), jnp.float32)
    shared_up = scatter_about(key_of[13], (D, SHARED), D ** -0.5, 0.125, ((0, 32), (1, 4)), jnp.float32)
    shared_down = scatter_about(key_of[14], (SHARED, D), SHARED ** -0.5, 0.109375, ((0, 4), (1, 32)), jnp.float32)
    expert_gate = scatter_about(key_of[15], (EXPERTS, D, FF), D ** -0.5, 0.125, ((0, 32), (2, 4)), jnp.float32)
    routed_expert_up = scatter_about(key_of[16], (EXPERTS, D, FF), D ** -0.5, 0.125, ((0, 32), (2, 4)), jnp.float32)
    expert_down = scatter_about(key_of[17], (EXPERTS, FF, D), (FF // 4) ** -0.5, 0.3125, ((0, 32), (1, 4)), jnp.float32)
    return {"hidden_in": hidden_in, "cotangent": cotangent, "segments": segments, "routes": routes, "attn_norm": attn_norm, "w_query": w_query, "w_latent": w_latent, "latent_norm": latent_norm, "w_expand": w_expand, "w_output": w_output, "ffn_norm": ffn_norm, "w_router": w_router, "shared_gate": shared_gate, "shared_up": shared_up, "shared_down": shared_down, "expert_gate": expert_gate, "routed_expert_up": routed_expert_up, "expert_down": expert_down}


@jax.custom_vjp
def low(v):
    return lax.optimization_barrier(v.astype(jnp.bfloat16)).astype(jnp.float32)

@jax.custom_vjp
def low_back(v):
    return v

def low_keep(v):
    return (low(v), None)

def low_pass(kept, grad):
    return (grad,)

def back_keep(v):
    return (v, None)

def back_low(kept, grad):
    return (low(grad),)
low.defvjp(low_keep, low_pass)
low_back.defvjp(back_keep, back_low)
HIGHEST_PREC = lax.Precision.HIGHEST
epsilon = 1e-06
masked_score = -1e+30
rope_base = 10000.0

def matmul(left_side, right_side):
    return jnp.dot(left_side, right_side, precision=HIGHEST_PREC, preferred_element_type=jnp.float32)

def rms_norm(values, gains):
    return values * lax.rsqrt(lax.optimization_barrier(jnp.mean(values * values, -1, keepdims=True)) + epsilon) * gains

def rope_tables(positions):
    half_dim = ROPE // 2
    freqs = rope_base ** (-jnp.arange(half_dim, dtype=jnp.float32) / half_dim)
    angles = positions.astype(jnp.float32)[:, None] * freqs[None, :]
    return (jnp.cos(angles), jnp.sin(angles))

def rotate(values, cosine, sine_tab):
    half_dim = values.shape[-1] // 2
    first_half = values[..., :half_dim]
    second_half = values[..., half_dim:]
    return jnp.concatenate([first_half * cosine - second_half * sine_tab, second_half * cosine + first_half * sine_tab], -1)

def slot_targets(routes):
    blocks = routes.reshape(N_EXPERT, TOK_DEV * TOP)
    onehot = (blocks[:, :, None] == jnp.arange(EXPERTS, dtype=jnp.int32)[None, None, :]).astype(jnp.int32)
    ranks = lax.optimization_barrier(jnp.sum(jnp.cumsum(onehot, 1) * onehot, -1)) - 1
    block_ids = jnp.arange(N_EXPERT, dtype=jnp.int32)[:, None]
    return (blocks * (N_EXPERT * CAP) + block_ids * CAP + ranks).reshape(-1).astype(jnp.int32)

def layer(segments, routes, hidden_f, attn_norm, w_query, w_latent, latent_norm, w_expand, w_output, ffn_norm, w_router, shared_gate, shared_up, shared_down, expert_gate, routed_expert_up, expert_down):
    token_total = hidden_f.shape[0]
    positions_all = jnp.arange(token_total, dtype=jnp.int32)
    starts = jnp.searchsorted(segments, segments, side='left').astype(jnp.int32)
    cosine, sine_tab = rope_tables(positions_all - starts)
    normed = low(rms_norm(hidden_f, low(attn_norm)))
    query_pre = low_back(matmul(normed, low(w_query))).reshape(token_total, H, NOPE + ROPE)
    queries = low(jnp.concatenate([query_pre[..., :NOPE], rotate(query_pre[..., NOPE:], cosine[:, None, :], sine_tab[:, None, :])], -1))
    latent = low_back(matmul(normed, low(w_latent)))
    compressed = low(rms_norm(latent[:, :RANK], low(latent_norm)))
    key_rope = low(rotate(latent[:, RANK:], cosine, sine_tab))
    expanded = low_back(low(matmul(compressed, low(w_expand)))).reshape(token_total, H, NOPE + VH)
    block_rows = min(512, token_total)
    nope_pad = jnp.pad(expanded[..., :NOPE], ((WINDOW, 0), (0, 0), (0, 0)))
    value_pad = jnp.pad(expanded[..., NOPE:], ((WINDOW, 0), (0, 0), (0, 0)))
    rope_pad = jnp.pad(key_rope, ((WINDOW, 0), (0, 0)))
    segment_pad = jnp.pad(segments, (WINDOW, 0), constant_values=-1)
    score_scale = (NOPE + ROPE) ** (-0.5)

    def attend(block_start):
        query_block = lax.dynamic_slice_in_dim(queries, block_start, block_rows, 0)
        nope_keys = lax.dynamic_slice_in_dim(nope_pad, block_start, block_rows + WINDOW, 0)
        value_keys = lax.dynamic_slice_in_dim(value_pad, block_start, block_rows + WINDOW, 0)
        rope_keys = lax.dynamic_slice_in_dim(rope_pad, block_start, block_rows + WINDOW, 0)
        key_segments = lax.dynamic_slice_in_dim(segment_pad, block_start, block_rows + WINDOW, 0)
        query_segments = lax.dynamic_slice_in_dim(segments, block_start, block_rows, 0)
        query_pos = block_start + jnp.arange(block_rows, dtype=jnp.int32)
        key_pos = block_start - WINDOW + jnp.arange(block_rows + WINDOW, dtype=jnp.int32)
        distance = query_pos[:, None] - key_pos[None, :]
        allowed = (distance >= 0) & (distance < WINDOW) & (query_segments[:, None] == key_segments[None, :])
        nope_part = jnp.einsum('qhd,khd->hqk', query_block[..., :NOPE], nope_keys, precision=HIGHEST_PREC)
        rope_part = jnp.einsum('qhr,kr->hqk', query_block[..., NOPE:], rope_keys, precision=HIGHEST_PREC)
        scores = low_back((nope_part + rope_part) * score_scale)
        masked = jnp.where(allowed[None], scores, masked_score)
        row_max = lax.optimization_barrier(jnp.max(masked, -1, keepdims=True))
        exponent = jnp.exp(masked - row_max)
        probabilities = low(exponent / lax.optimization_barrier(jnp.sum(exponent, -1, keepdims=True)))
        return jnp.einsum('hqk,khd->qhd', probabilities, value_keys, precision=HIGHEST_PREC)
    block_starts = jnp.arange(token_total // block_rows, dtype=jnp.int32) * block_rows
    mixed = lax.map(jax.checkpoint(attend), block_starts).reshape(token_total, H * VH)
    attended = low_back(low(mixed))
    middle = hidden_f + low_back(matmul(attended, low(w_output)))
    normed_two = low(rms_norm(middle, low(ffn_norm)))
    logits = matmul(normed_two, low(w_router))
    chosen = jnp.take_along_axis(logits, routes, 1)
    gate_weights = jax.nn.softmax(chosen, -1)
    shared_gate_pre = low_back(matmul(normed_two, low(shared_gate)))
    shared_up_pre = low_back(matmul(normed_two, low(shared_up)))
    shared_out = low_back(matmul(low(jax.nn.silu(shared_gate_pre) * shared_up_pre), low(shared_down)))
    targets = slot_targets(routes)
    token_of = jnp.arange(token_total * TOP, dtype=jnp.int32) // TOP
    slot_buffer = jnp.zeros((EXPERTS * N_EXPERT * CAP, D), jnp.float32).at[targets].set(normed_two[token_of])
    slot_buffer = low_back(slot_buffer).reshape(EXPERTS, N_EXPERT * CAP, D)

    def expert(pieces):
        slot_rows, weight_gate, weight_up, weight_down = pieces
        gate_pre = low_back(matmul(slot_rows, low(weight_gate)))
        up_pre = low_back(matmul(slot_rows, low(weight_up)))
        return low_back(low(matmul(low(jax.nn.silu(gate_pre) * up_pre), low(weight_down))))
    outputs = lax.map(jax.checkpoint(expert), (slot_buffer, expert_gate, routed_expert_up, expert_down)).reshape(-1, D)
    picked = outputs[targets].reshape(token_total, TOP, D)
    routed = lax.optimization_barrier(jnp.sum(gate_weights[..., None] * picked, 1))
    return middle + routed + shared_out

def reference(hidden_in, cotangent, segments, routes, attn_norm, w_query, w_latent, latent_norm, w_expand, w_output, ffn_norm, w_router, shared_gate, shared_up, shared_down, expert_gate, routed_expert_up, expert_down):
    output, pull = jax.vjp(partial(layer, segments, routes), hidden_in.astype(jnp.float32), attn_norm, w_query, w_latent, latent_norm, w_expand, w_output, ffn_norm, w_router, shared_gate, shared_up, shared_down, expert_gate, routed_expert_up, expert_down)
    grads = pull(cotangent.astype(jnp.float32))
    return (output.astype(jnp.bfloat16), grads[0].astype(jnp.bfloat16), grads[1], grads[2], grads[3], grads[4], grads[5], grads[6], grads[7], grads[8], grads[9], grads[10], grads[11], grads[12], grads[13], grads[14])
```

```python
import functools

import jax
import jax.numpy as jnp
from jax import lax
from jax.experimental import pallas as pl
from jax.experimental.pallas import tpu as pltpu
from jax.sharding import PartitionSpec as P

NOPE = 128
ROPE = 64
VH = 128
RANK = 512
WINDOW = 1024


epsilon = 1e-06
masked_score = -1e30
rope_base = 10000.0


MESH = pl.DeviceIdType.MESH
HBM = pl.BlockSpec(memory_space=pltpu.HBM)


def place():
    e = lax.axis_index("expert")
    return lax.axis_index("tensor"), e // 8, lax.rem(e // 2, 4), lax.rem(e, 2)


def at(x, z, c):
    return (x * 4 + z) * 2 + c


def wrap(v):
    return lax.rem(v + 4, 4)


def greet(peers):
    barrier = pltpu.get_barrier_semaphore()
    for peer in peers:
        pl.semaphore_signal(barrier, inc=1, device_id=peer, device_id_type=MESH)
    pl.semaphore_wait(barrier, len(peers))


def plane_gather_kernel(src, out, ssem, rsem, dssem, drsem, lsem):
    t, x, z, c = place()
    rows = src.shape[0]
    half, quarter = rows // 2, rows // 4
    sibling = (at(x, z, 1 - c), t)
    along_x = [(at(wrap(x - 1), z, c), t), (at(wrap(x + 1), z, c), t)]
    along_z = [(at(x, wrap(z - 1), c), t), (at(x, wrap(z + 1), c), t)]
    greet([sibling] + along_x + along_z)
    own = pltpu.make_async_copy(src, out.at[at(x, z, c)], lsem)
    own.start()
    sent = []

    def piece(h, j1, j2, part=None):
        if h == 0:
            index = at(wrap(x + j2), wrap(z + j1), c)
        else:
            index = at(wrap(x + j1), wrap(z + j2), c)
        if part is None:
            return index, pl.ds(h * half, half)
        return index, pl.ds(h * half + part * quarter, quarter)

    def send(h, slot, which, device, first):
        index, rows_of = which
        return pltpu.make_async_remote_copy(
            src_ref=src.at[rows_of] if first else out.at[index, rows_of],
            dst_ref=out.at[index, rows_of],
            send_sem=ssem.at[h, slot],
            recv_sem=rsem.at[h, slot],
            device_id=device,
            device_id_type=MESH,
        )

    def across(h, j1, j2):
        index, rows_of = piece(h, j1, j2)
        slot = (h * 4 + j1 % 4) * 4 + j2 % 4
        return pltpu.make_async_remote_copy(
            src_ref=src.at[rows_of] if j1 == 0 and j2 == 0 else out.at[index, rows_of],
            dst_ref=out.at[index, rows_of],
            send_sem=dssem.at[slot],
            recv_sem=drsem.at[slot],
            device_id=sibling,
            device_id_type=MESH,
        )

    def ring(h, stage):
        return along_z if (h == 0) == (stage == 1) else along_x

    def stage_one(h, kind):
        left, right = ring(h, 1)
        if kind == 0:
            return send(h, 0, piece(h, 0, 0), right, True)
        if kind == 1:
            return send(h, 1, piece(h, 0, 0), left, True)
        if kind == 2:
            return send(h, 2, piece(h, -1, 0, 0), right, False)
        return send(h, 3, piece(h, 1, 0, 1), left, False)

    def stage_two(h, j1, kind):
        left, right = ring(h, 2)
        slot = 4 + 4 * (j1 % 4) + kind
        if kind == 0:
            return send(h, slot, piece(h, j1, 0), right, j1 == 0)
        if kind == 1:
            return send(h, slot, piece(h, j1, 0), left, j1 == 0)
        if kind == 2:
            return send(h, slot, piece(h, j1, -1, 0), right, False)
        return send(h, slot, piece(h, j1, 1, 1), left, False)

    def go(copy):
        copy.start()
        sent.append(copy)

    for h in (0, 1):
        go(stage_one(h, 0))
        go(stage_one(h, 1))
        go(stage_two(h, 0, 0))
        go(stage_two(h, 0, 1))
        go(across(h, 0, 0))
    for h in (0, 1):
        for kind, j in ((0, -1), (1, 1)):
            stage_one(h, kind).wait_recv()
            go(stage_one(h, 2 + kind))
            go(stage_two(h, j, 0))
            go(stage_two(h, j, 1))
            go(across(h, j, 0))
    for h in (0, 1):
        for kind, j in ((0, -1), (1, 1)):
            stage_two(h, 0, kind).wait_recv()
            go(stage_two(h, 0, 2 + kind))
            go(across(h, 0, j))
    for h in (0, 1):
        stage_one(h, 2).wait_recv()
        stage_one(h, 3).wait_recv()
        go(stage_two(h, 2, 0))
        go(stage_two(h, 2, 1))
        go(across(h, 2, 0))
    for j1 in (-1, 1, 2):
        for h in (0, 1):
            for kind, j in ((0, -1), (1, 1)):
                stage_two(h, j1, kind).wait_recv()
                go(stage_two(h, j1, 2 + kind))
                go(across(h, j1, j))
    for j1 in (0, -1, 1, 2):
        for h in (0, 1):
            stage_two(h, j1, 2).wait_recv()
            stage_two(h, j1, 3).wait_recv()
            go(across(h, j1, 2))
    for h in (0, 1):
        for j1 in (0, -1, 1, 2):
            for j2 in (0, -1, 1, 2):
                across(h, j1, j2).wait_recv()
    for copy in sent:
        copy.wait_send()
    own.wait()


def plane_gather(rows, collective_id, name):
    grouped = rows.reshape(rows.shape[0] // 8, 8, rows.shape[1])
    gathered = pl.pallas_call(
        plane_gather_kernel,
        out_shape=jax.ShapeDtypeStruct((32, *grouped.shape), rows.dtype),
        in_specs=[HBM],
        out_specs=HBM,
        scratch_shapes=[
            pltpu.SemaphoreType.DMA((2, 20)),
            pltpu.SemaphoreType.DMA((2, 20)),
            pltpu.SemaphoreType.DMA((32,)),
            pltpu.SemaphoreType.DMA((32,)),
            pltpu.SemaphoreType.DMA,
        ],
        compiler_params=pltpu.CompilerParams(
            collective_id=collective_id, has_side_effects=True, vmem_limit_bytes=62 * 2**20
        ),
        cost_estimate=pl.CostEstimate(
            flops=0, bytes_accessed=64 * rows.size * rows.dtype.itemsize, transcendentals=0
        ),
        name=name,
    )(grouped)
    return gathered.reshape(32 * rows.shape[0], rows.shape[1])


class Line:
    def __init__(self, src, out, taken, ssem, rsem):
        e, t = lax.axis_index("expert"), lax.axis_index("tensor")
        self.src, self.out, self.taken, self.ssem, self.rsem = src, out, taken, ssem, rsem
        self.share, self.t = src.shape[0] // 4, t
        self.others = [(e, lax.rem(t + k, 4)) for k in (1, 2, 3)]

    def share_out(self, k):
        device = self.others[k - 1]
        return pltpu.make_async_remote_copy(
            src_ref=self.src.at[pl.ds(device[1] * self.share, self.share)],
            dst_ref=self.taken.at[k - 1],
            send_sem=self.ssem.at[0, k - 1],
            recv_sem=self.rsem.at[0, k - 1],
            device_id=device,
            device_id_type=MESH,
        )

    def pass_on(self, k):
        rows = pl.ds(self.t * self.share, self.share)
        return pltpu.make_async_remote_copy(
            src_ref=self.out.at[rows],
            dst_ref=self.out.at[rows],
            send_sem=self.ssem.at[1, k - 1],
            recv_sem=self.rsem.at[1, k - 1],
            device_id=self.others[k - 1],
            device_id_type=MESH,
        )

    def scatter(self):
        for k in (2, 1, 3):
            self.share_out(k).start()

    def add(self):
        for k in (2, 1, 3):
            self.share_out(k).wait_recv()

        def step(i, carry):
            total = self.src[self.t * self.share + i].astype(jnp.float32)
            for k in range(3):
                total = total + self.taken[k, i].astype(jnp.float32)
            self.out[self.t * self.share + i] = total.astype(self.out.dtype)
            return carry

        lax.fori_loop(0, self.share, step, 0)

    def gather(self):
        for k in (2, 1, 3):
            self.pass_on(k).start()

    def finish(self):
        for k in (2, 1, 3):
            self.pass_on(k).wait_recv()
        for k in (2, 1, 3):
            self.share_out(k).wait_send()
            self.pass_on(k).wait_send()


def line_sum_kernel(src, out, taken, ssem, rsem):
    line = Line(src, out, taken, ssem, rsem)
    greet(line.others)
    line.scatter()
    line.add()
    line.gather()
    line.finish()


def plane_sum_kernel(*refs, count, columns, beside):
    sources, refs = refs[:count], refs[count:]
    if beside:
        side_in, out, side_out, side_taken, side_ssem, side_rsem, *refs = refs
    else:
        out, *refs = refs
    mine, peer, one, two, last_one, last_two, lsem, pssem, prsem, ssem, rsem = refs
    t, x, z, c = place()
    groups = out.shape[0]
    half, quarter = groups // 2, groups // 4
    sibling = (at(x, z, 1 - c), t)
    along_x = [(at(wrap(x - 1), z, c), t), (at(wrap(x + 1), z, c), t)]
    along_z = [(at(x, wrap(z - 1), c), t), (at(x, wrap(z + 1), c), t)]
    if beside:
        line = Line(side_in, side_out, side_taken, side_ssem, side_rsem)
        greet([sibling] + along_x + along_z + line.others)
    else:
        greet([sibling] + along_x + along_z)
    order = (2, 1, 3, 0)
    sent = []

    def target(h, a, b, core):
        if h == 0:
            return at(wrap(x + a), wrap(z + b), core)
        return at(wrap(x + b), wrap(z + a), core)

    def outward(h, a, b):
        copies, start = [], 0
        for i, width in enumerate(columns):
            copies.append(
                pltpu.make_async_remote_copy(
                    src_ref=sources[i].at[target(h, a, b, 1 - c), pl.ds(h * half, half)],
                    dst_ref=peer.at[h, a, b, :, :, pl.ds(start, width)],
                    send_sem=pssem.at[i, h, a, b],
                    recv_sem=prsem.at[i, h, a, b],
                    device_id=sibling,
                    device_id_type=MESH,
                )
            )
            start += width
        return copies

    def inward(h, a, b):
        copies, start = [], 0
        for i, width in enumerate(columns):
            copies.append(
                pltpu.make_async_copy(
                    sources[i].at[target(h, a, b, c), pl.ds(h * half, half)],
                    mine.at[h, a, b, :, :, pl.ds(start, width)],
                    lsem.at[i, h, a, b],
                )
            )
            start += width
        return copies

    def hop(h, slot, src, dst, device):
        return pltpu.make_async_remote_copy(
            src_ref=src,
            dst_ref=dst,
            send_sem=ssem.at[h, slot],
            recv_sem=rsem.at[h, slot],
            device_id=device,
            device_id_type=MESH,
        )

    def ring(h, stage):
        return along_x if (h == 0) == (stage == 1) else along_z

    def first(h, b, side):
        return hop(
            h,
            4 * b + side,
            mine.at[h, 2, b, pl.ds(side * quarter, quarter)],
            one.at[h, b, side],
            ring(h, 1)[1 - side],
        )

    def second(h, b, side):
        return hop(
            h, 4 * b + 2 + side, mine.at[h, 1 + 2 * side, b], two.at[h, b, side], ring(h, 1)[1 - side]
        )

    def third(h, side):
        return hop(
            h,
            16 + side,
            mine.at[h, 0, 2, pl.ds(side * quarter, quarter)],
            last_one.at[h, side],
            ring(h, 2)[1 - side],
        )

    def fourth(h, side):
        return hop(
            h, 18 + side, mine.at[h, 0, 1 + 2 * side], last_two.at[h, side], ring(h, 2)[1 - side]
        )

    def go(copy):
        copy.start()
        sent.append(copy)

    def accumulate(into, sources_of, number):
        def step(i, carry):
            total = into[i].astype(jnp.float32)
            for source in sources_of:
                total = total + source[i].astype(jnp.float32)
            into[i] = total.astype(into.dtype)
            return carry

        lax.fori_loop(0, number, step, 0)

    spots = [(h, a, b) for a in order for b in order for h in (0, 1)]
    for spot in spots:
        for copy in inward(*spot):
            copy.start()
        for copy in outward(*spot):
            go(copy)

    if beside:
        line.scatter()

    def merge(h, a, b):
        for copy in inward(h, a, b):
            copy.wait()
        for copy in outward(h, a, b):
            copy.wait_recv()
        accumulate(mine.at[h, a, b], [peer.at[h, a, b]], half)

    for b in order:
        for h in (0, 1):
            merge(h, 2, b)
            for side in (0, 1):
                go(first(h, b, side))
    for side in (0, 1):
        for b in order:
            for h in (0, 1):
                a = 1 + 2 * side
                merge(h, a, b)
                first(h, b, side).wait_recv()
                accumulate(
                    mine.at[h, a, b, pl.ds(side * quarter, quarter)], [one.at[h, b, side]], quarter
                )
                go(second(h, b, side))

    if beside:
        line.add()
        line.gather()

    def gathered_here(h, b):
        merge(h, 0, b)
        for side in (0, 1):
            second(h, b, side).wait_recv()
        accumulate(mine.at[h, 0, b], [two.at[h, b, 0], two.at[h, b, 1]], half)

    for h in (0, 1):
        gathered_here(h, 2)
        for side in (0, 1):
            go(third(h, side))
    for side in (0, 1):
        b = 1 + 2 * side
        for h in (0, 1):
            gathered_here(h, b)
            third(h, side).wait_recv()
            accumulate(
                mine.at[h, 0, b, pl.ds(side * quarter, quarter)], [last_one.at[h, side]], quarter
            )
            go(fourth(h, side))
    for h in (0, 1):
        gathered_here(h, 0)
        for side in (0, 1):
            fourth(h, side).wait_recv()

        def finish(i, carry, h=h):
            total = mine[h, 0, 0, i].astype(jnp.float32)
            for side in (0, 1):
                total = total + last_two[h, side, i].astype(jnp.float32)
            out[h * half + i] = total
            return carry

        lax.fori_loop(0, half, finish, 0)
    for copy in sent:
        copy.wait_send()
    if beside:
        line.finish()


def plane_sum(parts, collective_id, name, beside=None):
    columns = tuple(part.shape[1] for part in parts)
    width = sum(columns)
    groups = parts[0].shape[0] // 256
    half, quarter = groups // 2, groups // 4
    low = jnp.bfloat16
    count = len(parts)
    vmem = pl.BlockSpec(memory_space=pltpu.VMEM)
    operands = [part.reshape(32, groups, 8, part.shape[1]) for part in parts]
    out_shape = [jax.ShapeDtypeStruct((groups, 8, width), jnp.float32)]
    side = []
    if beside is not None:
        lines, side_width = beside.shape
        operands.append(beside.reshape(lines // 8, 8, side_width))
        out_shape.append(jax.ShapeDtypeStruct((lines // 8, 8, side_width), beside.dtype))
        side = [
            pltpu.VMEM((3, lines // 32, 8, side_width), beside.dtype),
            pltpu.SemaphoreType.DMA((2, 3)),
            pltpu.SemaphoreType.DMA((2, 3)),
        ]
    results = pl.pallas_call(
        functools.partial(
            plane_sum_kernel, count=count, columns=columns, beside=beside is not None
        ),
        out_shape=out_shape,
        in_specs=[HBM] * count + [vmem] * (len(operands) - count),
        out_specs=[vmem] * len(out_shape),
        scratch_shapes=side
        + [
            pltpu.VMEM((2, 4, 4, half, 8, width), low),
            pltpu.VMEM((2, 4, 4, half, 8, width), low),
            pltpu.VMEM((2, 4, 2, quarter, 8, width), low),
            pltpu.VMEM((2, 4, 2, half, 8, width), low),
            pltpu.VMEM((2, 2, quarter, 8, width), low),
            pltpu.VMEM((2, 2, half, 8, width), low),
            pltpu.SemaphoreType.DMA((count, 2, 4, 4)),
            pltpu.SemaphoreType.DMA((count, 2, 4, 4)),
            pltpu.SemaphoreType.DMA((count, 2, 4, 4)),
            pltpu.SemaphoreType.DMA((2, 20)),
            pltpu.SemaphoreType.DMA((2, 20)),
        ],
        compiler_params=pltpu.CompilerParams(
            collective_id=collective_id, has_side_effects=True, vmem_limit_bytes=60 * 2**20
        ),
        cost_estimate=pl.CostEstimate(
            flops=0, bytes_accessed=256 * groups * width * 16, transcendentals=0
        ),
        name=name,
    )(*operands)
    summed = results[0].reshape(groups * 8, width)
    if beside is None:
        return summed
    return summed, results[1].reshape(beside.shape)


def line_sum(rows, collective_id, name):
    groups, width = rows.shape[0] // 8, rows.shape[1]
    vmem = pl.BlockSpec(memory_space=pltpu.VMEM)
    summed = pl.pallas_call(
        line_sum_kernel,
        out_shape=jax.ShapeDtypeStruct((groups, 8, width), rows.dtype),
        in_specs=[vmem],
        out_specs=vmem,
        scratch_shapes=[
            pltpu.VMEM((3, groups // 4, 8, width), rows.dtype),
            pltpu.SemaphoreType.DMA((2, 3)),
            pltpu.SemaphoreType.DMA((2, 3)),
        ],
        compiler_params=pltpu.CompilerParams(
            collective_id=collective_id, has_side_effects=True, vmem_limit_bytes=60 * 2**20
        ),
        cost_estimate=pl.CostEstimate(flops=0, bytes_accessed=40 * rows.size, transcendentals=0),
        name=name,
    )(rows.reshape(groups, 8, width))
    return summed.reshape(rows.shape)


def chip_at(x, z, c, distance):
    place_on = lax.rem(x * 4 + z + 16 + distance, 16)
    return place_on * 2 + c


def reach_back_kernel(src, out, lsem, ssem, rsem, pssem, prsem):
    t, x, z, c = place()
    sibling = (at(x, z, 1 - c), t)
    ahead = [(chip_at(x, z, c, k), t) for k in (1, 2, 3, 4)]
    behind = [(chip_at(x, z, c, -k), t) for k in (1, 2, 3, 4)]
    barrier = pltpu.get_barrier_semaphore()
    for peer in [sibling] + behind:
        pl.semaphore_signal(barrier, inc=1, device_id=peer, device_id_type=MESH)
    pl.semaphore_wait(barrier, 5)
    own = pltpu.make_async_copy(src, out.at[8], lsem)
    own.start()

    def far(k):
        return pltpu.make_async_remote_copy(
            src_ref=src,
            dst_ref=out.at[8 - 2 * k],
            send_sem=ssem.at[k - 1],
            recv_sem=rsem.at[k - 1],
            device_id=ahead[k - 1],
            device_id_type=MESH,
        )

    def near(i):
        return pltpu.make_async_remote_copy(
            src_ref=out.at[8 - 2 * (i + c)],
            dst_ref=out.at[7 - 2 * i],
            send_sem=pssem.at[i],
            recv_sem=prsem.at[i],
            device_id=sibling,
            device_id_type=MESH,
        )

    for k in (4, 3, 2, 1):
        far(k).start()
    own.wait()
    for k in (1, 2, 3, 4):
        far(k).wait_recv()
    for i in range(4):
        near(i).start()
    for i in range(4):
        near(i).wait()
    for k in (1, 2, 3, 4):
        far(k).wait_send()


def reach_back(rows, collective_id, name):
    groups, width = rows.shape[0] // 8, rows.shape[1]
    vmem = pl.BlockSpec(memory_space=pltpu.VMEM)
    keys = pl.pallas_call(
        reach_back_kernel,
        out_shape=jax.ShapeDtypeStruct((9, groups, 8, width), rows.dtype),
        in_specs=[vmem],
        out_specs=vmem,
        scratch_shapes=[
            pltpu.SemaphoreType.DMA,
            pltpu.SemaphoreType.DMA((4,)),
            pltpu.SemaphoreType.DMA((4,)),
            pltpu.SemaphoreType.DMA((4,)),
            pltpu.SemaphoreType.DMA((4,)),
        ],
        compiler_params=pltpu.CompilerParams(
            collective_id=collective_id, has_side_effects=True, vmem_limit_bytes=60 * 2**20
        ),
        cost_estimate=pl.CostEstimate(flops=0, bytes_accessed=200 * rows.size, transcendentals=0),
        name=name,
    )(rows.reshape(groups, 8, width))
    return keys.reshape(9 * rows.shape[0], width)


def send_back_kernel(src, out, held, near_in, far_in, lsem, ssem, rsem, pssem, prsem):
    t, x, z, c = place()
    groups = out.shape[0]
    sibling = (at(x, z, 1 - c), t)
    ahead = [(chip_at(x, z, c, k), t) for k in (1, 2, 3, 4)]
    behind = [(chip_at(x, z, c, -k), t) for k in (1, 2, 3, 4)]
    barrier = pltpu.get_barrier_semaphore()
    for peer in [sibling] + ahead:
        pl.semaphore_signal(barrier, inc=1, device_id=peer, device_id_type=MESH)
    pl.semaphore_wait(barrier, 5)

    def near(i):
        return pltpu.make_async_remote_copy(
            src_ref=src.at[7 - 2 * i],
            dst_ref=near_in.at[i],
            send_sem=pssem.at[i],
            recv_sem=prsem.at[i],
            device_id=sibling,
            device_id_type=MESH,
        )

    def far(k):
        return pltpu.make_async_remote_copy(
            src_ref=held.at[k],
            dst_ref=far_in.at[k - 1],
            send_sem=ssem.at[k - 1],
            recv_sem=rsem.at[k - 1],
            device_id=behind[k - 1],
            device_id_type=MESH,
        )

    for i in (3, 2, 1, 0):
        near(i).start()
    for i in (3, 2, 1, 0):
        near(i).wait_recv()
    for k in (4, 3, 2, 1, 0):

        def step(i, carry, k=k):
            total = src[8 - 2 * k, i].astype(jnp.float32)
            other = near_in[jnp.clip(k - c, 0, 3), i].astype(jnp.float32)
            covered = jnp.logical_and(k - c >= 0, k - c <= 3)
            total = total + jnp.where(covered, other, jnp.zeros_like(other))
            held[k, i] = total.astype(held.dtype)
            return carry

        lax.fori_loop(0, groups, step, 0)
        if k > 0:
            far(k).start()
    for k in (1, 2, 3, 4):
        far(k).wait_recv()

    def last(i, carry):
        total = held[0, i].astype(jnp.float32)
        for k in range(4):
            total = total + far_in[k, i].astype(jnp.float32)
        out[i] = total.astype(out.dtype)
        return carry

    lax.fori_loop(0, groups, last, 0)
    for k in (1, 2, 3, 4):
        far(k).wait_send()
    for i in range(4):
        near(i).wait_send()


def send_back(rows, collective_id, name):
    groups, width = rows.shape[0] // 72, rows.shape[1]
    vmem = pl.BlockSpec(memory_space=pltpu.VMEM)
    own = pl.pallas_call(
        send_back_kernel,
        out_shape=jax.ShapeDtypeStruct((groups, 8, width), rows.dtype),
        in_specs=[vmem],
        out_specs=vmem,
        scratch_shapes=[
            pltpu.VMEM((5, groups, 8, width), rows.dtype),
            pltpu.VMEM((4, groups, 8, width), rows.dtype),
            pltpu.VMEM((4, groups, 8, width), rows.dtype),
            pltpu.SemaphoreType.DMA,
            pltpu.SemaphoreType.DMA((4,)),
            pltpu.SemaphoreType.DMA((4,)),
            pltpu.SemaphoreType.DMA((4,)),
            pltpu.SemaphoreType.DMA((4,)),
        ],
        compiler_params=pltpu.CompilerParams(
            collective_id=collective_id, has_side_effects=True, vmem_limit_bytes=60 * 2**20
        ),
        cost_estimate=pl.CostEstimate(flops=0, bytes_accessed=20 * rows.size, transcendentals=0),
        name=name,
    )(rows.reshape(9, groups, 8, width))
    return own.reshape(8 * groups, width)


def contract(left_side, right_side, left_dim, right_dim):
    return lax.dot_general(
        left_side,
        right_side,
        (((left_dim,), (right_dim,)), ((), ())),
        preferred_element_type=jnp.float32,
    )


def experts_kernel(
    token_rows,
    grad_rows,
    gate_in,
    up_in,
    down_in,
    routed_out,
    back_out,
    gate_out,
    up_out,
    down_out,
    ranks,
    rows_x,
    rows_g,
    weights,
    dots,
    staged,
    gate_up,
    down,
    hidden,
    grads,
    sums_one,
    sums_two,
    in_sem,
    out_sem,
):
    step = pl.program_id(0)
    low = jnp.bfloat16
    units = down_in.shape[1]
    wide = down.shape[0]
    pair_slots = 48
    width = rows_x.shape[2]
    blocks = ranks.shape[0]
    count = rows_x.shape[1]
    part = 256

    def load(k, expert):
        source = (gate_in, up_in, down_in)[k].at[expert]
        return pltpu.make_async_copy(source, staged.at[k], in_sem.at[k])

    def store(k, expert):
        if k == 2:
            source = sums_two.at[pl.ds(0, units)]
        else:
            source = sums_one.at[pl.ds(k * wide, units)]
        target = (gate_out, up_out, down_out)[k].at[expert]
        return pltpu.make_async_copy(source, target, out_sem.at[k])

    def picks(block):
        row = lax.broadcasted_iota(jnp.int32, (pair_slots, 256), 0)
        column = lax.broadcasted_iota(jnp.int32, (pair_slots, 256), 1)
        second = row >= 24
        slot = jnp.where(second, row - 24, row).astype(jnp.float32)
        inside = second == (column >= 128)
        found = []
        for expert in (0, 1):
            rank = ranks[block, expert : expert + 1, :]
            found.append(jnp.logical_and(rank == slot, inside))
        return found

    @pl.when(step == 0)
    def _():
        for k in range(3):
            load(k, 0).start()

    def rank_slots(block):
        square = (128, 128)
        same = lax.broadcasted_iota(jnp.int32, square, 0) == lax.broadcasted_iota(
            jnp.int32, square, 1
        )
        turned = contract(
            jnp.where(same, 1.0, 0.0).astype(low), token_rows[0, :, width:], 1, 1
        )
        first = lax.broadcasted_iota(jnp.int32, (256, 256), 0)
        second = lax.broadcasted_iota(jnp.int32, (256, 256), 1)
        ahead = jnp.logical_and(first < second, (first >= 128) == (second >= 128))
        line = lax.broadcasted_iota(jnp.int32, (8, 256), 0)
        named = jnp.zeros((8, 256), jnp.float32)
        shares = jnp.zeros((8, 256), jnp.float32)
        for expert in (0, 1):
            number = (lax.axis_index("expert") * 2 + expert).astype(jnp.float32)
            match = turned[0:8] == number
            present = jnp.sum(jnp.where(match, 1.0, 0.0), 0, keepdims=True)
            share = jnp.sum(jnp.where(match, turned[8:16] + turned[16:24], 0.0), 0, keepdims=True)
            named = named + jnp.where(line == expert, present, 0.0)
            shares = shares + jnp.where(line == 2 + expert, share, 0.0)
        rank = contract(named.astype(low), jnp.where(ahead, 1.0, 0.0).astype(low), 1, 0)
        rank = jnp.where(named > 0.0, rank, -1.0)
        ranks[block] = jnp.where(line < 2, rank, shares)

    @pl.when(step < blocks)
    def _():
        rank_slots(step)
        found = picks(step)
        pick = jnp.concatenate([jnp.where(f, 1.0, 0.0) for f in found], 0).astype(low)
        from_x = contract(pick, token_rows[0, :, :width], 1, 0).astype(low)
        from_g = contract(pick, grad_rows[0], 1, 0).astype(low)
        here = pl.ds(pl.multiple_of(step * pair_slots, pair_slots), pair_slots)
        for expert in (0, 1):
            lines = slice(expert * pair_slots, (expert + 1) * pair_slots)
            rows_x[expert, here, :] = from_x[lines]
            rows_g[expert, here, :] = from_g[lines]
            shares = ranks[step, 2 + expert : 3 + expert, :]
            weight = jnp.sum(jnp.where(found[expert], shares, 0.0), 1, keepdims=True)
            weights[expert, here, :] = jnp.broadcast_to(weight, (pair_slots, 128))

    for expert in (0, 1):

        @pl.when(step == blocks + expert)
        def _(expert=expert):
            for k in range(3):
                load(k, expert).wait()
            nothing = jnp.zeros((wide - units, width), low)
            gate_up[pl.ds(units, wide - units), :] = nothing
            gate_up[pl.ds(wide + units, wide - units), :] = nothing
            down[pl.ds(units, wide - units), :] = nothing

            def cast(i, carry):
                rows = pl.ds(pl.multiple_of(i * 32, 32), 32)
                gate_up[rows, :] = staged[0, rows, :].astype(low)
                gate_up[pl.ds(pl.multiple_of(wide + i * 32, 32), 32), :] = staged[
                    1, rows, :
                ].astype(low)
                down[rows, :] = staged[2, rows, :].astype(low)
                return carry

            lax.fori_loop(0, units // 32, cast, 0)
            if expert == 0:
                for k in range(3):
                    load(k, 1).start()

            def middle(i, carry):
                rows = pl.ds(pl.multiple_of(i * part, part), part)
                before = contract(rows_x[expert, rows, :], gate_up[...], 1, 1)
                plain = contract(rows_g[expert, rows, :], down[...], 1, 1)
                weight = weights[expert, rows, :][:, 0:1]
                gate, up = before[:, :wide], before[:, wide:]
                sigmoid = 1.0 / (1.0 + jnp.exp(-gate))
                on = gate * sigmoid
                value = on * up
                hidden[rows, :] = (weight * value).astype(low)
                dot = jnp.sum(plain * value, 1, keepdims=True)
                mine = 64 + lax.axis_index("expert") * 2 + expert
                lane = lax.broadcasted_iota(jnp.int32, (part, 128), 1)
                dots[expert, rows, :] = jnp.where(lane == mine, dot, 0.0).astype(low)
                change = weight * plain
                grads[rows, :wide] = (change * up * (sigmoid * (1.0 + gate * (1.0 - sigmoid)))).astype(
                    low
                )
                grads[rows, wide:] = (change * on).astype(low)
                return carry

            lax.fori_loop(0, count // part, middle, 0)
            if expert == 1:
                for k in range(3):
                    store(k, 0).wait()

            def weight_grads(i, carry):
                columns = pl.ds(pl.multiple_of(i * part, part), part)
                sums_one[columns, :] = contract(grads[:, columns], rows_x[expert], 0, 0)
                return carry

            lax.fori_loop(0, 2 * wide // part, weight_grads, 0)
            for i in range(wide // 128):
                columns = pl.ds(i * 128, 128)
                sums_two[columns, :] = contract(hidden[:, columns], rows_g[expert], 0, 0)
            for k in range(3):
                store(k, expert).start()

            def results(i, carry):
                rows = pl.ds(pl.multiple_of(i * part, part), part)
                rows_x[expert, rows, :] = contract(hidden[rows, :], down[...], 1, 0).astype(low)
                rows_g[expert, rows, :] = contract(grads[rows, :], gate_up[...], 1, 0).astype(low)
                return carry

            lax.fori_loop(0, count // part, results, 0)

    @pl.when(step >= blocks + 2)
    def _():
        block = step - blocks - 2
        pick = jnp.concatenate([jnp.where(f, 1.0, 0.0) for f in picks(block)], 0).astype(low)
        here = pl.ds(pl.multiple_of(block * pair_slots, pair_slots), pair_slots)

        def both(ref):
            return jnp.concatenate([ref[0, here, :], ref[1, here, :]], 0)

        routed_out[0] = contract(pick, both(rows_x), 0, 0).astype(low)
        back_out[0, :, :width] = contract(pick, both(rows_g), 0, 0).astype(low)
        back_out[0, :, width:] = contract(pick, both(dots), 0, 0).astype(low)

    @pl.when(step == 2 * blocks + 1)
    def _():
        for k in range(3):
            store(k, 1).wait()


def experts(token_rows, grad_rows, gate, up, down):
    low = jnp.bfloat16
    blocks = token_rows.shape[0]
    local, units, width = down.shape
    wide = (units + 127) // 128 * 128
    count = blocks * 48
    last = blocks - 1

    def entering(i):
        return (jnp.minimum(i, last), 0, 0)

    def leaving(i):
        return (jnp.maximum(i - blocks - 2, 0), 0, 0)

    weight = jax.ShapeDtypeStruct((local, units, width), jnp.float32)
    return pl.pallas_call(
        experts_kernel,
        grid=(2 * blocks + 2,),
        out_shape=(
            jax.ShapeDtypeStruct((blocks, 256, width), low),
            jax.ShapeDtypeStruct((blocks, 256, width + 128), low),
            weight,
            weight,
            weight,
        ),
        in_specs=[
            pl.BlockSpec((1, 256, width + 128), entering),
            pl.BlockSpec((1, 256, width), entering),
            HBM,
            HBM,
            HBM,
        ],
        out_specs=(
            pl.BlockSpec((1, 256, width), leaving),
            pl.BlockSpec((1, 256, width + 128), leaving),
            HBM,
            HBM,
            HBM,
        ),
        scratch_shapes=[
            pltpu.VMEM((blocks, 8, 256), jnp.float32),
            pltpu.VMEM((local, count, width), low),
            pltpu.VMEM((local, count, width), low),
            pltpu.VMEM((local, count, 128), jnp.float32),
            pltpu.VMEM((local, count, 128), low),
            pltpu.VMEM((3, units, width), jnp.float32),
            pltpu.VMEM((2 * wide, width), low),
            pltpu.VMEM((wide, width), low),
            pltpu.VMEM((count, wide), low),
            pltpu.VMEM((count, 2 * wide), low),
            pltpu.VMEM((2 * wide, width), jnp.float32),
            pltpu.VMEM((wide, width), jnp.float32),
            pltpu.SemaphoreType.DMA((3,)),
            pltpu.SemaphoreType.DMA((3,)),
        ],
        compiler_params=pltpu.CompilerParams(
            dimension_semantics=("arbitrary",), vmem_limit_bytes=60 * 2**20
        ),
        cost_estimate=pl.CostEstimate(
            flops=18 * local * count * wide * width,
            bytes_accessed=100 * 2**20,
            transcendentals=local * count * wide,
        ),
        name="experts",
    )(token_rows, grad_rows, gate, up, down)


def rms_forward(values, gains):
    inverse = lax.rsqrt(jnp.mean(values * values, -1, keepdims=True) + epsilon)
    return (values * inverse * gains, inverse)


def rope_tables(positions):
    half_dim = ROPE // 2
    freqs = rope_base ** (-jnp.arange(half_dim, dtype=jnp.float32) / half_dim)
    angles = positions.astype(jnp.float32)[:, None] * freqs[None, :]
    return (jnp.cos(angles), jnp.sin(angles))


HEADS = 4
SCALE = (NOPE + ROPE) ** (-0.5)


def lanes(shape):
    return lax.broadcasted_iota(jnp.int32, shape, 1)


def turn_tables(cosine, sine_tab):
    lane = lanes(cosine.shape)
    kept = jnp.where(lane < 64, cosine, 0.0)
    crossed = jnp.where(lane < 32, -sine_tab, jnp.where(lane < 64, sine_tab, 0.0))
    return kept, crossed


def exchange_halves(values):
    shape = (128, 128)
    to = lanes(shape)
    from_lane = lax.broadcasted_iota(jnp.int32, shape, 0)
    other = jnp.where(to < 32, to + 32, jnp.where(to < 64, to - 32, to))
    swap = jnp.where(from_lane == other, 1.0, 0.0)
    return lax.dot_general(
        values,
        swap,
        (((1,), (0,)), ((), ())),
        precision=lax.Precision.HIGHEST,
        preferred_element_type=jnp.float32,
    )


def fold_matrix():
    shape = (128, 256)
    to = lanes(shape)
    wanted = jnp.where(to >= 128, 32, 0) + lax.rem(to, 32)
    return jnp.where(lax.broadcasted_iota(jnp.int32, shape, 0) == wanted, 1.0, 0.0).astype(
        jnp.bfloat16
    )


def head_lanes(values, head):
    lane = lanes(values.shape)
    inside = jnp.logical_and(lane >= 32 * head, lane < 32 * head + 32)
    return jnp.where(inside, values, jnp.zeros_like(values))


def pack_kernel(
    query,
    latent,
    gain_one,
    gain_two,
    gain_latent,
    output,
    expand,
    gate,
    router,
    up,
    down,
    attention_out,
    ffn_out,
):
    low = jnp.bfloat16
    shard = query.shape[0]
    for head in range(HEADS):
        start = 192 * head
        attention_out[:, 128 * head : 128 * head + 128] = query[:, start : start + 128].astype(low)
    for half in (0, 1):
        starts = [192 * head + 128 + 32 * half for head in range(HEADS)]
        pieces = [query[:, start : start + 32] for start in starts]
        to = 512 + 128 * half
        attention_out[:, to : to + 128] = jnp.concatenate(pieces, 1).astype(low)
    attention_out[:, 768:1280] = latent[:, :RANK].astype(low)
    row = lax.broadcasted_iota(jnp.int32, (shard, shard), 0)
    gains = jnp.where(row == 0, gain_one[...], 0.0)
    gains = jnp.where(row == 1, gain_two[...], gains)
    gains = jnp.where(row == 2, gain_latent[...], gains)
    attention_out[:, 1280:1408] = jnp.concatenate([latent[:, RANK:], gains], 1).astype(low)
    attention_out[:, 1408:1920] = output[...].astype(low)
    for j in range(4):
        attention_out[16 * j : 16 * j + 16, 1920:] = expand[:, 256 * j : 256 * j + 256].astype(low)
    gap = jnp.zeros((shard, 64), jnp.float32)
    for k, (wide, narrow) in enumerate(((gate, router[...]), (up, gap), (down, gap))):
        start = 768 * k
        ffn_out[:, start : start + 640] = wide[:, :640].astype(low)
        ffn_out[:, start + 640 : start + 768] = jnp.concatenate(
            [wide[:, 640:704], narrow], 1
        ).astype(low)


def project_kernel(
    hidden, weights, gain, gain_latent, cosine, sine_tab, normed_out, query_out, key_out, latent_out
):
    low = jnp.bfloat16
    normed = rms_forward(hidden[...].astype(jnp.float32), gain[...])[0].astype(low)
    normed_out[...] = normed
    query = contract(normed, weights[:, :768], 1, 0)
    first, second = query[:, 512:640], query[:, 640:768]
    cos, sin = cosine[...], sine_tab[...]
    query_out[:, :512] = query[:, :512].astype(low)
    query_out[:, 512:640] = (first * cos - second * sin).astype(low)
    query_out[:, 640:768] = (second * cos + first * sin).astype(low)
    latent = contract(normed, weights[:, 768:1408], 1, 0)
    latent_out[...] = latent[:, :RANK]
    key_out[:, :RANK] = rms_forward(latent[:, :RANK], gain_latent[...])[0].astype(low)
    rope = latent[:, RANK:]
    kept, crossed = turn_tables(cos, sin)
    key_out[:, RANK:] = (rope * kept + exchange_halves(rope) * crossed).astype(low)


def attend_kernel(
    keys,
    expand,
    query,
    own_segment,
    key_segment,
    wo_0,
    wo_1,
    wo_2,
    wo_3,
    out,
    attended,
    probs,
    expanded,
    key_rope,
):
    low = jnp.bfloat16
    rows = query.shape[0]
    count = keys.shape[0]
    fold = fold_matrix()

    def expand_rows(i, carry):
        part = pl.ds(pl.multiple_of(i * rows, rows), rows)
        expanded[part, :] = contract(keys[part, :RANK], expand[...], 1, 0).astype(low)
        key_rope[part, :] = contract(keys[part, RANK:], fold, 1, 0).astype(low)
        return carry

    lax.fori_loop(0, count // rows, expand_rows, 0)
    shape = (rows, count)
    distance = lax.broadcasted_iota(jnp.int32, shape, 0) + WINDOW - lanes(shape)
    allowed = jnp.logical_and(distance >= 0, distance < WINDOW)
    allowed = jnp.logical_and(allowed, own_segment[...] == key_segment[...])
    total = jnp.zeros(out.shape, jnp.float32)
    for head, wo in enumerate((wo_0, wo_1, wo_2, wo_3)):
        start = 256 * head
        scores = contract(query[:, 128 * head : 128 * head + 128], expanded[:, start : start + 128], 1, 1)
        scores += contract(head_lanes(query[:, 512:640], head), key_rope[:, :128], 1, 1)
        scores += contract(head_lanes(query[:, 640:768], head), key_rope[:, 128:], 1, 1)
        scores = jnp.where(allowed, scores * SCALE, masked_score)
        exponent = jnp.exp(scores - jnp.max(scores, 1, keepdims=True))
        share = exponent / jnp.sum(exponent, 1, keepdims=True)
        probs[head] = share
        mixed = contract(share.astype(low), expanded[:, start + 128 : start + 256], 1, 0).astype(low)
        attended[:, 128 * head : 128 * head + 128] = mixed
        total += contract(mixed, wo[...], 1, 1)
    out[...] = total.astype(low)


def route_kernel(hidden, attention, gain, router, routes, token_out, middle_out, gates_out):
    low = jnp.bfloat16
    middle = hidden[...].astype(jnp.float32) + attention[...].astype(jnp.float32)
    middle_out[...] = middle
    normed = rms_forward(middle, gain[...])[0].astype(low)
    width = normed.shape[1]
    token_out[:, :width] = normed
    logits = contract(normed, router[...], 1, 0)
    lane = lanes(logits.shape)
    named = [routes[:, r : r + 1] for r in range(6)]
    chosen = [
        jnp.sum(jnp.where(lane == number + 64, logits, 0.0), 1, keepdims=True) for number in named
    ]
    most = functools.reduce(jnp.maximum, chosen)
    exponents = [jnp.exp(value - most) for value in chosen]
    total = functools.reduce(jnp.add, exponents)
    extra = jnp.where(jnp.logical_or(lane == 6, lane == 7), 128.0, 0.0)
    gates = jnp.zeros(logits.shape, jnp.float32)
    for r in range(6):
        weight = exponents[r] / total
        high = weight.astype(low).astype(jnp.float32)
        extra += jnp.where(lane == r, named[r].astype(jnp.float32), 0.0)
        extra += jnp.where(lane == 8 + r, high, 0.0)
        extra += jnp.where(lane == 16 + r, weight - high, 0.0)
        gates += jnp.where(lane == r, weight, 0.0)
    token_out[:, width:] = extra.astype(low)
    gates_out[...] = gates


def shared_kernel(normed, cotangent, weights, part_out, back_out, grads_out):
    low = jnp.bfloat16
    gate = contract(normed[...], weights[:, :768], 1, 0)
    up = contract(normed[...], weights[:, 768:1536], 1, 0)
    sigmoid = 1.0 / (1.0 + jnp.exp(-gate))
    on = gate * sigmoid
    hidden = (on * up).astype(low)
    part_out[...] = contract(hidden, weights[:, 1536:], 1, 1)
    change = contract(cotangent[...], weights[:, 1536:], 1, 0)
    grad_gate = (change * up * (sigmoid * (1.0 + gate * (1.0 - sigmoid)))).astype(low)
    grad_up = (change * on).astype(low)
    back_out[...] = contract(grad_gate, weights[:, :768], 1, 1) + contract(
        grad_up, weights[:, 768:1536], 1, 1
    )

    def grads(i, carry):
        part = pl.ds(pl.multiple_of(i * 256, 256), 256)
        rows = normed[:, part]
        grads_out[part, :768] = contract(rows, grad_gate, 0, 0).astype(low)
        grads_out[part, 768:1536] = contract(rows, grad_up, 0, 0).astype(low)
        grads_out[part, 1536:] = contract(cotangent[:, part], hidden, 0, 0).astype(low)
        return carry

    lax.fori_loop(0, grads_out.shape[0] // 256, grads, 0)


def attend_back_kernel(
    back,
    middle,
    gain,
    gates,
    routes,
    router,
    cotangent,
    wo_0,
    wo_1,
    wo_2,
    wo_3,
    probs,
    expanded,
    key_rope,
    query,
    keys,
    expand,
    query_w,
    cosine,
    sine_tab,
    middle_out,
    attention_out,
    gain_out,
    logits_out,
    query_out,
    back_out,
    keys_out,
    expand_out,
    changes,
    ropes,
):
    low = jnp.bfloat16
    width = middle.shape[1]
    rows = middle.shape[0]
    lane = lanes((rows, 128))
    sums = back[:, width:].astype(jnp.float32)
    named = [routes[:, r : r + 1] for r in range(6)]
    weight = [gates[:, r : r + 1] for r in range(6)]
    change = [
        jnp.sum(jnp.where(lane == number + 64, sums, 0.0), 1, keepdims=True) for number in named
    ]
    inner = functools.reduce(jnp.add, [w * c for w, c in zip(weight, change)])
    logits = jnp.zeros((rows, 128), jnp.float32)
    for r in range(6):
        logits += jnp.where(lane == named[r] + 64, weight[r] * (change[r] - inner), 0.0)
    logits_low = logits.astype(low)
    logits_out[...] = logits_low
    grad_normed = back[:, :width].astype(jnp.float32) + contract(logits_low, router[...], 1, 1)
    values = middle[...]
    inverse = lax.rsqrt(jnp.mean(values * values, 1, keepdims=True) + epsilon)
    weighted = grad_normed * gain[...]
    aligned = jnp.mean(values * weighted, 1, keepdims=True)
    gain_out[...] = jnp.sum(grad_normed * values * inverse, 0, keepdims=True)
    grad_middle = (
        cotangent[...].astype(jnp.float32)
        + inverse * weighted
        - values * (inverse * inverse * inverse) * aligned
    )
    middle_out[...] = grad_middle
    grad_attn = grad_middle.astype(low)
    attention_out[...] = grad_attn
    first = jnp.zeros((rows, 128), jnp.float32)
    second = jnp.zeros((rows, 128), jnp.float32)
    for head, wo in enumerate((wo_0, wo_1, wo_2, wo_3)):
        start = 256 * head
        nope, value = slice(start, start + 128), slice(start + 128, start + 256)
        own = slice(128 * head, 128 * head + 128)
        grad_mixed = contract(grad_attn, wo[...], 1, 0).astype(low)
        share = probs[head]
        changes[:, value] = contract(share.astype(low), grad_mixed, 0, 0).astype(low)
        grad_share = contract(grad_mixed, expanded[:, value], 1, 1)
        grad_scores = share * (grad_share - jnp.sum(share * grad_share, 1, keepdims=True))
        grad_scores = grad_scores.astype(low)
        query_out[:, own] = (contract(grad_scores, expanded[:, nope], 1, 0) * SCALE).astype(low)
        both = contract(grad_scores, key_rope[...], 1, 0) * SCALE
        first += head_lanes(both[:, :128], head)
        second += head_lanes(both[:, 128:], head)
        changes[:, nope] = (contract(grad_scores, query[:, own], 0, 0) * SCALE).astype(low)
        from_first = contract(grad_scores, head_lanes(query[:, 512:640], head), 0, 0) * SCALE
        from_second = contract(grad_scores, head_lanes(query[:, 640:768], head), 0, 0) * SCALE
        if head == 0:
            ropes[:, :128] = from_first
            ropes[:, 128:] = from_second
        else:
            ropes[:, :128] += from_first
            ropes[:, 128:] += from_second
    cos, sin = cosine[...], sine_tab[...]
    query_out[:, 512:640] = (first * cos + second * sin).astype(low)
    query_out[:, 640:768] = (second * cos - first * sin).astype(low)
    back_out[...] = contract(query_out[...], query_w[...], 1, 1).astype(low)
    fold = fold_matrix()

    def key_rows(i, carry):
        part = pl.ds(pl.multiple_of(i * rows, rows), rows)
        keys_out[part, :RANK] = contract(changes[part, :], expand[...], 1, 1).astype(low)
        keys_out[part, RANK:] = contract(ropes[part, :].astype(low), fold, 1, 1).astype(low)
        return carry

    lax.fori_loop(0, keys.shape[0] // rows, key_rows, 0)
    for j in range(4):
        grad_expand = contract(keys[:, :RANK], changes[:, 256 * j : 256 * j + 256], 0, 0)
        expand_out[:, 16 * j : 16 * j + 16, :] = grad_expand.astype(low).reshape(32, 16, 256)


def finish_kernel(
    summed,
    latent,
    gain_latent,
    cosine,
    sine_tab,
    wl_0,
    wl_1,
    wl_2,
    wl_3,
    wl_4,
    hidden,
    gain,
    grad_middle,
    normed,
    grad_attn,
    normed_two,
    grad_logits,
    grad_query,
    attended,
    input_out,
    gain_out,
    gain_latent_out,
    grads_out,
    changes,
):
    low = jnp.bfloat16
    width = hidden.shape[1]
    grad_latent = summed[:, width : width + RANK].astype(jnp.float32)
    rope = summed[:, width + RANK :].astype(jnp.float32)
    values = latent[...]
    inverse = lax.rsqrt(jnp.mean(values * values, 1, keepdims=True) + epsilon)
    weighted = grad_latent * gain_latent[...]
    aligned = jnp.mean(values * weighted, 1, keepdims=True)
    gain_latent_out[...] = jnp.sum(grad_latent * values * inverse, 0, keepdims=True)
    changes[:, :RANK] = (
        inverse * weighted - values * (inverse * inverse * inverse) * aligned
    ).astype(low)
    kept, crossed = turn_tables(cosine[...], sine_tab[...])
    changes[:, RANK:] = (rope * kept - exchange_halves(rope) * crossed).astype(low)
    grad_normed = summed[:, :width].astype(jnp.float32)
    for j, wl in enumerate((wl_0, wl_1, wl_2, wl_3, wl_4)):
        grad_normed += contract(changes[:, 128 * j : 128 * j + 128], wl[...], 1, 1)
    values = hidden[...].astype(jnp.float32)
    inverse = lax.rsqrt(jnp.mean(values * values, 1, keepdims=True) + epsilon)
    weighted = grad_normed * gain[...]
    aligned = jnp.mean(values * weighted, 1, keepdims=True)
    gain_out[...] = jnp.sum(grad_normed * values * inverse, 0, keepdims=True)
    input_out[...] = (
        grad_middle[...] + inverse * weighted - values * (inverse * inverse * inverse) * aligned
    ).astype(low)

    def grads(i, carry):
        part = pl.ds(pl.multiple_of(i * 256, 256), 256)
        rows = normed[:, part]
        grads_out[part, :768] = contract(rows, grad_query[...], 0, 0).astype(low)
        grads_out[part, 768:1280] = contract(rows, changes[:, :RANK], 0, 0).astype(low)
        mixed = contract(rows, changes[:, RANK:], 0, 0)
        mixed += contract(normed_two[:, part], grad_logits[...], 0, 0)
        grads_out[part, 1280:1408] = mixed.astype(low)
        grads_out[part, 1408:] = contract(grad_attn[:, part], attended[...], 0, 0).astype(low)
        return carry

    lax.fori_loop(0, grads_out.shape[0] // 256, grads, 0)


def unpack_kernel(
    own,
    ffn,
    middle,
    layer,
    layer_out,
    query_out,
    latent_out,
    router_out,
    output_out,
    gains_out,
    expand_out,
    gate_out,
    up_out,
    down_out,
):
    layer_out[...] = (middle[...] + layer[...].astype(jnp.float32)).astype(layer_out.dtype)
    for head in range(HEADS):
        query_out[:, 192 * head : 192 * head + 128] = own[:, 128 * head : 128 * head + 128]
        for half in (0, 1):
            to, start = 192 * head + 128 + 32 * half, 512 + 128 * half + 32 * head
            query_out[:, to : to + 32] = own[:, start : start + 32]
    latent_out[...] = own[:, 768:1344]
    router_out[...] = own[:, 1344:1408]
    output_out[...] = own[:, 1408:1920]
    gains_out[...] = own[0:8, 1920:2048]
    for j in range(4):
        expand_out[:, 256 * j : 256 * j + 256] = own[16 * j : 16 * j + 16, 2048:2304]
    gate_out[...] = ffn[:, :704].astype(jnp.float32)
    up_out[...] = ffn[:, 768:1472].astype(jnp.float32)
    down_out[...] = ffn[:, 1536:2240].astype(jnp.float32)


def local_call(kernel, name, operands, out_shapes, scratch=()):
    arrays, specs = [], []
    for operand in operands:
        if isinstance(operand, tuple):
            array, block, index = operand
            specs.append(pl.BlockSpec(block, lambda i, index=index: index))
        else:
            array = operand
            zeros = (0,) * array.ndim
            specs.append(pl.BlockSpec(array.shape, lambda i, zeros=zeros: zeros))
        arrays.append(array)
    shapes = [jax.ShapeDtypeStruct(shape, dtype) for shape, dtype in out_shapes]
    return pl.pallas_call(
        kernel,
        grid=(1,),
        out_shape=shapes,
        in_specs=specs,
        out_specs=[
            pl.BlockSpec(shape.shape, lambda i, zeros=(0,) * len(shape.shape): zeros)
            for shape in shapes
        ],
        scratch_shapes=[pltpu.VMEM(shape, dtype) for shape, dtype in scratch],
        compiler_params=pltpu.CompilerParams(vmem_limit_bytes=60 * 2**20),
        name=name,
    )(*arrays)


def column_blocks(array, first, number):
    return [(array, (array.shape[0], 128), (0, first + j)) for j in range(number)]


def body(
    hidden_in,
    cotangent,
    segments,
    routes,
    attn_norm,
    w_query,
    w_latent,
    latent_norm,
    w_expand,
    w_output,
    ffn_norm,
    w_router,
    shared_gate,
    shared_up,
    shared_down,
    expert_gate,
    routed_expert_up,
    expert_down,
):
    tokens, model_width = hidden_in.shape
    devices = lax.axis_size("expert")
    own_index = lax.axis_index("expert")
    low = jnp.bfloat16
    full = jnp.float32
    shard = w_query.shape[0]

    attention_shard, ffn_shard = local_call(
        pack_kernel,
        "pack",
        (
            w_query,
            w_latent,
            attn_norm[None],
            ffn_norm[None],
            jnp.pad(latent_norm, (0, shard - latent_norm.shape[0]))[None],
            w_output.T,
            w_expand,
            shared_gate,
            w_router,
            shared_up,
            shared_down.T,
        ),
        (((shard, 2176), low), ((shard, 2304), low)),
    )
    ffn_all = lax.all_gather(ffn_shard, "expert", axis=0, tiled=True)
    grad_rows = lax.all_gather(cotangent, "expert", axis=0)
    attention_all = plane_gather(attention_shard, 1, "gather_attention")
    gains = attention_all.reshape(devices, shard, -1)[:, :8, 1344:1408].astype(full)
    gain_one = gains[:, 0].reshape(1, -1)
    gain_two = gains[:, 1].reshape(1, -1)
    gain_latent = gains[:, 2, : latent_norm.shape[0]].reshape(1, -1)
    expand_w = (
        attention_all[:, 1920:].reshape(devices, 4, 16, 256).swapaxes(1, 2).reshape(RANK, -1)
    )
    output_blocks = column_blocks(attention_all, 11, 4)
    latent_blocks = column_blocks(attention_all, 6, 5)
    router_block = column_blocks(ffn_all, 5, 1)[0]

    first_row = own_index * tokens
    row_index = first_row + jnp.arange(tokens, dtype=jnp.int32)
    own_segments = lax.dynamic_slice_in_dim(segments, first_row, tokens)
    doc_start = jnp.sum((segments[None, :] < own_segments[:, None]).astype(jnp.int32), 1)
    cosine, sine_tab = rope_tables(row_index - doc_start)
    cosine, sine_tab = jnp.tile(cosine, (1, 4)), jnp.tile(sine_tab, (1, 4))
    normed, queries, key_row, latent = local_call(
        project_kernel,
        "project",
        (
            hidden_in,
            (attention_all, (model_width, 1408), (0, 0)),
            gain_one,
            gain_latent,
            cosine,
            sine_tab,
        ),
        (
            ((tokens, model_width), low),
            ((tokens, 768), low),
            ((tokens, 640), low),
            ((tokens, RANK), full),
        ),
    )
    keys_all = reach_back(key_row, 2, "reach_back")
    key_count = keys_all.shape[0]
    key_segments = lax.dynamic_slice_in_dim(
        jnp.pad(segments, (key_count - tokens, 0), constant_values=-1), first_row, key_count
    )
    attn_part, attended, probs, expanded, key_rope = local_call(
        attend_kernel,
        "attend",
        (keys_all, expand_w, queries, own_segments[:, None], key_segments[None], *output_blocks),
        (
            ((tokens, model_width), low),
            ((tokens, HEADS * VH), low),
            ((HEADS, tokens, key_count), full),
            ((key_count, HEADS * (NOPE + VH)), low),
            ((key_count, 256), low),
        ),
    )
    attn_out = line_sum(attn_part, 3, "sum_heads")

    token_row, middle, gates = local_call(
        route_kernel,
        "route",
        (hidden_in, attn_out, gain_two, router_block, routes),
        (
            ((tokens, model_width + 128), low),
            ((tokens, model_width), full),
            ((tokens, 128), full),
        ),
    )
    token_rows = plane_gather(token_row, 4, "gather_tokens")
    token_row, token_rows = lax.optimization_barrier((token_row, token_rows))
    normed_two = (token_row, (tokens, model_width), (0, 0))

    shared_part, shared_back, ffn_grads = local_call(
        shared_kernel,
        "shared",
        (normed_two, cotangent, ffn_all),
        (
            ((tokens, model_width), full),
            ((tokens, model_width), full),
            (ffn_all.shape, low),
        ),
    )
    ffn_grads, token_rows = lax.optimization_barrier((ffn_grads, token_rows))
    own_ffn = lax.psum_scatter(ffn_grads, "expert", scatter_dimension=0, tiled=True)

    routed_part, back_part, out_egate, out_eup, out_edown = experts(
        token_rows.reshape(devices // 2, 2 * tokens, -1),
        grad_rows.reshape(devices // 2, 2 * tokens, -1),
        expert_gate.swapaxes(1, 2),
        routed_expert_up.swapaxes(1, 2),
        expert_down,
    )
    out_egate, out_eup = out_egate.swapaxes(1, 2), out_eup.swapaxes(1, 2)
    routed_own = lax.psum_scatter(
        routed_part.reshape(-1, model_width), "expert", scatter_dimension=0, tiled=True
    )
    layer_part = (routed_own.astype(full) + shared_part).astype(low)
    back_own = plane_sum((back_part.reshape(devices * tokens, -1),), 5, "sum_tokens")
    back_wide = back_own + jnp.pad(shared_back, ((0, 0), (0, 128)))
    back_all = line_sum(back_wide.astype(low), 6, "sum_units")

    (
        grad_middle,
        grad_attn,
        grad_gain_two,
        grad_logits,
        grad_query_pre,
        query_back,
        grad_keys,
        grad_expand,
    ) = local_call(
        attend_back_kernel,
        "attend_back",
        (
            back_all,
            middle,
            gain_two,
            gates,
            routes,
            router_block,
            cotangent,
            *output_blocks,
            probs,
            expanded,
            key_rope,
            queries,
            keys_all,
            expand_w,
            (attention_all, (model_width, 768), (0, 0)),
            cosine,
            sine_tab,
        ),
        (
            ((tokens, model_width), full),
            ((tokens, model_width), low),
            ((1, model_width), full),
            ((tokens, 128), low),
            ((tokens, 768), low),
            ((tokens, model_width), low),
            ((key_count, 640), low),
            ((devices, shard, 256), low),
        ),
        (((key_count, HEADS * (NOPE + VH)), low), ((key_count, 256), full)),
    )
    latent_part = send_back(grad_keys, 7, "send_back")
    summed = line_sum(jnp.concatenate([query_back, latent_part], 1), 8, "sum_inputs")
    grad_input, grad_gain_one, grad_gain_latent, many_grads = local_call(
        finish_kernel,
        "finish",
        (
            summed,
            latent,
            gain_latent,
            cosine,
            sine_tab,
            *latent_blocks,
            hidden_in,
            gain_one,
            grad_middle,
            normed,
            grad_attn,
            normed_two,
            grad_logits,
            grad_query_pre,
            attended,
        ),
        (
            ((tokens, model_width), low),
            ((1, model_width), full),
            ((1, RANK), full),
            ((model_width, 1920), low),
        ),
        (((tokens, 640), low),),
    )

    gain_grads = jnp.stack(
        [
            grad_gain_one.reshape(devices, shard),
            grad_gain_two.reshape(devices, shard),
            jnp.pad(
                grad_gain_latent.reshape(devices, -1), ((0, 0), (0, shard - latent_norm.shape[0]))
            ),
        ],
        1,
    ).astype(low)
    gain_grads = jnp.pad(gain_grads, ((0, 0), (0, shard - 3), (0, 128 - shard)))
    own, layer_sum = plane_sum(
        (many_grads, gain_grads.reshape(model_width, 128), grad_expand.reshape(model_width, 256)),
        9,
        "sum_attention",
        layer_part,
    )
    (
        layer_out,
        out_query,
        out_latent,
        out_router,
        out_output,
        out_gains,
        out_expand,
        out_sgate,
        out_sup,
        out_sdown,
    ) = local_call(
        unpack_kernel,
        "unpack",
        (own, own_ffn, middle, layer_sum),
        (
            ((tokens, model_width), low),
            (w_query.shape, full),
            (w_latent.shape, full),
            (w_router.shape, full),
            ((shard, w_output.shape[0]), full),
            ((8, 128), full),
            (w_expand.shape, full),
            (shared_gate.shape, full),
            (shared_up.shape, full),
            ((shard, shared_down.shape[0]), full),
        ),
    )
    return (
        layer_out,
        grad_input,
        out_gains[0, :shard],
        out_query,
        out_latent,
        out_gains[2, : latent_norm.shape[0]],
        out_expand,
        out_output.T,
        out_gains[1, :shard],
        out_router,
        out_sgate,
        out_sup,
        out_sdown.T,
        out_egate,
        out_eup,
        out_edown,
    )


def solution(mesh):
    in_specs = (
        P("expert", None),
        P("expert", None),
        P(),
        P("expert", None),
        P("expert"),
        P("expert", "tensor"),
        P("expert", None),
        P("expert"),
        P("expert", "tensor"),
        P("tensor", "expert"),
        P("expert"),
        P("expert", None),
        P("expert", "tensor"),
        P("expert", "tensor"),
        P("tensor", "expert"),
        P("expert", None, "tensor"),
        P("expert", None, "tensor"),
        P("expert", "tensor", None),
    )
    out_specs = (
        P("expert", None),
        P("expert", None),
        P("expert"),
        P("expert", "tensor"),
        P("expert", None),
        P("expert"),
        P("expert", "tensor"),
        P("tensor", "expert"),
        P("expert"),
        P("expert", None),
        P("expert", "tensor"),
        P("expert", "tensor"),
        P("tensor", "expert"),
        P("expert", None, "tensor"),
        P("expert", None, "tensor"),
        P("expert", "tensor", None),
    )
    return jax.shard_map(body, mesh=mesh, in_specs=in_specs, out_specs=out_specs, check_vma=False)
```

```python
import functools

import jax
import jax.numpy as jnp
from jax import lax
from jax.experimental import pallas as pl
from jax.experimental.pallas import tpu as pltpu
from jax.sharding import PartitionSpec as P

NOPE = 128
ROPE = 64
VH = 128
RANK = 512
WINDOW = 1024


epsilon = 1e-06
masked_score = -1e30
rope_base = 10000.0


MESH = pl.DeviceIdType.MESH
HBM = pl.BlockSpec(memory_space=pltpu.HBM)


def place():
    e = lax.axis_index("expert")
    return lax.axis_index("tensor"), e // 8, lax.rem(e // 2, 4), lax.rem(e, 2)


def at(x, z, c):
    return (x * 4 + z) * 2 + c


def wrap(v):
    return lax.rem(v + 4, 4)


def greet(peers):
    call(peers)
    hear(peers)


def call(peers):
    barrier = pltpu.get_barrier_semaphore()
    for peer in peers:
        pl.semaphore_signal(barrier, inc=1, device_id=peer, device_id_type=MESH)


def hear(peers):
    pl.semaphore_wait(pltpu.get_barrier_semaphore(), len(peers))


def plane_gather_kernel(src, out, ssem, rsem, dssem, drsem, lsem):
    t, x, z, c = place()
    rows = src.shape[0]
    half, quarter = rows // 2, rows // 4
    sibling = (at(x, z, 1 - c), t)
    along_x = [(at(wrap(x - 1), z, c), t), (at(wrap(x + 1), z, c), t)]
    along_z = [(at(x, wrap(z - 1), c), t), (at(x, wrap(z + 1), c), t)]
    greet([sibling] + along_x + along_z)
    own = pltpu.make_async_copy(src, out.at[at(x, z, c)], lsem)
    own.start()
    sent = []

    def piece(h, j1, j2, part=None):
        if h == 0:
            index = at(wrap(x + j2), wrap(z + j1), c)
        else:
            index = at(wrap(x + j1), wrap(z + j2), c)
        if part is None:
            return index, pl.ds(h * half, half)
        return index, pl.ds(h * half + part * quarter, quarter)

    def send(h, slot, which, device, first):
        index, rows_of = which
        return pltpu.make_async_remote_copy(
            src_ref=src.at[rows_of] if first else out.at[index, rows_of],
            dst_ref=out.at[index, rows_of],
            send_sem=ssem.at[h, slot],
            recv_sem=rsem.at[h, slot],
            device_id=device,
            device_id_type=MESH,
        )

    def across(h, j1, j2):
        index, rows_of = piece(h, j1, j2)
        slot = (h * 4 + j1 % 4) * 4 + j2 % 4
        return pltpu.make_async_remote_copy(
            src_ref=src.at[rows_of] if j1 == 0 and j2 == 0 else out.at[index, rows_of],
            dst_ref=out.at[index, rows_of],
            send_sem=dssem.at[slot],
            recv_sem=drsem.at[slot],
            device_id=sibling,
            device_id_type=MESH,
        )

    def ring(h, stage):
        return along_z if (h == 0) == (stage == 1) else along_x

    def stage_one(h, kind):
        left, right = ring(h, 1)
        if kind == 0:
            return send(h, 0, piece(h, 0, 0), right, True)
        if kind == 1:
            return send(h, 1, piece(h, 0, 0), left, True)
        if kind == 2:
            return send(h, 2, piece(h, -1, 0, 0), right, False)
        return send(h, 3, piece(h, 1, 0, 1), left, False)

    def stage_two(h, j1, kind):
        left, right = ring(h, 2)
        slot = 4 + 4 * (j1 % 4) + kind
        if kind == 0:
            return send(h, slot, piece(h, j1, 0), right, j1 == 0)
        if kind == 1:
            return send(h, slot, piece(h, j1, 0), left, j1 == 0)
        if kind == 2:
            return send(h, slot, piece(h, j1, -1, 0), right, False)
        return send(h, slot, piece(h, j1, 1, 1), left, False)

    def go(copy):
        copy.start()
        sent.append(copy)

    for h in (0, 1):
        go(stage_one(h, 0))
        go(stage_one(h, 1))
        go(stage_two(h, 0, 0))
        go(stage_two(h, 0, 1))
        go(across(h, 0, 0))
    for h in (0, 1):
        for kind, j in ((0, -1), (1, 1)):
            stage_one(h, kind).wait_recv()
            go(stage_one(h, 2 + kind))
            go(stage_two(h, j, 0))
            go(stage_two(h, j, 1))
            go(across(h, j, 0))
    for h in (0, 1):
        for kind, j in ((0, -1), (1, 1)):
            stage_two(h, 0, kind).wait_recv()
            go(stage_two(h, 0, 2 + kind))
            go(across(h, 0, j))
    for h in (0, 1):
        stage_one(h, 2).wait_recv()
        stage_one(h, 3).wait_recv()
        go(stage_two(h, 2, 0))
        go(stage_two(h, 2, 1))
        go(across(h, 2, 0))
    for j1 in (-1, 1, 2):
        for h in (0, 1):
            for kind, j in ((0, -1), (1, 1)):
                stage_two(h, j1, kind).wait_recv()
                go(stage_two(h, j1, 2 + kind))
                go(across(h, j1, j))
    for j1 in (0, -1, 1, 2):
        for h in (0, 1):
            stage_two(h, j1, 2).wait_recv()
            stage_two(h, j1, 3).wait_recv()
            go(across(h, j1, 2))
    for h in (0, 1):
        for j1 in (0, -1, 1, 2):
            for j2 in (0, -1, 1, 2):
                across(h, j1, j2).wait_recv()
    for copy in sent:
        copy.wait_send()
    own.wait()


def plane_gather(rows, collective_id, name):
    grouped = rows.reshape(rows.shape[0] // 8, 8, rows.shape[1])
    gathered = pl.pallas_call(
        plane_gather_kernel,
        out_shape=jax.ShapeDtypeStruct((32, *grouped.shape), rows.dtype),
        in_specs=[HBM],
        out_specs=HBM,
        scratch_shapes=[
            pltpu.SemaphoreType.DMA((2, 20)),
            pltpu.SemaphoreType.DMA((2, 20)),
            pltpu.SemaphoreType.DMA((32,)),
            pltpu.SemaphoreType.DMA((32,)),
            pltpu.SemaphoreType.DMA,
        ],
        compiler_params=pltpu.CompilerParams(
            collective_id=collective_id, has_side_effects=True, vmem_limit_bytes=62 * 2**20
        ),
        cost_estimate=pl.CostEstimate(
            flops=0, bytes_accessed=64 * rows.size * rows.dtype.itemsize, transcendentals=0
        ),
        name=name,
    )(grouped)
    return gathered.reshape(32 * rows.shape[0], rows.shape[1])


def line_peers():
    e, t = lax.axis_index("expert"), lax.axis_index("tensor")
    return [(e, lax.rem(t + k, 4)) for k in (1, 2, 3)]


class Line:
    def __init__(self, src, out, taken, ssem, rsem):
        t = lax.axis_index("tensor")
        self.src, self.out, self.taken, self.ssem, self.rsem = src, out, taken, ssem, rsem
        self.share, self.t = src.shape[0] // 4, t
        self.others = line_peers()

    def share_out(self, k):
        device = self.others[k - 1]
        return pltpu.make_async_remote_copy(
            src_ref=self.src.at[pl.ds(device[1] * self.share, self.share)],
            dst_ref=self.taken.at[k - 1],
            send_sem=self.ssem.at[0, k - 1],
            recv_sem=self.rsem.at[0, k - 1],
            device_id=device,
            device_id_type=MESH,
        )

    def pass_on(self, k):
        rows = pl.ds(self.t * self.share, self.share)
        return pltpu.make_async_remote_copy(
            src_ref=self.out.at[rows],
            dst_ref=self.out.at[rows],
            send_sem=self.ssem.at[1, k - 1],
            recv_sem=self.rsem.at[1, k - 1],
            device_id=self.others[k - 1],
            device_id_type=MESH,
        )

    def scatter(self):
        for k in (2, 1, 3):
            self.share_out(k).start()

    def add(self):
        for k in (2, 1, 3):
            self.share_out(k).wait_recv()

        def step(i, carry):
            total = self.src[self.t * self.share + i].astype(jnp.float32)
            for k in range(3):
                total = total + self.taken[k, i].astype(jnp.float32)
            self.out[self.t * self.share + i] = total.astype(self.out.dtype)
            return carry

        lax.fori_loop(0, self.share, step, 0)

    def gather(self):
        for k in (2, 1, 3):
            self.pass_on(k).start()

    def finish(self):
        for k in (2, 1, 3):
            self.pass_on(k).wait_recv()
        for k in (2, 1, 3):
            self.share_out(k).wait_send()
            self.pass_on(k).wait_send()


def line_sum_kernel(src, out, taken, ssem, rsem):
    line = Line(src, out, taken, ssem, rsem)
    greet(line.others)
    line.scatter()
    line.add()
    line.gather()
    line.finish()


PLANE_STEPS = 1 + 8 + 16 + 2 + 4 + 2


def plane_sum_steps(source, emit, scratch):
    mine, peer, one, two, last_one, last_two, lsem, pssem, prsem, ssem, rsem = scratch
    t, x, z, c = place()
    groups = mine.shape[2]
    half, quarter = groups // 2, groups // 4
    sibling = (at(x, z, 1 - c), t)
    along_x = [(at(wrap(x - 1), z, c), t), (at(wrap(x + 1), z, c), t)]
    along_z = [(at(x, wrap(z - 1), c), t), (at(x, wrap(z + 1), c), t)]
    order = (2, 1, 3, 0)
    sent = []

    def view(ref, h, a, b):
        if h == 0:
            return ref.at[a, b, pl.ds(0, half)]
        return ref.at[b, a, pl.ds(half, half)]

    def target(dx, dz, core):
        return at(wrap(x + dx), wrap(z + dz), core)

    def outward(dx, dz):
        return pltpu.make_async_remote_copy(
            src_ref=source.at[target(dx, dz, 1 - c)],
            dst_ref=peer.at[dx, dz],
            send_sem=pssem.at[dx, dz],
            recv_sem=prsem.at[dx, dz],
            device_id=sibling,
            device_id_type=MESH,
        )

    def inward(dx, dz):
        return pltpu.make_async_copy(
            source.at[target(dx, dz, c)], mine.at[dx, dz], lsem.at[dx, dz]
        )

    def hop(h, slot, src, dst, device):
        return pltpu.make_async_remote_copy(
            src_ref=src,
            dst_ref=dst,
            send_sem=ssem.at[h, slot],
            recv_sem=rsem.at[h, slot],
            device_id=device,
            device_id_type=MESH,
        )

    def ring(h, stage):
        return along_x if (h == 0) == (stage == 1) else along_z

    def first(h, b, side):
        return hop(
            h,
            4 * b + side,
            view(mine, h, 2, b).at[pl.ds(side * quarter, quarter)],
            one.at[h, b, side],
            ring(h, 1)[1 - side],
        )

    def second(h, b, side):
        return hop(
            h, 4 * b + 2 + side, view(mine, h, 1 + 2 * side, b), two.at[h, b, side], ring(h, 1)[1 - side]
        )

    def third(h, side):
        return hop(
            h,
            16 + side,
            view(mine, h, 0, 2).at[pl.ds(side * quarter, quarter)],
            last_one.at[h, side],
            ring(h, 2)[1 - side],
        )

    def fourth(h, side):
        return hop(
            h, 18 + side, view(mine, h, 0, 1 + 2 * side), last_two.at[h, side], ring(h, 2)[1 - side]
        )

    def go(copy):
        copy.start()
        sent.append(copy)

    def accumulate(into, sources_of, number):
        def step(i, carry):
            total = into[i].astype(jnp.float32)
            for source in sources_of:
                total = total + source[i].astype(jnp.float32)
            into[i] = total.astype(into.dtype)
            return carry

        lax.fori_loop(0, number, step, 0)

    spots = [(2, 2), (2, 1), (1, 2), (2, 3), (3, 2), (2, 0), (0, 2), (1, 1)]
    spots += [(1, 3), (3, 1), (3, 3), (1, 0), (0, 1), (3, 0), (0, 3), (0, 0)]
    for spot in spots:
        inward(*spot).start()
        go(outward(*spot))
    merged = set()

    yield

    def merge(h, a, b):
        spot = (a, b) if h == 0 else (b, a)
        if spot in merged:
            return
        merged.add(spot)
        inward(*spot).wait()
        outward(*spot).wait_recv()
        accumulate(mine.at[spot[0], spot[1]], [peer.at[spot[0], spot[1]]], groups)

    for b in order:
        for h in (0, 1):
            merge(h, 2, b)
            for side in (0, 1):
                go(first(h, b, side))
            yield
    for side in (0, 1):
        for b in order:
            for h in (0, 1):
                a = 1 + 2 * side
                merge(h, a, b)
                first(h, b, side).wait_recv()
                accumulate(
                    view(mine, h, a, b).at[pl.ds(side * quarter, quarter)],
                    [one.at[h, b, side]],
                    quarter,
                )
                go(second(h, b, side))
                yield

    def gathered_here(h, b):
        merge(h, 0, b)
        for side in (0, 1):
            second(h, b, side).wait_recv()
        accumulate(view(mine, h, 0, b), [two.at[h, b, 0], two.at[h, b, 1]], half)

    for h in (0, 1):
        gathered_here(h, 2)
        for side in (0, 1):
            go(third(h, side))
        yield
    for side in (0, 1):
        b = 1 + 2 * side
        for h in (0, 1):
            gathered_here(h, b)
            third(h, side).wait_recv()
            accumulate(
                view(mine, h, 0, b).at[pl.ds(side * quarter, quarter)],
                [last_one.at[h, side]],
                quarter,
            )
            go(fourth(h, side))
            yield
    for h in (0, 1):
        gathered_here(h, 0)
        for side in (0, 1):
            fourth(h, side).wait_recv()

        def finish(i, carry, h=h):
            total = mine[0, 0, h * half + i].astype(jnp.float32)
            for side in (0, 1):
                total = total + last_two[h, side, i].astype(jnp.float32)
            emit(h * half + i, total)
            return carry

        lax.fori_loop(0, half, finish, 0)
        yield
    for copy in sent:
        copy.wait_send()


def plane_peers():
    t, x, z, c = place()
    return [
        (at(x, z, 1 - c), t),
        (at(wrap(x - 1), z, c), t),
        (at(wrap(x + 1), z, c), t),
        (at(x, wrap(z - 1), c), t),
        (at(x, wrap(z + 1), c), t),
    ]


def plane_scratch(groups, width):
    half, quarter = groups // 2, groups // 4
    low = jnp.bfloat16
    return [
        pltpu.VMEM((4, 4, groups, 8, width), low),
        pltpu.VMEM((4, 4, groups, 8, width), low),
        pltpu.VMEM((2, 4, 2, quarter, 8, width), low),
        pltpu.VMEM((2, 4, 2, half, 8, width), low),
        pltpu.VMEM((2, 2, quarter, 8, width), low),
        pltpu.VMEM((2, 2, half, 8, width), low),
        pltpu.SemaphoreType.DMA((4, 4)),
        pltpu.SemaphoreType.DMA((4, 4)),
        pltpu.SemaphoreType.DMA((4, 4)),
        pltpu.SemaphoreType.DMA((2, 20)),
        pltpu.SemaphoreType.DMA((2, 20)),
    ]


def line_scratch(groups, width):
    return [
        pltpu.VMEM((3, groups // 4, 8, width), jnp.bfloat16),
        pltpu.SemaphoreType.DMA((2, 3)),
        pltpu.SemaphoreType.DMA((2, 3)),
    ]


def advance(task, number):
    for _ in range(number):
        next(task, None)


def by_expert(part, groups):
    return part.reshape(32, groups, 8, part.shape[1])


def by_group(part):
    return part.reshape(part.shape[0] // 8, 8, part.shape[1])


def communicate(kernel, collective_id, name, operands, where, out_shapes, scratch, moved):
    vmem = pl.BlockSpec(memory_space=pltpu.VMEM)
    shapes = [jax.ShapeDtypeStruct(shape, dtype) for shape, dtype in out_shapes]
    return pl.pallas_call(
        kernel,
        out_shape=shapes,
        in_specs=[vmem if inside else HBM for inside in where],
        out_specs=[vmem] * len(shapes),
        scratch_shapes=scratch,
        compiler_params=pltpu.CompilerParams(
            collective_id=collective_id, has_side_effects=True, vmem_limit_bytes=60 * 2**20
        ),
        cost_estimate=pl.CostEstimate(flops=0, bytes_accessed=moved, transcendentals=0),
        name=name,
    )(*operands)


def sum_tokens_kernel(source, shared, out, held, taken, line_ssem, line_rsem, *scratch):
    half = out.shape[0] // 2

    def emit(i, total):
        held[i] = (total + shared[i]).astype(held.dtype)

    greet(plane_peers() + line_peers())
    plane = plane_sum_steps(source, emit, scratch)
    lines = []
    for h in (0, 1):
        rows = pl.ds(h * half, half)
        lines.append(
            Line(held.at[rows], out.at[rows], taken.at[h], line_ssem.at[h], line_rsem.at[h])
        )
    advance(plane, PLANE_STEPS - 1)
    lines[0].scatter()
    advance(plane, 1)
    lines[1].scatter()
    for line in lines:
        line.add()
        line.gather()
    for line in lines:
        line.finish()
    advance(plane, 1)


def sum_tokens(part, shared, collective_id):
    groups, width = part.shape[0] // 256, part.shape[1]
    (summed,) = communicate(
        sum_tokens_kernel,
        collective_id,
        "sum_tokens",
        (by_expert(part, groups), by_group(shared)),
        (False, True),
        (((groups, 8, width), jnp.bfloat16),),
        [
            pltpu.VMEM((groups, 8, width), jnp.bfloat16),
            pltpu.VMEM((2, 3, groups // 8, 8, width), jnp.bfloat16),
            pltpu.SemaphoreType.DMA((2, 2, 3)),
            pltpu.SemaphoreType.DMA((2, 2, 3)),
        ]
        + plane_scratch(groups, width),
        16 * part.size,
    )
    return summed.reshape(8 * groups, width)


def reach_back_peers():
    t, x, z, c = place()
    along = [(at(x, wrap(z - r), c), t) for r in (1, 2, 3)]
    return [(at(x, z, 1 - c), t), (at(wrap(x - 1), z, c), t)] + along


def reach_back_run(src, out, lsem, ssem, rsem, pssem, prsem):
    t, x, z, c = place()
    sibling = (at(x, z, 1 - c), t)
    own = pltpu.make_async_copy(src, out.at[8], lsem)
    own.start()

    def onward():
        return pltpu.make_async_remote_copy(
            src_ref=src,
            dst_ref=out.at[0],
            send_sem=ssem.at[3],
            recv_sem=rsem.at[3],
            device_id=(at(wrap(x + 1), z, c), t),
            device_id_type=MESH,
        )

    def along(r, source):
        return pltpu.make_async_remote_copy(
            src_ref=source,
            dst_ref=out.at[8 - 2 * r],
            send_sem=ssem.at[r - 1],
            recv_sem=rsem.at[r - 1],
            device_id=(at(x, wrap(z + r), c), t),
            device_id_type=MESH,
        )

    def near(i):
        return pltpu.make_async_remote_copy(
            src_ref=out.at[8 - 2 * (i + c)],
            dst_ref=out.at[7 - 2 * i],
            send_sem=pssem.at[i],
            recv_sem=prsem.at[i],
            device_id=sibling,
            device_id_type=MESH,
        )

    onward().start()
    for r in (2, 1, 3):

        @pl.when(z + r < 4)
        def _(r=r):
            along(r, src).start()

    own.wait()
    onward().wait_recv()
    for r in (2, 3, 1):

        @pl.when(z + r >= 4)
        def _(r=r):
            along(r, out.at[0]).start()

    for r in (1, 3, 2):
        along(r, src).wait_recv()
    for i in range(4):
        near(i).start()
    for i in range(4):
        near(i).wait()
    onward().wait_send()
    for r in (1, 2, 3):
        along(r, src).wait_send()


def chip_at(x, z, c, distance):
    place_on = lax.rem(x * 4 + z + 16 + distance, 16)
    return place_on * 2 + c


def send_back_steps(src, out, held, near_in, far_in, ssem, rsem, pssem, prsem):
    t, x, z, c = place()
    groups = out.shape[0]
    sibling = (at(x, z, 1 - c), t)
    behind = [(chip_at(x, z, c, -k), t) for k in (1, 2, 3, 4)]

    def near(i):
        return pltpu.make_async_remote_copy(
            src_ref=src.at[7 - 2 * i],
            dst_ref=near_in.at[i],
            send_sem=pssem.at[i],
            recv_sem=prsem.at[i],
            device_id=sibling,
            device_id_type=MESH,
        )

    def far(k):
        return pltpu.make_async_remote_copy(
            src_ref=held.at[k],
            dst_ref=far_in.at[k - 1],
            send_sem=ssem.at[k - 1],
            recv_sem=rsem.at[k - 1],
            device_id=behind[k - 1],
            device_id_type=MESH,
        )

    for i in (3, 2, 1, 0):
        near(i).start()
    yield
    for i in (3, 2, 1, 0):
        near(i).wait_recv()
    for k in (4, 3, 2, 1, 0):

        def step(i, carry, k=k):
            total = src[8 - 2 * k, i].astype(jnp.float32)
            other = near_in[jnp.clip(k - c, 0, 3), i].astype(jnp.float32)
            covered = jnp.logical_and(k - c >= 0, k - c <= 3)
            total = total + jnp.where(covered, other, jnp.zeros_like(other))
            held[k, i] = total.astype(held.dtype)
            return carry

        lax.fori_loop(0, groups, step, 0)
        if k > 0:
            far(k).start()
    yield
    for k in (1, 2, 3, 4):
        far(k).wait_recv()

    def last(i, carry):
        total = held[0, i].astype(jnp.float32)
        for k in range(4):
            total = total + far_in[k, i].astype(jnp.float32)
        out[i] = total.astype(out.dtype)
        return carry

    lax.fori_loop(0, groups, last, 0)
    yield
    for k in (1, 2, 3, 4):
        far(k).wait_send()
    for i in range(4):
        near(i).wait_send()


def contract(left_side, right_side, left_dim, right_dim):
    return lax.dot_general(
        left_side,
        right_side,
        (((left_dim,), (right_dim,)), ((), ())),
        preferred_element_type=jnp.float32,
    )


def experts_kernel(
    token_rows,
    grad_rows,
    gate_in,
    up_in,
    down_in,
    routed_out,
    back_out,
    gate_out,
    up_out,
    down_out,
    ranks,
    rows_x,
    rows_g,
    weights,
    dots,
    staged,
    gate_up,
    down,
    hidden,
    grads,
    sums_one,
    sums_two,
    in_sem,
    out_sem,
):
    step = pl.program_id(0)
    low = jnp.bfloat16
    units = down_in.shape[1]
    wide = down.shape[0]
    pair_slots = 48
    width = rows_x.shape[2]
    blocks = ranks.shape[0]
    count = rows_x.shape[1]
    part = 256

    def load(k, expert):
        source = (gate_in, up_in, down_in)[k].at[expert]
        return pltpu.make_async_copy(source, staged.at[k], in_sem.at[k])

    def store(k, expert):
        if k == 2:
            source = sums_two.at[pl.ds(0, units)]
        else:
            source = sums_one.at[pl.ds(k * wide, units)]
        target = (gate_out, up_out, down_out)[k].at[expert]
        return pltpu.make_async_copy(source, target, out_sem.at[k])

    def picks(block):
        row = lax.broadcasted_iota(jnp.int32, (pair_slots, 256), 0)
        column = lax.broadcasted_iota(jnp.int32, (pair_slots, 256), 1)
        second = row >= 24
        slot = jnp.where(second, row - 24, row).astype(jnp.float32)
        inside = second == (column >= 128)
        found = []
        for expert in (0, 1):
            rank = ranks[block, expert : expert + 1, :]
            found.append(jnp.logical_and(rank == slot, inside))
        return found

    @pl.when(step == 0)
    def _():
        for k in range(3):
            load(k, 0).start()

    def rank_slots(block):
        square = (128, 128)
        same = lax.broadcasted_iota(jnp.int32, square, 0) == lax.broadcasted_iota(
            jnp.int32, square, 1
        )
        turned = contract(
            jnp.where(same, 1.0, 0.0).astype(low), token_rows[0, :, width:], 1, 1
        )
        first = lax.broadcasted_iota(jnp.int32, (256, 256), 0)
        second = lax.broadcasted_iota(jnp.int32, (256, 256), 1)
        ahead = jnp.logical_and(first < second, (first >= 128) == (second >= 128))
        line = lax.broadcasted_iota(jnp.int32, (8, 256), 0)
        named = jnp.zeros((8, 256), jnp.float32)
        shares = jnp.zeros((8, 256), jnp.float32)
        for expert in (0, 1):
            number = (lax.axis_index("expert") * 2 + expert).astype(jnp.float32)
            match = turned[0:8] == number
            present = jnp.sum(jnp.where(match, 1.0, 0.0), 0, keepdims=True)
            share = jnp.sum(jnp.where(match, turned[8:16] + turned[16:24], 0.0), 0, keepdims=True)
            named = named + jnp.where(line == expert, present, 0.0)
            shares = shares + jnp.where(line == 2 + expert, share, 0.0)
        rank = contract(named.astype(low), jnp.where(ahead, 1.0, 0.0).astype(low), 1, 0)
        rank = jnp.where(named > 0.0, rank, -1.0)
        ranks[block] = jnp.where(line < 2, rank, shares)

    @pl.when(step < blocks)
    def _():
        rank_slots(step)
        found = picks(step)
        pick = jnp.concatenate([jnp.where(f, 1.0, 0.0) for f in found], 0).astype(low)
        from_x = contract(pick, token_rows[0, :, :width], 1, 0).astype(low)
        from_g = contract(pick, grad_rows[0], 1, 0).astype(low)
        here = pl.ds(pl.multiple_of(step * pair_slots, pair_slots), pair_slots)
        for expert in (0, 1):
            lines = slice(expert * pair_slots, (expert + 1) * pair_slots)
            rows_x[expert, here, :] = from_x[lines]
            rows_g[expert, here, :] = from_g[lines]
            shares = ranks[step, 2 + expert : 3 + expert, :]
            weight = jnp.sum(jnp.where(found[expert], shares, 0.0), 1, keepdims=True)
            weights[expert, here, :] = jnp.broadcast_to(weight, (pair_slots, 128))

    for expert in (0, 1):

        @pl.when(step == blocks + expert)
        def _(expert=expert):
            for k in range(3):
                load(k, expert).wait()
            nothing = jnp.zeros((wide - units, width), low)
            gate_up[pl.ds(units, wide - units), :] = nothing
            gate_up[pl.ds(wide + units, wide - units), :] = nothing
            down[pl.ds(units, wide - units), :] = nothing

            def cast(i, carry):
                rows = pl.ds(pl.multiple_of(i * 32, 32), 32)
                gate_up[rows, :] = staged[0, rows, :].astype(low)
                gate_up[pl.ds(pl.multiple_of(wide + i * 32, 32), 32), :] = staged[
                    1, rows, :
                ].astype(low)
                down[rows, :] = staged[2, rows, :].astype(low)
                return carry

            lax.fori_loop(0, units // 32, cast, 0)
            if expert == 0:
                for k in range(3):
                    load(k, 1).start()

            def middle(i, carry):
                rows = pl.ds(pl.multiple_of(i * part, part), part)
                before = contract(rows_x[expert, rows, :], gate_up[...], 1, 1)
                plain = contract(rows_g[expert, rows, :], down[...], 1, 1)
                weight = weights[expert, rows, :][:, 0:1]
                gate, up = before[:, :wide], before[:, wide:]
                sigmoid = 1.0 / (1.0 + jnp.exp(-gate))
                on = gate * sigmoid
                value = on * up
                hidden[rows, :] = (weight * value).astype(low)
                dot = jnp.sum(plain * value, 1, keepdims=True)
                mine = 64 + lax.axis_index("expert") * 2 + expert
                lane = lax.broadcasted_iota(jnp.int32, (part, 128), 1)
                dots[expert, rows, :] = jnp.where(lane == mine, dot, 0.0).astype(low)
                change = weight * plain
                grads[rows, :wide] = (change * up * (sigmoid * (1.0 + gate * (1.0 - sigmoid)))).astype(
                    low
                )
                grads[rows, wide:] = (change * on).astype(low)
                return carry

            lax.fori_loop(0, count // part, middle, 0)
            if expert == 1:
                for k in range(3):
                    store(k, 0).wait()

            def weight_grads(i, carry):
                columns = pl.ds(pl.multiple_of(i * part, part), part)
                sums_one[columns, :] = contract(grads[:, columns], rows_x[expert], 0, 0)
                return carry

            lax.fori_loop(0, 2 * wide // part, weight_grads, 0)
            for i in range(wide // 128):
                columns = pl.ds(i * 128, 128)
                sums_two[columns, :] = contract(hidden[:, columns], rows_g[expert], 0, 0)
            for k in range(3):
                store(k, expert).start()

            def results(i, carry):
                rows = pl.ds(pl.multiple_of(i * part, part), part)
                rows_x[expert, rows, :] = contract(hidden[rows, :], down[...], 1, 0).astype(low)
                rows_g[expert, rows, :] = contract(grads[rows, :], gate_up[...], 1, 0).astype(low)
                return carry

            lax.fori_loop(0, count // part, results, 0)

    @pl.when(step >= blocks + 2)
    def _():
        block = step - blocks - 2
        pick = jnp.concatenate([jnp.where(f, 1.0, 0.0) for f in picks(block)], 0).astype(low)
        here = pl.ds(pl.multiple_of(block * pair_slots, pair_slots), pair_slots)

        def both(ref):
            return jnp.concatenate([ref[0, here, :], ref[1, here, :]], 0)

        routed_out[0] = contract(pick, both(rows_x), 0, 0).astype(low)
        back_out[0, :, :width] = contract(pick, both(rows_g), 0, 0).astype(low)
        back_out[0, :, width:] = contract(pick, both(dots), 0, 0).astype(low)

    @pl.when(step == 2 * blocks + 1)
    def _():
        for k in range(3):
            store(k, 1).wait()


def experts(token_rows, grad_rows, gate, up, down):
    low = jnp.bfloat16
    blocks = token_rows.shape[0]
    local, units, width = down.shape
    wide = (units + 127) // 128 * 128
    count = blocks * 48
    last = blocks - 1

    def entering(i):
        return (jnp.minimum(i, last), 0, 0)

    def leaving(i):
        return (jnp.maximum(i - blocks - 2, 0), 0, 0)

    weight = jax.ShapeDtypeStruct((local, units, width), jnp.float32)
    return pl.pallas_call(
        experts_kernel,
        grid=(2 * blocks + 2,),
        out_shape=(
            jax.ShapeDtypeStruct((blocks, 256, width), low),
            jax.ShapeDtypeStruct((blocks, 256, width + 128), low),
            weight,
            weight,
            weight,
        ),
        in_specs=[
            pl.BlockSpec((1, 256, width + 128), entering),
            pl.BlockSpec((1, 256, width), entering),
            HBM,
            HBM,
            HBM,
        ],
        out_specs=(
            pl.BlockSpec((1, 256, width), leaving),
            pl.BlockSpec((1, 256, width + 128), leaving),
            HBM,
            HBM,
            HBM,
        ),
        scratch_shapes=[
            pltpu.VMEM((blocks, 8, 256), jnp.float32),
            pltpu.VMEM((local, count, width), low),
            pltpu.VMEM((local, count, width), low),
            pltpu.VMEM((local, count, 128), jnp.float32),
            pltpu.VMEM((local, count, 128), low),
            pltpu.VMEM((3, units, width), jnp.float32),
            pltpu.VMEM((2 * wide, width), low),
            pltpu.VMEM((wide, width), low),
            pltpu.VMEM((count, wide), low),
            pltpu.VMEM((count, 2 * wide), low),
            pltpu.VMEM((2 * wide, width), jnp.float32),
            pltpu.VMEM((wide, width), jnp.float32),
            pltpu.SemaphoreType.DMA((3,)),
            pltpu.SemaphoreType.DMA((3,)),
        ],
        compiler_params=pltpu.CompilerParams(
            dimension_semantics=("arbitrary",), vmem_limit_bytes=60 * 2**20
        ),
        cost_estimate=pl.CostEstimate(
            flops=18 * local * count * wide * width,
            bytes_accessed=100 * 2**20,
            transcendentals=local * count * wide,
        ),
        name="experts",
    )(token_rows, grad_rows, gate, up, down)


def rms_forward(values, gains):
    inverse = lax.rsqrt(jnp.mean(values * values, -1, keepdims=True) + epsilon)
    return (values * inverse * gains, inverse)


def rope_tables(positions):
    half_dim = ROPE // 2
    freqs = rope_base ** (-jnp.arange(half_dim, dtype=jnp.float32) / half_dim)
    angles = positions.astype(jnp.float32)[:, None] * freqs[None, :]
    return (jnp.cos(angles), jnp.sin(angles))


HEADS = 4
SCALE = (NOPE + ROPE) ** (-0.5)


def in_groups(values):
    return values.reshape(values.shape[0] // 8, 8, values.shape[1])


def lanes(shape):
    return lax.broadcasted_iota(jnp.int32, shape, 1)


def turn_tables(cosine, sine_tab):
    lane = lanes(cosine.shape)
    kept = jnp.where(lane < 64, cosine, 0.0)
    crossed = jnp.where(lane < 32, -sine_tab, jnp.where(lane < 64, sine_tab, 0.0))
    return kept, crossed


def exchange_halves(values):
    shape = (128, 128)
    to = lanes(shape)
    from_lane = lax.broadcasted_iota(jnp.int32, shape, 0)
    other = jnp.where(to < 32, to + 32, jnp.where(to < 64, to - 32, to))
    swap = jnp.where(from_lane == other, 1.0, 0.0)
    return lax.dot_general(
        values,
        swap,
        (((1,), (0,)), ((), ())),
        precision=lax.Precision.HIGHEST,
        preferred_element_type=jnp.float32,
    )


def fold_matrix():
    shape = (128, 256)
    to = lanes(shape)
    wanted = jnp.where(to >= 128, 32, 0) + lax.rem(to, 32)
    return jnp.where(lax.broadcasted_iota(jnp.int32, shape, 0) == wanted, 1.0, 0.0).astype(
        jnp.bfloat16
    )


def head_lanes(values, head):
    lane = lanes(values.shape)
    inside = jnp.logical_and(lane >= 32 * head, lane < 32 * head + 32)
    return jnp.where(inside, values, jnp.zeros_like(values))


def pack_kernel(
    query,
    latent,
    gain_one,
    gain_two,
    gain_latent,
    output,
    expand,
    gate,
    router,
    up,
    down,
    attention_out,
    ffn_out,
):
    low = jnp.bfloat16
    shard = query.shape[0]
    for head in range(HEADS):
        start = 192 * head
        attention_out[:, 128 * head : 128 * head + 128] = query[:, start : start + 128].astype(low)
    for half in (0, 1):
        starts = [192 * head + 128 + 32 * half for head in range(HEADS)]
        pieces = [query[:, start : start + 32] for start in starts]
        to = 512 + 128 * half
        attention_out[:, to : to + 128] = jnp.concatenate(pieces, 1).astype(low)
    attention_out[:, 768:1280] = latent[:, :RANK].astype(low)
    row = lax.broadcasted_iota(jnp.int32, (shard, shard), 0)
    gains = jnp.where(row == 0, gain_one[...], 0.0)
    gains = jnp.where(row == 1, gain_two[...], gains)
    gains = jnp.where(row == 2, gain_latent[...], gains)
    attention_out[:, 1280:1408] = jnp.concatenate([latent[:, RANK:], gains], 1).astype(low)
    attention_out[:, 1408:1920] = output[...].astype(low)
    for j in range(4):
        attention_out[16 * j : 16 * j + 16, 1920:] = expand[:, 256 * j : 256 * j + 256].astype(low)
    gap = jnp.zeros((shard, 64), jnp.float32)
    for k, (wide, narrow) in enumerate(((gate, router[...]), (up, gap), (down, gap))):
        start = 768 * k
        ffn_out[:, start : start + 640] = wide[:, :640].astype(low)
        ffn_out[:, start + 640 : start + 768] = jnp.concatenate(
            [wide[:, 640:704], narrow], 1
        ).astype(low)


def project_kernel(
    hidden,
    weights,
    gain,
    gain_latent,
    cosine,
    sine_tab,
    normed_out,
    query_out,
    latent_out,
    keys_out,
    key_row,
    landed,
    *scratch,
):
    low = jnp.bfloat16
    peers = reach_back_peers()
    call(peers)
    normed = rms_forward(hidden[...].astype(jnp.float32), gain[...])[0].astype(low)
    normed_out[...] = normed
    query = contract(normed, weights[:, :768], 1, 0)
    first, second = query[:, 512:640], query[:, 640:768]
    cos, sin = cosine[...], sine_tab[...]
    query_out[:, :512] = query[:, :512].astype(low)
    query_out[:, 512:640] = (first * cos - second * sin).astype(low)
    query_out[:, 640:768] = (second * cos + first * sin).astype(low)
    latent = contract(normed, weights[:, 768:1408], 1, 0)
    latent_out[...] = latent[:, :RANK]
    compressed = rms_forward(latent[:, :RANK], gain_latent[...])[0]
    key_row[:, :, :RANK] = in_groups(compressed).astype(low)
    rope = latent[:, RANK:]
    kept, crossed = turn_tables(cos, sin)
    turned = rope * kept + exchange_halves(rope) * crossed
    key_row[:, :, RANK:] = in_groups(turned).astype(low)
    hear(peers)
    reach_back_run(key_row, landed, *scratch)
    keys_out[...] = landed[...]


def attend_kernel(
    keys,
    expand,
    query,
    own_segment,
    key_segment,
    wo_0,
    wo_1,
    wo_2,
    wo_3,
    out,
    attended,
    probs,
    expanded,
    key_rope,
    held,
    landed,
    *scratch,
):
    low = jnp.bfloat16
    peers = line_peers()
    call(peers)
    rows = query.shape[0]
    count = keys.shape[0]
    fold = fold_matrix()

    def expand_rows(i, carry):
        part = pl.ds(pl.multiple_of(i * rows, rows), rows)
        expanded[part, :] = contract(keys[part, :RANK], expand[...], 1, 0).astype(low)
        key_rope[part, :] = contract(keys[part, RANK:], fold, 1, 0).astype(low)
        return carry

    lax.fori_loop(0, count // rows, expand_rows, 0)
    shape = (rows, count)
    distance = lax.broadcasted_iota(jnp.int32, shape, 0) + WINDOW - lanes(shape)
    allowed = jnp.logical_and(distance >= 0, distance < WINDOW)
    allowed = jnp.logical_and(allowed, own_segment[...] == key_segment[...])
    total = jnp.zeros((rows, wo_0.shape[0]), jnp.float32)
    for head, wo in enumerate((wo_0, wo_1, wo_2, wo_3)):
        start = 256 * head
        scores = contract(query[:, 128 * head : 128 * head + 128], expanded[:, start : start + 128], 1, 1)
        scores += contract(head_lanes(query[:, 512:640], head), key_rope[:, :128], 1, 1)
        scores += contract(head_lanes(query[:, 640:768], head), key_rope[:, 128:], 1, 1)
        scores = jnp.where(allowed, scores * SCALE, masked_score)
        exponent = jnp.exp(scores - jnp.max(scores, 1, keepdims=True))
        share = exponent / jnp.sum(exponent, 1, keepdims=True)
        probs[head] = share
        mixed = contract(share.astype(low), expanded[:, start + 128 : start + 256], 1, 0).astype(low)
        attended[:, 128 * head : 128 * head + 128] = mixed
        total += contract(mixed, wo[...], 1, 1)
    held[...] = in_groups(total).astype(low)
    hear(peers)
    line = Line(held, landed, *scratch)
    line.scatter()
    line.add()
    line.gather()
    line.finish()
    out[...] = landed[...]


def route_kernel(hidden, attention, gain, router, routes, token_out, middle_out, gates_out):
    low = jnp.bfloat16
    middle = hidden[...].astype(jnp.float32) + attention[...].astype(jnp.float32)
    middle_out[...] = middle
    normed = rms_forward(middle, gain[...])[0].astype(low)
    width = normed.shape[1]
    token_out[:, :width] = normed
    logits = contract(normed, router[...], 1, 0)
    lane = lanes(logits.shape)
    named = [routes[:, r : r + 1] for r in range(6)]
    chosen = [
        jnp.sum(jnp.where(lane == number + 64, logits, 0.0), 1, keepdims=True) for number in named
    ]
    most = functools.reduce(jnp.maximum, chosen)
    exponents = [jnp.exp(value - most) for value in chosen]
    total = functools.reduce(jnp.add, exponents)
    extra = jnp.where(jnp.logical_or(lane == 6, lane == 7), 128.0, 0.0)
    gates = jnp.zeros(logits.shape, jnp.float32)
    for r in range(6):
        weight = exponents[r] / total
        high = weight.astype(low).astype(jnp.float32)
        extra += jnp.where(lane == r, named[r].astype(jnp.float32), 0.0)
        extra += jnp.where(lane == 8 + r, high, 0.0)
        extra += jnp.where(lane == 16 + r, weight - high, 0.0)
        gates += jnp.where(lane == r, weight, 0.0)
    token_out[:, width:] = extra.astype(low)
    gates_out[...] = gates


def shared_kernel(normed, cotangent, weights, part_out, back_out, grads_out):
    low = jnp.bfloat16
    gate = contract(normed[...], weights[:, :768], 1, 0)
    up = contract(normed[...], weights[:, 768:1536], 1, 0)
    sigmoid = 1.0 / (1.0 + jnp.exp(-gate))
    on = gate * sigmoid
    hidden = (on * up).astype(low)
    part_out[...] = contract(hidden, weights[:, 1536:], 1, 1)
    change = contract(cotangent[...], weights[:, 1536:], 1, 0)
    grad_gate = (change * up * (sigmoid * (1.0 + gate * (1.0 - sigmoid)))).astype(low)
    grad_up = (change * on).astype(low)
    width = normed.shape[1]
    back_out[:, :width] = contract(grad_gate, weights[:, :768], 1, 1) + contract(
        grad_up, weights[:, 768:1536], 1, 1
    )
    back_out[:, width:] = jnp.zeros((normed.shape[0], 128), jnp.float32)

    def grads(i, carry):
        part = pl.ds(pl.multiple_of(i * 256, 256), 256)
        rows = normed[:, part]
        grads_out[part, :768] = contract(rows, grad_gate, 0, 0).astype(low)
        grads_out[part, 768:1536] = contract(rows, grad_up, 0, 0).astype(low)
        grads_out[part, 1536:] = contract(cotangent[:, part], hidden, 0, 0).astype(low)
        return carry

    lax.fori_loop(0, grads_out.shape[0] // 256, grads, 0)


def attend_back_kernel(
    back,
    middle,
    gain,
    gates,
    routes,
    router,
    cotangent,
    wo_0,
    wo_1,
    wo_2,
    wo_3,
    probs,
    expanded,
    key_rope,
    query,
    keys,
    expand,
    query_w,
    cosine,
    sine_tab,
    normed,
    attended,
    middle_out,
    attention_out,
    gain_out,
    logits_out,
    own_out,
    query_sum_out,
    latent_sum_out,
    changes,
    ropes,
    query_out,
    back_out,
    keys_out,
    grads_out,
    held,
    near_in,
    far_in,
    ssem,
    rsem,
    pssem,
    prsem,
    latent,
    landed_one,
    landed_two,
    *scratch,
):
    low = jnp.bfloat16
    t, x, z, c = place()
    peers = plane_peers() + line_peers() + [(chip_at(x, z, c, k), t) for k in (1, 2, 3, 4)]
    call(peers)
    width = middle.shape[1]
    rows = middle.shape[0]
    lane = lanes((rows, 128))
    sums = back[:, width:].astype(jnp.float32)
    named = [routes[:, r : r + 1] for r in range(6)]
    weight = [gates[:, r : r + 1] for r in range(6)]
    change = [
        jnp.sum(jnp.where(lane == number + 64, sums, 0.0), 1, keepdims=True) for number in named
    ]
    inner = functools.reduce(jnp.add, [w * c for w, c in zip(weight, change)])
    logits = jnp.zeros((rows, 128), jnp.float32)
    for r in range(6):
        logits += jnp.where(lane == named[r] + 64, weight[r] * (change[r] - inner), 0.0)
    logits_low = logits.astype(low)
    logits_out[...] = logits_low
    grad_normed = back[:, :width].astype(jnp.float32) + contract(logits_low, router[...], 1, 1)
    values = middle[...]
    inverse = lax.rsqrt(jnp.mean(values * values, 1, keepdims=True) + epsilon)
    weighted = grad_normed * gain[...]
    aligned = jnp.mean(values * weighted, 1, keepdims=True)
    gain_out[...] = jnp.sum(grad_normed * values * inverse, 0, keepdims=True)
    grad_middle = (
        cotangent[...].astype(jnp.float32)
        + inverse * weighted
        - values * (inverse * inverse * inverse) * aligned
    )
    middle_out[...] = grad_middle
    grad_attn = grad_middle.astype(low)
    attention_out[...] = grad_attn
    first = jnp.zeros((rows, 128), jnp.float32)
    second = jnp.zeros((rows, 128), jnp.float32)
    for head, wo in enumerate((wo_0, wo_1, wo_2, wo_3)):
        start = 256 * head
        nope, value = slice(start, start + 128), slice(start + 128, start + 256)
        own = slice(128 * head, 128 * head + 128)
        grad_mixed = contract(grad_attn, wo[...], 1, 0).astype(low)
        share = probs[head]
        changes[:, value] = contract(share.astype(low), grad_mixed, 0, 0).astype(low)
        grad_share = contract(grad_mixed, expanded[:, value], 1, 1)
        grad_scores = share * (grad_share - jnp.sum(share * grad_share, 1, keepdims=True))
        grad_scores = grad_scores.astype(low)
        query_out[:, own] = (contract(grad_scores, expanded[:, nope], 1, 0) * SCALE).astype(low)
        both = contract(grad_scores, key_rope[...], 1, 0) * SCALE
        first += head_lanes(both[:, :128], head)
        second += head_lanes(both[:, 128:], head)
        changes[:, nope] = (contract(grad_scores, query[:, own], 0, 0) * SCALE).astype(low)
        from_first = contract(grad_scores, head_lanes(query[:, 512:640], head), 0, 0) * SCALE
        from_second = contract(grad_scores, head_lanes(query[:, 640:768], head), 0, 0) * SCALE
        if head == 0:
            ropes[:, :128] = from_first
            ropes[:, 128:] = from_second
        else:
            ropes[:, :128] += from_first
            ropes[:, 128:] += from_second
    cos, sin = cosine[...], sine_tab[...]
    query_out[:, 512:640] = (first * cos + second * sin).astype(low)
    query_out[:, 640:768] = (second * cos - first * sin).astype(low)
    back_out[...] = in_groups(contract(query_out[...], query_w[...], 1, 1)).astype(low)
    fold = fold_matrix()

    def key_rows(i, carry):
        part = pl.ds(pl.multiple_of(i * rows, rows), rows)
        compressed = contract(changes[part, :], expand[...], 1, 1)
        keys_out[i, :, :, :RANK] = in_groups(compressed).astype(low)
        rope = contract(ropes[part, :].astype(low), fold, 1, 1)
        keys_out[i, :, :, RANK:] = in_groups(rope).astype(low)
        return carry

    lax.fori_loop(0, keys.shape[0] // rows, key_rows, 0)
    hear(peers)
    back = send_back_steps(keys_out, latent, held, near_in, far_in, ssem, rsem, pssem, prsem)
    advance(back, 1)
    line_one = Line(back_out, landed_one, *scratch[:3])
    line_two = Line(latent, landed_two, *scratch[3:6])
    line_one.scatter()
    advance(back, 1)
    for j in range(4):
        grad_expand = contract(keys[:, :RANK], changes[:, 256 * j : 256 * j + 256], 0, 0)
        grads_out[:, 2 * j : 2 * j + 2, :, 1280:] = grad_expand.reshape(32, 2, 8, 256).astype(low)

    def grads(i, carry):
        part = pl.ds(pl.multiple_of(i * 256, 256), 256)
        some = pl.ds(i * 4, 4)
        of_query = contract(normed[:, part], query_out[...], 0, 0)
        grads_out[some, :, :, :768] = of_query.reshape(4, 8, 8, 768).astype(low)
        of_output = contract(attention_out[:, part], attended[...], 0, 0)
        grads_out[some, :, :, 768:1280] = of_output.reshape(4, 8, 8, 512).astype(low)
        return carry

    lax.fori_loop(0, width // 256, grads, 0)
    line_one.add()
    line_one.gather()

    def emit(i, total):
        own_out[i] = total

    plane = plane_sum_steps(grads_out, emit, scratch[6:])
    advance(plane, 5)
    advance(back, 1)
    line_two.scatter()
    advance(plane, 8)
    line_two.add()
    line_two.gather()
    advance(plane, PLANE_STEPS - 13)
    line_one.finish()
    query_sum_out[...] = landed_one[...]
    line_two.finish()
    latent_sum_out[...] = landed_two[...]
    advance(back, 1)
    advance(plane, 1)


def finish_kernel(
    query_sum,
    latent_sum,
    latent,
    gain_latent,
    cosine,
    sine_tab,
    wl_0,
    wl_1,
    wl_2,
    wl_3,
    wl_4,
    hidden,
    gain,
    grad_middle,
    normed,
    normed_two,
    grad_logits,
    gain_two_grad,
    layer,
    input_out,
    own_out,
    layer_out,
    changes,
    grads_out,
    landed,
    *scratch,
):
    low = jnp.bfloat16
    peers = plane_peers() + line_peers()
    call(peers)
    grad_latent = latent_sum[:, :RANK].astype(jnp.float32)
    rope = latent_sum[:, RANK:].astype(jnp.float32)
    values = latent[...]
    inverse = lax.rsqrt(jnp.mean(values * values, 1, keepdims=True) + epsilon)
    weighted = grad_latent * gain_latent[...]
    aligned = jnp.mean(values * weighted, 1, keepdims=True)
    gain_latent_grad = jnp.sum(grad_latent * values * inverse, 0, keepdims=True)
    changes[:, :RANK] = (
        inverse * weighted - values * (inverse * inverse * inverse) * aligned
    ).astype(low)
    kept, crossed = turn_tables(cosine[...], sine_tab[...])
    changes[:, RANK:] = (rope * kept - exchange_halves(rope) * crossed).astype(low)
    grad_normed = query_sum[...].astype(jnp.float32)
    width = hidden.shape[1]
    for j, wl in enumerate((wl_0, wl_1, wl_2, wl_3, wl_4)):
        grad_normed += contract(changes[:, 128 * j : 128 * j + 128], wl[...], 1, 1)
    values = hidden[...].astype(jnp.float32)
    inverse = lax.rsqrt(jnp.mean(values * values, 1, keepdims=True) + epsilon)
    weighted = grad_normed * gain[...]
    aligned = jnp.mean(values * weighted, 1, keepdims=True)
    gain_grad = jnp.sum(grad_normed * values * inverse, 0, keepdims=True)
    input_out[...] = (
        grad_middle[...] + inverse * weighted - values * (inverse * inverse * inverse) * aligned
    ).astype(low)

    def grads(i, carry):
        part = pl.ds(pl.multiple_of(i * 256, 256), 256)
        some = pl.ds(i * 4, 4)
        rows = normed[:, part]
        of_latent = contract(rows, changes[:, :RANK], 0, 0)
        grads_out[some, :, :, :RANK] = of_latent.reshape(4, 8, 8, RANK).astype(low)
        mixed = contract(rows, changes[:, RANK:], 0, 0)
        mixed += contract(normed_two[:, part], grad_logits[...], 0, 0)
        grads_out[some, :, :, RANK : RANK + 128] = mixed.reshape(4, 8, 8, 128).astype(low)
        return carry

    lax.fori_loop(0, width // 256, grads, 0)
    grads_out[:, 1:, :, RANK + 128 :] = jnp.zeros((32, 7, 8, 128), low)
    line_number = lax.broadcasted_iota(jnp.int32, (8, 128), 0)
    gain_two = gain_two_grad[...]
    for e in range(32):
        block = jnp.zeros((8, 128), jnp.float32)
        for row, (values, size) in enumerate(
            ((gain_grad, 64), (gain_two, 64), (gain_latent_grad, 16))
        ):
            piece = values[:, size * e : size * e + size]
            piece = jnp.concatenate([piece, jnp.zeros((1, 128 - size), jnp.float32)], 1)
            block = jnp.where(line_number == row, piece, block)
        grads_out[e, 0, :, RANK + 128 :] = block.astype(low)
    hear(peers)
    line = Line(layer, landed, *scratch[:3])
    line.scatter()

    def emit(i, total):
        own_out[i] = total

    plane = plane_sum_steps(grads_out, emit, scratch[3:])
    advance(plane, 10)
    line.add()
    line.gather()
    advance(plane, PLANE_STEPS)
    line.finish()
    layer_out[...] = landed[...]


def unpack_kernel(
    own,
    last,
    ffn,
    middle,
    layer,
    layer_out,
    query_out,
    latent_out,
    router_out,
    output_out,
    gains_out,
    expand_out,
    gate_out,
    up_out,
    down_out,
):
    layer_out[...] = (middle[...] + layer[...].astype(jnp.float32)).astype(layer_out.dtype)
    for head in range(HEADS):
        query_out[:, 192 * head : 192 * head + 128] = own[:, 128 * head : 128 * head + 128]
        for half in (0, 1):
            to, start = 192 * head + 128 + 32 * half, 512 + 128 * half + 32 * head
            query_out[:, to : to + 32] = own[:, start : start + 32]
    latent_out[...] = last[:, :576]
    router_out[...] = last[:, 576:640]
    output_out[...] = own[:, 768:1280]
    gains_out[...] = last[0:8, 640:768]
    for j in range(4):
        expand_out[:, 256 * j : 256 * j + 256] = own[16 * j : 16 * j + 16, 1280:1536]
    gate_out[...] = ffn[:, :704].astype(jnp.float32)
    up_out[...] = ffn[:, 768:1472].astype(jnp.float32)
    down_out[...] = ffn[:, 1536:2240].astype(jnp.float32)


def local_call(kernel, name, operands, out_shapes, scratch=()):
    arrays, specs = [], []
    for operand in operands:
        if isinstance(operand, tuple):
            array, block, index = operand
            specs.append(pl.BlockSpec(block, lambda i, index=index: index))
        else:
            array = operand
            zeros = (0,) * array.ndim
            specs.append(pl.BlockSpec(array.shape, lambda i, zeros=zeros: zeros))
        arrays.append(array)
    shapes = [jax.ShapeDtypeStruct(shape, dtype) for shape, dtype in out_shapes]
    return pl.pallas_call(
        kernel,
        grid=(1,),
        out_shape=shapes,
        in_specs=specs,
        out_specs=[
            pl.BlockSpec(shape.shape, lambda i, zeros=(0,) * len(shape.shape): zeros)
            for shape in shapes
        ],
        scratch_shapes=[pltpu.VMEM(shape, dtype) for shape, dtype in scratch],
        compiler_params=pltpu.CompilerParams(vmem_limit_bytes=60 * 2**20),
        name=name,
    )(*arrays)


def joint_call(kernel, collective_id, name, operands, out_shapes, scratch, moved):
    arrays, specs = [], []
    for operand in operands:
        if isinstance(operand, tuple):
            array, block, index = operand
        else:
            array, block, index = operand, operand.shape, (0,) * operand.ndim
        specs.append(
            pl.BlockSpec(block, lambda i, index=index: index, pipeline_mode=pl.Buffered(1))
        )
        arrays.append(array)
    return pl.pallas_call(
        kernel,
        grid=(1,),
        out_shape=[jax.ShapeDtypeStruct(shape, dtype) for shape, dtype in out_shapes],
        in_specs=specs,
        out_specs=[
            pl.BlockSpec(
                shape,
                lambda i, zeros=(0,) * len(shape): zeros,
                pipeline_mode=pl.Buffered(1),
            )
            for shape, _ in out_shapes
        ],
        scratch_shapes=scratch,
        compiler_params=pltpu.CompilerParams(
            collective_id=collective_id, has_side_effects=True, vmem_limit_bytes=60 * 2**20
        ),
        cost_estimate=pl.CostEstimate(flops=0, bytes_accessed=moved, transcendentals=0),
        name=name,
    )(*arrays)


def column_blocks(array, first, number):
    return [(array, (array.shape[0], 128), (0, first + j)) for j in range(number)]


def body(
    hidden_in,
    cotangent,
    segments,
    routes,
    attn_norm,
    w_query,
    w_latent,
    latent_norm,
    w_expand,
    w_output,
    ffn_norm,
    w_router,
    shared_gate,
    shared_up,
    shared_down,
    expert_gate,
    routed_expert_up,
    expert_down,
):
    tokens, model_width = hidden_in.shape
    devices = lax.axis_size("expert")
    own_index = lax.axis_index("expert")
    low = jnp.bfloat16
    full = jnp.float32
    shard = w_query.shape[0]

    attention_shard, ffn_shard = local_call(
        pack_kernel,
        "pack",
        (
            w_query,
            w_latent,
            attn_norm[None],
            ffn_norm[None],
            jnp.pad(latent_norm, (0, shard - latent_norm.shape[0]))[None],
            w_output.T,
            w_expand,
            shared_gate,
            w_router,
            shared_up,
            shared_down.T,
        ),
        (((shard, 2176), low), ((shard, 2304), low)),
    )
    ffn_all = lax.all_gather(ffn_shard, "expert", axis=0, tiled=True)
    grad_rows = lax.all_gather(cotangent, "expert", axis=0)
    attention_all = plane_gather(attention_shard, 1, "gather_attention")
    gains = attention_all.reshape(devices, shard, -1)[:, :8, 1344:1408].astype(full)
    gain_one = gains[:, 0].reshape(1, -1)
    gain_two = gains[:, 1].reshape(1, -1)
    gain_latent = gains[:, 2, : latent_norm.shape[0]].reshape(1, -1)
    expand_w = (
        attention_all[:, 1920:].reshape(devices, 4, 16, 256).swapaxes(1, 2).reshape(RANK, -1)
    )
    output_blocks = column_blocks(attention_all, 11, 4)
    latent_blocks = column_blocks(attention_all, 6, 5)
    router_block = column_blocks(ffn_all, 5, 1)[0]

    first_row = own_index * tokens
    row_index = first_row + jnp.arange(tokens, dtype=jnp.int32)
    own_segments = lax.dynamic_slice_in_dim(segments, first_row, tokens)
    doc_start = jnp.sum((segments[None, :] < own_segments[:, None]).astype(jnp.int32), 1)
    cosine, sine_tab = rope_tables(row_index - doc_start)
    cosine, sine_tab = jnp.tile(cosine, (1, 4)), jnp.tile(sine_tab, (1, 4))
    key_count = 9 * tokens
    normed, queries, latent, keys_all = joint_call(
        project_kernel,
        2,
        "project",
        (
            hidden_in,
            (attention_all, (model_width, 1408), (0, 0)),
            gain_one,
            gain_latent,
            cosine,
            sine_tab,
        ),
        (
            ((tokens, model_width), low),
            ((tokens, 768), low),
            ((tokens, RANK), full),
            ((9, tokens // 8, 8, 640), low),
        ),
        [
            pltpu.VMEM((tokens // 8, 8, 640), low),
            pltpu.VMEM((9, tokens // 8, 8, 640), low),
            pltpu.SemaphoreType.DMA,
            pltpu.SemaphoreType.DMA((4,)),
            pltpu.SemaphoreType.DMA((4,)),
            pltpu.SemaphoreType.DMA((4,)),
            pltpu.SemaphoreType.DMA((4,)),
        ],
        2**25,
    )
    keys_all = keys_all.reshape(key_count, 640)
    key_segments = lax.dynamic_slice_in_dim(
        jnp.pad(segments, (key_count - tokens, 0), constant_values=-1), first_row, key_count
    )
    attn_out, attended, probs, expanded, key_rope = joint_call(
        attend_kernel,
        3,
        "attend",
        (keys_all, expand_w, queries, own_segments[:, None], key_segments[None], *output_blocks),
        (
            ((tokens // 8, 8, model_width), low),
            ((tokens, HEADS * VH), low),
            ((HEADS, tokens, key_count), full),
            ((key_count, HEADS * (NOPE + VH)), low),
            ((key_count, 256), low),
        ),
        [pltpu.VMEM((tokens // 8, 8, model_width), low)] * 2
        + line_scratch(tokens // 8, model_width),
        2**25,
    )
    attn_out = attn_out.reshape(tokens, model_width)

    token_row, middle, gates = local_call(
        route_kernel,
        "route",
        (hidden_in, attn_out, gain_two, router_block, routes),
        (
            ((tokens, model_width + 128), low),
            ((tokens, model_width), full),
            ((tokens, 128), full),
        ),
    )
    normed_two = (token_row, (tokens, model_width), (0, 0))

    shared_part, shared_back, ffn_grads = local_call(
        shared_kernel,
        "shared",
        (normed_two, cotangent, ffn_all),
        (
            ((tokens, model_width), full),
            ((tokens, model_width + 128), full),
            (ffn_all.shape, low),
        ),
    )
    own_ffn = lax.psum_scatter(ffn_grads, "expert", scatter_dimension=0, tiled=True)
    token_row, _ = lax.optimization_barrier((token_row, ffn_grads))
    token_rows = plane_gather(token_row, 4, "gather_tokens")

    routed_part, back_part, out_egate, out_eup, out_edown = experts(
        token_rows.reshape(devices // 2, 2 * tokens, -1),
        grad_rows.reshape(devices // 2, 2 * tokens, -1),
        expert_gate.swapaxes(1, 2),
        routed_expert_up.swapaxes(1, 2),
        expert_down,
    )
    out_egate, out_eup = out_egate.swapaxes(1, 2), out_eup.swapaxes(1, 2)
    routed_part, own_ffn = lax.optimization_barrier((routed_part, own_ffn))
    routed_own = lax.psum_scatter(
        routed_part.reshape(-1, model_width), "expert", scatter_dimension=0, tiled=True
    )
    layer_part = (routed_own.astype(full) + shared_part).astype(low)
    back_all = sum_tokens(back_part.reshape(devices * tokens, -1), shared_back, 5)

    (
        grad_middle,
        grad_attn,
        grad_gain_two,
        grad_logits,
        own,
        query_sum,
        latent_sum,
    ) = joint_call(
        attend_back_kernel,
        7,
        "attend_back",
        (
            back_all,
            middle,
            gain_two,
            gates,
            routes,
            router_block,
            cotangent,
            *output_blocks,
            probs,
            expanded,
            key_rope,
            queries,
            keys_all,
            expand_w,
            (attention_all, (model_width, 768), (0, 0)),
            cosine,
            sine_tab,
            normed,
            attended,
        ),
        (
            ((tokens, model_width), full),
            ((tokens, model_width), low),
            ((1, model_width), full),
            ((tokens, 128), low),
            ((shard // 8, 8, 1536), full),
            ((tokens // 8, 8, model_width), low),
            ((tokens // 8, 8, 640), low),
        ),
        [
            pltpu.VMEM((key_count, HEADS * (NOPE + VH)), low),
            pltpu.VMEM((key_count, 256), full),
            pltpu.VMEM((tokens, 768), low),
            pltpu.VMEM((tokens // 8, 8, model_width), low),
            pltpu.VMEM((9, tokens // 8, 8, 640), low),
            pltpu.VMEM((devices, shard // 8, 8, 1536), low),
            pltpu.VMEM((5, tokens // 8, 8, 640), low),
            pltpu.VMEM((4, tokens // 8, 8, 640), low),
            pltpu.VMEM((4, tokens // 8, 8, 640), low),
            pltpu.SemaphoreType.DMA((4,)),
            pltpu.SemaphoreType.DMA((4,)),
            pltpu.SemaphoreType.DMA((4,)),
            pltpu.SemaphoreType.DMA((4,)),
            pltpu.VMEM((tokens // 8, 8, 640), low),
            pltpu.VMEM((tokens // 8, 8, model_width), low),
            pltpu.VMEM((tokens // 8, 8, 640), low),
        ]
        + line_scratch(tokens // 8, model_width)
        + line_scratch(tokens // 8, 640)
        + plane_scratch(shard // 8, 1536),
        2**26,
    )
    own = own.reshape(shard, 1536)
    query_sum = query_sum.reshape(tokens, model_width)
    latent_sum = latent_sum.reshape(tokens, 640)
    grad_input, own_last, layer_sum = joint_call(
        finish_kernel,
        9,
        "finish",
        (
            query_sum,
            latent_sum,
            latent,
            gain_latent,
            cosine,
            sine_tab,
            *latent_blocks,
            hidden_in,
            gain_one,
            grad_middle,
            normed,
            normed_two,
            grad_logits,
            grad_gain_two,
            layer_part.reshape(tokens // 8, 8, model_width),
        ),
        (
            ((tokens, model_width), low),
            ((shard // 8, 8, 768), full),
            ((tokens // 8, 8, model_width), low),
        ),
        [
            pltpu.VMEM((tokens, 640), low),
            pltpu.VMEM((devices, shard // 8, 8, 768), low),
            pltpu.VMEM((tokens // 8, 8, model_width), low),
        ]
        + line_scratch(tokens // 8, model_width)
        + plane_scratch(shard // 8, 768),
        2**25,
    )
    own_last = own_last.reshape(shard, 768)
    layer_sum = layer_sum.reshape(tokens, model_width)
    (
        layer_out,
        out_query,
        out_latent,
        out_router,
        out_output,
        out_gains,
        out_expand,
        out_sgate,
        out_sup,
        out_sdown,
    ) = local_call(
        unpack_kernel,
        "unpack",
        (own, own_last, own_ffn, middle, layer_sum),
        (
            ((tokens, model_width), low),
            (w_query.shape, full),
            (w_latent.shape, full),
            (w_router.shape, full),
            ((shard, w_output.shape[0]), full),
            ((8, 128), full),
            (w_expand.shape, full),
            (shared_gate.shape, full),
            (shared_up.shape, full),
            ((shard, shared_down.shape[0]), full),
        ),
    )
    return (
        layer_out,
        grad_input,
        out_gains[0, :shard],
        out_query,
        out_latent,
        out_gains[2, : latent_norm.shape[0]],
        out_expand,
        out_output.T,
        out_gains[1, :shard],
        out_router,
        out_sgate,
        out_sup,
        out_sdown.T,
        out_egate,
        out_eup,
        out_edown,
    )


def solution(mesh):
    in_specs = (
        P("expert", None),
        P("expert", None),
        P(),
        P("expert", None),
        P("expert"),
        P("expert", "tensor"),
        P("expert", None),
        P("expert"),
        P("expert", "tensor"),
        P("tensor", "expert"),
        P("expert"),
        P("expert", None),
        P("expert", "tensor"),
        P("expert", "tensor"),
        P("tensor", "expert"),
        P("expert", None, "tensor"),
        P("expert", None, "tensor"),
        P("expert", "tensor", None),
    )
    out_specs = (
        P("expert", None),
        P("expert", None),
        P("expert"),
        P("expert", "tensor"),
        P("expert", None),
        P("expert"),
        P("expert", "tensor"),
        P("tensor", "expert"),
        P("expert"),
        P("expert", None),
        P("expert", "tensor"),
        P("expert", "tensor"),
        P("tensor", "expert"),
        P("expert", None, "tensor"),
        P("expert", None, "tensor"),
        P("expert", "tensor", None),
    )
    return jax.shard_map(body, mesh=mesh, in_specs=in_specs, out_specs=out_specs, check_vma=False)
```

```python
import functools

import jax
import jax.numpy as jnp
from jax import lax
from jax.experimental import pallas as pl
from jax.experimental.pallas import tpu as pltpu
from jax.sharding import PartitionSpec as P

NOPE = 128
ROPE = 64
VH = 128
RANK = 512
WINDOW = 1024


epsilon = 1e-06
masked_score = -1e30
rope_base = 10000.0


MESH = pl.DeviceIdType.MESH
HBM = pl.BlockSpec(memory_space=pltpu.HBM)


def place():
    e = lax.axis_index("expert")
    return lax.axis_index("tensor"), e // 8, lax.rem(e // 2, 4), lax.rem(e, 2)


def at(x, z, c):
    return (x * 4 + z) * 2 + c


def wrap(v):
    return lax.rem(v + 4, 4)


def greet(peers):
    call(peers)
    hear(peers)


def call(peers):
    barrier = pltpu.get_barrier_semaphore()
    for peer in peers:
        pl.semaphore_signal(barrier, inc=1, device_id=peer, device_id_type=MESH)


def hear(peers):
    pl.semaphore_wait(pltpu.get_barrier_semaphore(), len(peers))


def plane_gather_kernel(src, out, ssem, rsem, dssem, drsem, lsem):
    t, x, z, c = place()
    rows = src.shape[0]
    half, quarter = rows // 2, rows // 4
    sibling = (at(x, z, 1 - c), t)
    along_x = [(at(wrap(x - 1), z, c), t), (at(wrap(x + 1), z, c), t)]
    along_z = [(at(x, wrap(z - 1), c), t), (at(x, wrap(z + 1), c), t)]
    greet([sibling] + along_x + along_z)
    own = pltpu.make_async_copy(src, out.at[at(x, z, c)], lsem)
    own.start()
    sent = []

    def piece(h, j1, j2, part=None):
        if h == 0:
            index = at(wrap(x + j2), wrap(z + j1), c)
        else:
            index = at(wrap(x + j1), wrap(z + j2), c)
        if part is None:
            return index, pl.ds(h * half, half)
        return index, pl.ds(h * half + part * quarter, quarter)

    def send(h, slot, which, device, first):
        index, rows_of = which
        return pltpu.make_async_remote_copy(
            src_ref=src.at[rows_of] if first else out.at[index, rows_of],
            dst_ref=out.at[index, rows_of],
            send_sem=ssem.at[h, slot],
            recv_sem=rsem.at[h, slot],
            device_id=device,
            device_id_type=MESH,
        )

    def across(h, j1, j2):
        index, rows_of = piece(h, j1, j2)
        slot = (h * 4 + j1 % 4) * 4 + j2 % 4
        return pltpu.make_async_remote_copy(
            src_ref=src.at[rows_of] if j1 == 0 and j2 == 0 else out.at[index, rows_of],
            dst_ref=out.at[index, rows_of],
            send_sem=dssem.at[slot],
            recv_sem=drsem.at[slot],
            device_id=sibling,
            device_id_type=MESH,
        )

    def ring(h, stage):
        return along_z if (h == 0) == (stage == 1) else along_x

    def stage_one(h, kind):
        left, right = ring(h, 1)
        if kind == 0:
            return send(h, 0, piece(h, 0, 0), right, True)
        if kind == 1:
            return send(h, 1, piece(h, 0, 0), left, True)
        if kind == 2:
            return send(h, 2, piece(h, -1, 0, 0), right, False)
        return send(h, 3, piece(h, 1, 0, 1), left, False)

    def stage_two(h, j1, kind):
        left, right = ring(h, 2)
        slot = 4 + 4 * (j1 % 4) + kind
        if kind == 0:
            return send(h, slot, piece(h, j1, 0), right, j1 == 0)
        if kind == 1:
            return send(h, slot, piece(h, j1, 0), left, j1 == 0)
        if kind == 2:
            return send(h, slot, piece(h, j1, -1, 0), right, False)
        return send(h, slot, piece(h, j1, 1, 1), left, False)

    def go(copy):
        copy.start()
        sent.append(copy)

    for h in (0, 1):
        go(stage_one(h, 0))
        go(stage_one(h, 1))
        go(stage_two(h, 0, 0))
        go(stage_two(h, 0, 1))
        go(across(h, 0, 0))
    for h in (0, 1):
        for kind, j in ((0, -1), (1, 1)):
            stage_one(h, kind).wait_recv()
            go(stage_one(h, 2 + kind))
            go(stage_two(h, j, 0))
            go(stage_two(h, j, 1))
            go(across(h, j, 0))
    for h in (0, 1):
        for kind, j in ((0, -1), (1, 1)):
            stage_two(h, 0, kind).wait_recv()
            go(stage_two(h, 0, 2 + kind))
            go(across(h, 0, j))
    for h in (0, 1):
        stage_one(h, 2).wait_recv()
        stage_one(h, 3).wait_recv()
        go(stage_two(h, 2, 0))
        go(stage_two(h, 2, 1))
        go(across(h, 2, 0))
    for j1 in (-1, 1, 2):
        for h in (0, 1):
            for kind, j in ((0, -1), (1, 1)):
                stage_two(h, j1, kind).wait_recv()
                go(stage_two(h, j1, 2 + kind))
                go(across(h, j1, j))
    for j1 in (0, -1, 1, 2):
        for h in (0, 1):
            stage_two(h, j1, 2).wait_recv()
            stage_two(h, j1, 3).wait_recv()
            go(across(h, j1, 2))
    for h in (0, 1):
        for j1 in (0, -1, 1, 2):
            for j2 in (0, -1, 1, 2):
                across(h, j1, j2).wait_recv()
    for copy in sent:
        copy.wait_send()
    own.wait()


def plane_gather(rows, collective_id, name):
    grouped = rows.reshape(rows.shape[0] // 8, 8, rows.shape[1])
    gathered = pl.pallas_call(
        plane_gather_kernel,
        out_shape=jax.ShapeDtypeStruct((32, *grouped.shape), rows.dtype),
        in_specs=[HBM],
        out_specs=HBM,
        scratch_shapes=[
            pltpu.SemaphoreType.DMA((2, 20)),
            pltpu.SemaphoreType.DMA((2, 20)),
            pltpu.SemaphoreType.DMA((32,)),
            pltpu.SemaphoreType.DMA((32,)),
            pltpu.SemaphoreType.DMA,
        ],
        compiler_params=pltpu.CompilerParams(
            collective_id=collective_id, has_side_effects=True, vmem_limit_bytes=62 * 2**20
        ),
        cost_estimate=pl.CostEstimate(
            flops=0, bytes_accessed=64 * rows.size * rows.dtype.itemsize, transcendentals=0
        ),
        name=name,
    )(grouped)
    return gathered.reshape(32 * rows.shape[0], rows.shape[1])


def line_peers():
    e, t = lax.axis_index("expert"), lax.axis_index("tensor")
    return [(e, lax.rem(t + k, 4)) for k in (1, 2, 3)]


class Line:
    def __init__(self, src, out, taken, ssem, rsem):
        t = lax.axis_index("tensor")
        self.src, self.out, self.taken, self.ssem, self.rsem = src, out, taken, ssem, rsem
        self.share, self.t = src.shape[0] // 4, t
        self.others = line_peers()

    def share_out(self, k):
        device = self.others[k - 1]
        return pltpu.make_async_remote_copy(
            src_ref=self.src.at[pl.ds(device[1] * self.share, self.share)],
            dst_ref=self.taken.at[k - 1],
            send_sem=self.ssem.at[0, k - 1],
            recv_sem=self.rsem.at[0, k - 1],
            device_id=device,
            device_id_type=MESH,
        )

    def pass_on(self, k):
        rows = pl.ds(self.t * self.share, self.share)
        return pltpu.make_async_remote_copy(
            src_ref=self.out.at[rows],
            dst_ref=self.out.at[rows],
            send_sem=self.ssem.at[1, k - 1],
            recv_sem=self.rsem.at[1, k - 1],
            device_id=self.others[k - 1],
            device_id_type=MESH,
        )

    def scatter(self):
        for k in (2, 1, 3):
            self.share_out(k).start()

    def add(self):
        for k in (2, 1, 3):
            self.share_out(k).wait_recv()

        def step(i, carry):
            total = self.src[self.t * self.share + i].astype(jnp.float32)
            for k in range(3):
                total = total + self.taken[k, i].astype(jnp.float32)
            self.out[self.t * self.share + i] = total.astype(self.out.dtype)
            return carry

        lax.fori_loop(0, self.share, step, 0)

    def gather(self):
        for k in (2, 1, 3):
            self.pass_on(k).start()

    def finish(self):
        for k in (2, 1, 3):
            self.pass_on(k).wait_recv()
        for k in (2, 1, 3):
            self.share_out(k).wait_send()
            self.pass_on(k).wait_send()


def line_sum_kernel(src, out, taken, ssem, rsem):
    line = Line(src, out, taken, ssem, rsem)
    greet(line.others)
    line.scatter()
    line.add()
    line.gather()
    line.finish()


PLANE_STEPS = 1 + 8 + 16 + 2 + 4 + 2


def plane_sum_steps(source, emit, scratch):
    mine, peer, one, two, last_one, last_two, lsem, pssem, prsem, ssem, rsem = scratch
    t, x, z, c = place()
    groups = mine.shape[2]
    half, quarter = groups // 2, groups // 4
    sibling = (at(x, z, 1 - c), t)
    along_x = [(at(wrap(x - 1), z, c), t), (at(wrap(x + 1), z, c), t)]
    along_z = [(at(x, wrap(z - 1), c), t), (at(x, wrap(z + 1), c), t)]
    order = (2, 1, 3, 0)
    sent = []

    def view(ref, h, a, b):
        if h == 0:
            return ref.at[a, b, pl.ds(0, half)]
        return ref.at[b, a, pl.ds(half, half)]

    def target(dx, dz, core):
        return at(wrap(x + dx), wrap(z + dz), core)

    def outward(dx, dz):
        return pltpu.make_async_remote_copy(
            src_ref=source.at[target(dx, dz, 1 - c)],
            dst_ref=peer.at[dx, dz],
            send_sem=pssem.at[dx, dz],
            recv_sem=prsem.at[dx, dz],
            device_id=sibling,
            device_id_type=MESH,
        )

    def inward(dx, dz):
        return pltpu.make_async_copy(
            source.at[target(dx, dz, c)], mine.at[dx, dz], lsem.at[dx, dz]
        )

    def hop(h, slot, src, dst, device):
        return pltpu.make_async_remote_copy(
            src_ref=src,
            dst_ref=dst,
            send_sem=ssem.at[h, slot],
            recv_sem=rsem.at[h, slot],
            device_id=device,
            device_id_type=MESH,
        )

    def ring(h, stage):
        return along_x if (h == 0) == (stage == 1) else along_z

    def first(h, b, side):
        return hop(
            h,
            4 * b + side,
            view(mine, h, 2, b).at[pl.ds(side * quarter, quarter)],
            one.at[h, b, side],
            ring(h, 1)[1 - side],
        )

    def second(h, b, side):
        return hop(
            h, 4 * b + 2 + side, view(mine, h, 1 + 2 * side, b), two.at[h, b, side], ring(h, 1)[1 - side]
        )

    def third(h, side):
        return hop(
            h,
            16 + side,
            view(mine, h, 0, 2).at[pl.ds(side * quarter, quarter)],
            last_one.at[h, side],
            ring(h, 2)[1 - side],
        )

    def fourth(h, side):
        return hop(
            h, 18 + side, view(mine, h, 0, 1 + 2 * side), last_two.at[h, side], ring(h, 2)[1 - side]
        )

    def go(copy):
        copy.start()
        sent.append(copy)

    def accumulate(into, sources_of, number):
        def step(i, carry):
            total = into[i].astype(jnp.float32)
            for source in sources_of:
                total = total + source[i].astype(jnp.float32)
            into[i] = total.astype(into.dtype)
            return carry

        lax.fori_loop(0, number, step, 0)

    spots = [(2, 2), (2, 1), (1, 2), (2, 3), (3, 2), (2, 0), (0, 2), (1, 1)]
    spots += [(1, 3), (3, 1), (3, 3), (1, 0), (0, 1), (3, 0), (0, 3), (0, 0)]
    for spot in spots:
        inward(*spot).start()
        go(outward(*spot))
    merged = set()

    yield

    def merge(h, a, b):
        spot = (a, b) if h == 0 else (b, a)
        if spot in merged:
            return
        merged.add(spot)
        inward(*spot).wait()
        outward(*spot).wait_recv()
        accumulate(mine.at[spot[0], spot[1]], [peer.at[spot[0], spot[1]]], groups)

    for b in order:
        for h in (0, 1):
            merge(h, 2, b)
            for side in (0, 1):
                go(first(h, b, side))
            yield
    for side in (0, 1):
        for b in order:
            for h in (0, 1):
                a = 1 + 2 * side
                merge(h, a, b)
                first(h, b, side).wait_recv()
                accumulate(
                    view(mine, h, a, b).at[pl.ds(side * quarter, quarter)],
                    [one.at[h, b, side]],
                    quarter,
                )
                go(second(h, b, side))
                yield

    def gathered_here(h, b):
        merge(h, 0, b)
        for side in (0, 1):
            second(h, b, side).wait_recv()
        accumulate(view(mine, h, 0, b), [two.at[h, b, 0], two.at[h, b, 1]], half)

    for h in (0, 1):
        gathered_here(h, 2)
        for side in (0, 1):
            go(third(h, side))
        yield
    for side in (0, 1):
        b = 1 + 2 * side
        for h in (0, 1):
            gathered_here(h, b)
            third(h, side).wait_recv()
            accumulate(
                view(mine, h, 0, b).at[pl.ds(side * quarter, quarter)],
                [last_one.at[h, side]],
                quarter,
            )
            go(fourth(h, side))
            yield
    for h in (0, 1):
        gathered_here(h, 0)
        for side in (0, 1):
            fourth(h, side).wait_recv()

        def finish(i, carry, h=h):
            total = mine[0, 0, h * half + i].astype(jnp.float32)
            for side in (0, 1):
                total = total + last_two[h, side, i].astype(jnp.float32)
            emit(h * half + i, total)
            return carry

        lax.fori_loop(0, half, finish, 0)
        yield
    for copy in sent:
        copy.wait_send()


def plane_peers():
    t, x, z, c = place()
    return [
        (at(x, z, 1 - c), t),
        (at(wrap(x - 1), z, c), t),
        (at(wrap(x + 1), z, c), t),
        (at(x, wrap(z - 1), c), t),
        (at(x, wrap(z + 1), c), t),
    ]


def plane_scratch(groups, width):
    half, quarter = groups // 2, groups // 4
    low = jnp.bfloat16
    return [
        pltpu.VMEM((4, 4, groups, 8, width), low),
        pltpu.VMEM((4, 4, groups, 8, width), low),
        pltpu.VMEM((2, 4, 2, quarter, 8, width), low),
        pltpu.VMEM((2, 4, 2, half, 8, width), low),
        pltpu.VMEM((2, 2, quarter, 8, width), low),
        pltpu.VMEM((2, 2, half, 8, width), low),
        pltpu.SemaphoreType.DMA((4, 4)),
        pltpu.SemaphoreType.DMA((4, 4)),
        pltpu.SemaphoreType.DMA((4, 4)),
        pltpu.SemaphoreType.DMA((2, 20)),
        pltpu.SemaphoreType.DMA((2, 20)),
    ]


def line_scratch(groups, width):
    return [
        pltpu.VMEM((3, groups // 4, 8, width), jnp.bfloat16),
        pltpu.SemaphoreType.DMA((2, 3)),
        pltpu.SemaphoreType.DMA((2, 3)),
    ]


def advance(task, number):
    for _ in range(number):
        next(task, None)


def by_expert(part, groups):
    return part.reshape(32, groups, 8, part.shape[1])


def by_group(part):
    return part.reshape(part.shape[0] // 8, 8, part.shape[1])


def communicate(kernel, collective_id, name, operands, where, out_shapes, scratch, moved):
    vmem = pl.BlockSpec(memory_space=pltpu.VMEM)
    shapes = [jax.ShapeDtypeStruct(shape, dtype) for shape, dtype in out_shapes]
    return pl.pallas_call(
        kernel,
        out_shape=shapes,
        in_specs=[vmem if inside else HBM for inside in where],
        out_specs=[vmem] * len(shapes),
        scratch_shapes=scratch,
        compiler_params=pltpu.CompilerParams(
            collective_id=collective_id, has_side_effects=True, vmem_limit_bytes=60 * 2**20
        ),
        cost_estimate=pl.CostEstimate(flops=0, bytes_accessed=moved, transcendentals=0),
        name=name,
    )(*operands)


def sum_tokens_kernel(source, shared, out, held, taken, line_ssem, line_rsem, *scratch):
    half = out.shape[0] // 2

    def emit(i, total):
        held[i] = (total + shared[i]).astype(held.dtype)

    greet(plane_peers() + line_peers())
    plane = plane_sum_steps(source, emit, scratch)
    lines = []
    for h in (0, 1):
        rows = pl.ds(h * half, half)
        lines.append(
            Line(held.at[rows], out.at[rows], taken.at[h], line_ssem.at[h], line_rsem.at[h])
        )
    advance(plane, PLANE_STEPS - 1)
    lines[0].scatter()
    advance(plane, 1)
    lines[1].scatter()
    for line in lines:
        line.add()
        line.gather()
    for line in lines:
        line.finish()
    advance(plane, 1)


def sum_tokens(part, shared, collective_id):
    groups, width = part.shape[0] // 256, part.shape[1]
    (summed,) = communicate(
        sum_tokens_kernel,
        collective_id,
        "sum_tokens",
        (by_expert(part, groups), by_group(shared)),
        (False, True),
        (((groups, 8, width), jnp.bfloat16),),
        [
            pltpu.VMEM((groups, 8, width), jnp.bfloat16),
            pltpu.VMEM((2, 3, groups // 8, 8, width), jnp.bfloat16),
            pltpu.SemaphoreType.DMA((2, 2, 3)),
            pltpu.SemaphoreType.DMA((2, 2, 3)),
        ]
        + plane_scratch(groups, width),
        16 * part.size,
    )
    return summed.reshape(8 * groups, width)


def reach_back_peers():
    t, x, z, c = place()
    along = [(at(x, wrap(z - r), c), t) for r in (1, 2, 3)]
    return [(at(x, z, 1 - c), t), (at(wrap(x - 1), z, c), t)] + along


def reach_back_run(src, out, lsem, ssem, rsem, pssem, prsem):
    t, x, z, c = place()
    sibling = (at(x, z, 1 - c), t)
    own = pltpu.make_async_copy(src, out.at[8], lsem)
    own.start()

    def onward():
        return pltpu.make_async_remote_copy(
            src_ref=src,
            dst_ref=out.at[0],
            send_sem=ssem.at[3],
            recv_sem=rsem.at[3],
            device_id=(at(wrap(x + 1), z, c), t),
            device_id_type=MESH,
        )

    def along(r, source):
        return pltpu.make_async_remote_copy(
            src_ref=source,
            dst_ref=out.at[8 - 2 * r],
            send_sem=ssem.at[r - 1],
            recv_sem=rsem.at[r - 1],
            device_id=(at(x, wrap(z + r), c), t),
            device_id_type=MESH,
        )

    def near(i):
        return pltpu.make_async_remote_copy(
            src_ref=out.at[8 - 2 * (i + c)],
            dst_ref=out.at[7 - 2 * i],
            send_sem=pssem.at[i],
            recv_sem=prsem.at[i],
            device_id=sibling,
            device_id_type=MESH,
        )

    onward().start()
    for r in (2, 1, 3):

        @pl.when(z + r < 4)
        def _(r=r):
            along(r, src).start()

    own.wait()
    onward().wait_recv()
    for r in (2, 3, 1):

        @pl.when(z + r >= 4)
        def _(r=r):
            along(r, out.at[0]).start()

    for r in (1, 3, 2):
        along(r, src).wait_recv()
    for i in range(4):
        near(i).start()
    for i in range(4):
        near(i).wait()
    onward().wait_send()
    for r in (1, 2, 3):
        along(r, src).wait_send()


def chip_at(x, z, c, distance):
    place_on = lax.rem(x * 4 + z + 16 + distance, 16)
    return place_on * 2 + c


def send_back_steps(src, out, held, near_in, far_in, ssem, rsem, pssem, prsem):
    t, x, z, c = place()
    groups = out.shape[0]
    sibling = (at(x, z, 1 - c), t)
    behind = [(chip_at(x, z, c, -k), t) for k in (1, 2, 3, 4)]

    def near(i):
        return pltpu.make_async_remote_copy(
            src_ref=src.at[7 - 2 * i],
            dst_ref=near_in.at[i],
            send_sem=pssem.at[i],
            recv_sem=prsem.at[i],
            device_id=sibling,
            device_id_type=MESH,
        )

    def far(k):
        return pltpu.make_async_remote_copy(
            src_ref=held.at[k],
            dst_ref=far_in.at[k - 1],
            send_sem=ssem.at[k - 1],
            recv_sem=rsem.at[k - 1],
            device_id=behind[k - 1],
            device_id_type=MESH,
        )

    for i in (3, 2, 1, 0):
        near(i).start()
    yield
    for i in (3, 2, 1, 0):
        near(i).wait_recv()
    for k in (4, 3, 2, 1, 0):

        def step(i, carry, k=k):
            total = src[8 - 2 * k, i].astype(jnp.float32)
            other = near_in[jnp.clip(k - c, 0, 3), i].astype(jnp.float32)
            covered = jnp.logical_and(k - c >= 0, k - c <= 3)
            total = total + jnp.where(covered, other, jnp.zeros_like(other))
            held[k, i] = total.astype(held.dtype)
            return carry

        lax.fori_loop(0, groups, step, 0)
        if k > 0:
            far(k).start()
    yield
    for k in (1, 2, 3, 4):
        far(k).wait_recv()

    def last(i, carry):
        total = held[0, i].astype(jnp.float32)
        for k in range(4):
            total = total + far_in[k, i].astype(jnp.float32)
        out[i] = total.astype(out.dtype)
        return carry

    lax.fori_loop(0, groups, last, 0)
    yield
    for k in (1, 2, 3, 4):
        far(k).wait_send()
    for i in range(4):
        near(i).wait_send()


def contract(left_side, right_side, left_dim, right_dim):
    return lax.dot_general(
        left_side,
        right_side,
        (((left_dim,), (right_dim,)), ((), ())),
        preferred_element_type=jnp.float32,
    )


def experts_kernel(
    token_rows,
    grad_rows,
    gate_in,
    up_in,
    down_in,
    routed_out,
    back_out,
    gate_out,
    up_out,
    down_out,
    ranks,
    rows_x,
    rows_g,
    weights,
    dots,
    staged,
    gate_up,
    down,
    hidden,
    grads,
    sums_one,
    sums_two,
    in_sem,
    out_sem,
):
    step = pl.program_id(0)
    low = jnp.bfloat16
    units = down_in.shape[1]
    wide = down.shape[0]
    pair_slots = 48
    width = rows_x.shape[2]
    blocks = ranks.shape[0]
    count = rows_x.shape[1]
    part = 256

    def load(k, expert):
        source = (gate_in, up_in, down_in)[k].at[expert]
        return pltpu.make_async_copy(source, staged.at[k], in_sem.at[k])

    def store(k, expert):
        if k == 2:
            source = sums_two.at[pl.ds(0, units)]
        else:
            source = sums_one.at[pl.ds(k * wide, units)]
        target = (gate_out, up_out, down_out)[k].at[expert]
        return pltpu.make_async_copy(source, target, out_sem.at[k])

    def picks(block):
        row = lax.broadcasted_iota(jnp.int32, (pair_slots, 256), 0)
        column = lax.broadcasted_iota(jnp.int32, (pair_slots, 256), 1)
        second = row >= 24
        slot = jnp.where(second, row - 24, row).astype(jnp.float32)
        inside = second == (column >= 128)
        found = []
        for expert in (0, 1):
            rank = ranks[block, expert : expert + 1, :]
            found.append(jnp.logical_and(rank == slot, inside))
        return found

    @pl.when(step == 0)
    def _():
        for k in range(3):
            load(k, 0).start()

    def rank_slots(block):
        square = (128, 128)
        same = lax.broadcasted_iota(jnp.int32, square, 0) == lax.broadcasted_iota(
            jnp.int32, square, 1
        )
        turned = contract(
            jnp.where(same, 1.0, 0.0).astype(low), token_rows[0, :, width:], 1, 1
        )
        first = lax.broadcasted_iota(jnp.int32, (256, 256), 0)
        second = lax.broadcasted_iota(jnp.int32, (256, 256), 1)
        ahead = jnp.logical_and(first < second, (first >= 128) == (second >= 128))
        line = lax.broadcasted_iota(jnp.int32, (8, 256), 0)
        named = jnp.zeros((8, 256), jnp.float32)
        shares = jnp.zeros((8, 256), jnp.float32)
        for expert in (0, 1):
            number = (lax.axis_index("expert") * 2 + expert).astype(jnp.float32)
            match = turned[0:8] == number
            present = jnp.sum(jnp.where(match, 1.0, 0.0), 0, keepdims=True)
            share = jnp.sum(jnp.where(match, turned[8:16] + turned[16:24], 0.0), 0, keepdims=True)
            named = named + jnp.where(line == expert, present, 0.0)
            shares = shares + jnp.where(line == 2 + expert, share, 0.0)
        rank = contract(named.astype(low), jnp.where(ahead, 1.0, 0.0).astype(low), 1, 0)
        rank = jnp.where(named > 0.0, rank, -1.0)
        ranks[block] = jnp.where(line < 2, rank, shares)

    @pl.when(step < blocks)
    def _():
        rank_slots(step)
        found = picks(step)
        pick = jnp.concatenate([jnp.where(f, 1.0, 0.0) for f in found], 0).astype(low)
        from_x = contract(pick, token_rows[0, :, :width], 1, 0).astype(low)
        from_g = contract(pick, grad_rows[0], 1, 0).astype(low)
        here = pl.ds(pl.multiple_of(step * pair_slots, pair_slots), pair_slots)
        for expert in (0, 1):
            lines = slice(expert * pair_slots, (expert + 1) * pair_slots)
            rows_x[expert, here, :] = from_x[lines]
            rows_g[expert, here, :] = from_g[lines]
            shares = ranks[step, 2 + expert : 3 + expert, :]
            weight = jnp.sum(jnp.where(found[expert], shares, 0.0), 1, keepdims=True)
            weights[expert, here, :] = jnp.broadcast_to(weight, (pair_slots, 128))

    for expert in (0, 1):

        @pl.when(step == blocks + expert)
        def _(expert=expert):
            for k in range(3):
                load(k, expert).wait()
            nothing = jnp.zeros((wide - units, width), low)
            gate_up[pl.ds(units, wide - units), :] = nothing
            gate_up[pl.ds(wide + units, wide - units), :] = nothing
            down[pl.ds(units, wide - units), :] = nothing

            def cast(i, carry):
                rows = pl.ds(pl.multiple_of(i * 32, 32), 32)
                gate_up[rows, :] = staged[0, rows, :].astype(low)
                gate_up[pl.ds(pl.multiple_of(wide + i * 32, 32), 32), :] = staged[
                    1, rows, :
                ].astype(low)
                down[rows, :] = staged[2, rows, :].astype(low)
                return carry

            lax.fori_loop(0, units // 32, cast, 0)
            if expert == 0:
                for k in range(3):
                    load(k, 1).start()

            def middle(i, carry):
                rows = pl.ds(pl.multiple_of(i * part, part), part)
                before = contract(rows_x[expert, rows, :], gate_up[...], 1, 1)
                plain = contract(rows_g[expert, rows, :], down[...], 1, 1)
                weight = weights[expert, rows, :][:, 0:1]
                gate, up = before[:, :wide], before[:, wide:]
                sigmoid = 1.0 / (1.0 + jnp.exp(-gate))
                on = gate * sigmoid
                value = on * up
                hidden[rows, :] = (weight * value).astype(low)
                dot = jnp.sum(plain * value, 1, keepdims=True)
                mine = 64 + lax.axis_index("expert") * 2 + expert
                lane = lax.broadcasted_iota(jnp.int32, (part, 128), 1)
                dots[expert, rows, :] = jnp.where(lane == mine, dot, 0.0).astype(low)
                change = weight * plain
                grads[rows, :wide] = (change * up * (sigmoid * (1.0 + gate * (1.0 - sigmoid)))).astype(
                    low
                )
                grads[rows, wide:] = (change * on).astype(low)
                return carry

            lax.fori_loop(0, count // part, middle, 0)
            if expert == 1:
                for k in range(3):
                    store(k, 0).wait()

            def weight_grads(i, carry):
                columns = pl.ds(pl.multiple_of(i * part, part), part)
                sums_one[columns, :] = contract(grads[:, columns], rows_x[expert], 0, 0)
                return carry

            lax.fori_loop(0, 2 * wide // part, weight_grads, 0)
            for i in range(wide // 128):
                columns = pl.ds(i * 128, 128)
                sums_two[columns, :] = contract(hidden[:, columns], rows_g[expert], 0, 0)
            for k in range(3):
                store(k, expert).start()

            def results(i, carry):
                rows = pl.ds(pl.multiple_of(i * part, part), part)
                rows_x[expert, rows, :] = contract(hidden[rows, :], down[...], 1, 0).astype(low)
                rows_g[expert, rows, :] = contract(grads[rows, :], gate_up[...], 1, 0).astype(low)
                return carry

            lax.fori_loop(0, count // part, results, 0)

    @pl.when(step >= blocks + 2)
    def _():
        block = step - blocks - 2
        pick = jnp.concatenate([jnp.where(f, 1.0, 0.0) for f in picks(block)], 0).astype(low)
        here = pl.ds(pl.multiple_of(block * pair_slots, pair_slots), pair_slots)

        def both(ref):
            return jnp.concatenate([ref[0, here, :], ref[1, here, :]], 0)

        routed_out[0] = contract(pick, both(rows_x), 0, 0).astype(low)
        back_out[0, :, :width] = contract(pick, both(rows_g), 0, 0).astype(low)
        back_out[0, :, width:] = contract(pick, both(dots), 0, 0).astype(low)

    @pl.when(step == 2 * blocks + 1)
    def _():
        for k in range(3):
            store(k, 1).wait()


def experts(token_rows, grad_rows, gate, up, down):
    low = jnp.bfloat16
    blocks = token_rows.shape[0]
    local, units, width = down.shape
    wide = (units + 127) // 128 * 128
    count = blocks * 48
    last = blocks - 1

    def entering(i):
        return (jnp.minimum(i, last), 0, 0)

    def leaving(i):
        return (jnp.maximum(i - blocks - 2, 0), 0, 0)

    weight = jax.ShapeDtypeStruct((local, units, width), jnp.float32)
    return pl.pallas_call(
        experts_kernel,
        grid=(2 * blocks + 2,),
        out_shape=(
            jax.ShapeDtypeStruct((blocks, 256, width), low),
            jax.ShapeDtypeStruct((blocks, 256, width + 128), low),
            weight,
            weight,
            weight,
        ),
        in_specs=[
            pl.BlockSpec((1, 256, width + 128), entering),
            pl.BlockSpec((1, 256, width), entering),
            HBM,
            HBM,
            HBM,
        ],
        out_specs=(
            pl.BlockSpec((1, 256, width), leaving),
            pl.BlockSpec((1, 256, width + 128), leaving),
            HBM,
            HBM,
            HBM,
        ),
        scratch_shapes=[
            pltpu.VMEM((blocks, 8, 256), jnp.float32),
            pltpu.VMEM((local, count, width), low),
            pltpu.VMEM((local, count, width), low),
            pltpu.VMEM((local, count, 128), jnp.float32),
            pltpu.VMEM((local, count, 128), low),
            pltpu.VMEM((3, units, width), jnp.float32),
            pltpu.VMEM((2 * wide, width), low),
            pltpu.VMEM((wide, width), low),
            pltpu.VMEM((count, wide), low),
            pltpu.VMEM((count, 2 * wide), low),
            pltpu.VMEM((2 * wide, width), jnp.float32),
            pltpu.VMEM((wide, width), jnp.float32),
            pltpu.SemaphoreType.DMA((3,)),
            pltpu.SemaphoreType.DMA((3,)),
        ],
        compiler_params=pltpu.CompilerParams(
            dimension_semantics=("arbitrary",), vmem_limit_bytes=60 * 2**20
        ),
        cost_estimate=pl.CostEstimate(
            flops=18 * local * count * wide * width,
            bytes_accessed=100 * 2**20,
            transcendentals=local * count * wide,
        ),
        name="experts",
    )(token_rows, grad_rows, gate, up, down)


def rms_forward(values, gains):
    inverse = lax.rsqrt(jnp.mean(values * values, -1, keepdims=True) + epsilon)
    return (values * inverse * gains, inverse)


HEADS = 4
SCALE = (NOPE + ROPE) ** (-0.5)


def column(row):
    shape = (128, 128)
    same = lax.broadcasted_iota(jnp.int32, shape, 0) == lanes(shape)
    return jnp.sum(jnp.where(same, row.astype(jnp.float32), 0.0), 1, keepdims=True)


def in_groups(values):
    return values.reshape(values.shape[0] // 8, 8, values.shape[1])


def lanes(shape):
    return lax.broadcasted_iota(jnp.int32, shape, 1)


def turn_tables(cosine, sine_tab):
    lane = lanes(cosine.shape)
    kept = jnp.where(lane < 64, cosine, 0.0)
    crossed = jnp.where(lane < 32, -sine_tab, jnp.where(lane < 64, sine_tab, 0.0))
    return kept, crossed


def exchange_halves(values):
    shape = (128, 128)
    to = lanes(shape)
    from_lane = lax.broadcasted_iota(jnp.int32, shape, 0)
    other = jnp.where(to < 32, to + 32, jnp.where(to < 64, to - 32, to))
    swap = jnp.where(from_lane == other, 1.0, 0.0)
    return lax.dot_general(
        values,
        swap,
        (((1,), (0,)), ((), ())),
        precision=lax.Precision.HIGHEST,
        preferred_element_type=jnp.float32,
    )


def fold_matrix():
    shape = (128, 256)
    to = lanes(shape)
    wanted = jnp.where(to >= 128, 32, 0) + lax.rem(to, 32)
    return jnp.where(lax.broadcasted_iota(jnp.int32, shape, 0) == wanted, 1.0, 0.0).astype(
        jnp.bfloat16
    )


def head_lanes(values, head):
    lane = lanes(values.shape)
    inside = jnp.logical_and(lane >= 32 * head, lane < 32 * head + 32)
    return jnp.where(inside, values, jnp.zeros_like(values))


def pack_kernel(
    query,
    latent,
    gain_one,
    gain_two,
    gain_latent,
    output,
    expand,
    gate,
    router,
    up,
    down,
    attention_out,
    ffn_out,
):
    low = jnp.bfloat16
    shard = query.shape[0]
    for head in range(HEADS):
        start = 192 * head
        attention_out[:, 128 * head : 128 * head + 128] = query[:, start : start + 128].astype(low)
    for half in (0, 1):
        starts = [192 * head + 128 + 32 * half for head in range(HEADS)]
        pieces = [query[:, start : start + 32] for start in starts]
        to = 512 + 128 * half
        attention_out[:, to : to + 128] = jnp.concatenate(pieces, 1).astype(low)
    attention_out[:, 768:1280] = latent[:, :RANK].astype(low)
    row = lax.broadcasted_iota(jnp.int32, (shard, shard), 0)
    gains = jnp.where(row == 0, gain_one[...], 0.0)
    gains = jnp.where(row == 1, gain_two[...], gains)
    rest = jnp.zeros((1, shard - gain_latent.shape[1]), jnp.float32)
    gains = jnp.where(row == 2, jnp.concatenate([gain_latent[...], rest], 1), gains)
    attention_out[:, 1280:1408] = jnp.concatenate([latent[:, RANK:], gains], 1).astype(low)
    attention_out[:, 1408:1920] = output[...].astype(low)
    for j in range(4):
        attention_out[16 * j : 16 * j + 16, 1920:] = expand[:, 256 * j : 256 * j + 256].astype(low)
    gap = jnp.zeros((shard, 64), jnp.float32)
    for k, (wide, narrow) in enumerate(((gate, router[...]), (up, gap), (down, gap))):
        start = 768 * k
        ffn_out[:, start : start + 640] = wide[:, :640].astype(low)
        ffn_out[:, start + 640 : start + 768] = jnp.concatenate(
            [wide[:, 640:704], narrow], 1
        ).astype(low)


def project_kernel(
    hidden,
    weights,
    segments,
    frequencies,
    normed_out,
    query_out,
    latent_out,
    keys_out,
    cosine_out,
    sine_out,
    gain_one_out,
    gain_two_out,
    gain_latent_out,
    key_row,
    landed,
    *scratch,
):
    low = jnp.bfloat16
    peers = reach_back_peers()
    call(peers)
    own_index = lax.axis_index("expert")
    rows = hidden.shape[0]
    own = column(segments[pl.ds(own_index, 1), :])
    before = jnp.zeros((rows, 128), jnp.float32)
    for i in range(segments.shape[0]):
        before += jnp.where(segments[i : i + 1, :].astype(jnp.float32) < own, 1.0, 0.0)
    start = jnp.sum(before, 1, keepdims=True)
    index = (lax.broadcasted_iota(jnp.int32, (rows, 1), 0) + own_index * rows).astype(jnp.float32)
    angles = (index - start) * frequencies[...]
    cos, sin = jnp.cos(angles), jnp.sin(angles)
    cosine_out[...] = cos
    sine_out[...] = sin
    gains = [
        weights[64 * e : 64 * e + 16, 1280:1408].astype(jnp.float32) for e in range(32)
    ]
    gain_one_out[...] = jnp.concatenate([block[0:1, 64:128] for block in gains], 1)
    gain_two_out[...] = jnp.concatenate([block[1:2, 64:128] for block in gains], 1)
    gain_latent_out[...] = jnp.concatenate([block[2:3, 64:80] for block in gains], 1)
    normed = rms_forward(hidden[...].astype(jnp.float32), gain_one_out[...])[0].astype(low)
    normed_out[...] = normed
    query = contract(normed, weights[:, :768], 1, 0)
    first, second = query[:, 512:640], query[:, 640:768]
    query_out[:, :512] = query[:, :512].astype(low)
    query_out[:, 512:640] = (first * cos - second * sin).astype(low)
    query_out[:, 640:768] = (second * cos + first * sin).astype(low)
    latent = contract(normed, weights[:, 768:1408], 1, 0)
    latent_out[...] = latent[:, :RANK]
    compressed = rms_forward(latent[:, :RANK], gain_latent_out[...])[0]
    key_row[:, :, :RANK] = in_groups(compressed).astype(low)
    rope = latent[:, RANK:]
    kept, crossed = turn_tables(cos, sin)
    turned = rope * kept + exchange_halves(rope) * crossed
    key_row[:, :, RANK:] = in_groups(turned).astype(low)
    hear(peers)
    reach_back_run(key_row, landed, *scratch)
    keys_out[...] = landed[...]


def attend_kernel(
    keys,
    expand_0,
    expand_1,
    query,
    segments,
    wo_0,
    wo_1,
    wo_2,
    wo_3,
    out,
    attended,
    probs,
    expanded,
    key_rope,
    expand,
    held,
    landed,
    *scratch,
):
    low = jnp.bfloat16
    peers = line_peers()
    call(peers)
    rows = query.shape[0]
    count = keys.shape[0]
    fold = fold_matrix()
    for k, block in enumerate((expand_0, expand_1)):
        for j in range(4):
            part = block[...].reshape(32, 64, 128)[:, 16 * j : 16 * j + 16, :]
            expand[:, 256 * j + 128 * k : 256 * j + 128 * k + 128] = part.reshape(RANK, 128)
    own_index = lax.axis_index("expert")
    own_segment = column(segments[pl.ds(own_index, 1), :])
    key_segments = []
    for j in range(9):
        where = own_index - 8 + j
        row = segments[pl.ds(jnp.maximum(where, 0), 1), :].astype(jnp.float32)
        key_segments.append(jnp.where(where >= 0, row, -1.0))
    key_segment = jnp.concatenate(key_segments, 1)

    def expand_rows(i, carry):
        part = pl.ds(pl.multiple_of(i * rows, rows), rows)
        expanded[part, :] = contract(keys[part, :RANK], expand[...], 1, 0).astype(low)
        key_rope[part, :] = contract(keys[part, RANK:], fold, 1, 0).astype(low)
        return carry

    lax.fori_loop(0, count // rows, expand_rows, 0)
    shape = (rows, count)
    distance = lax.broadcasted_iota(jnp.int32, shape, 0) + WINDOW - lanes(shape)
    allowed = jnp.logical_and(distance >= 0, distance < WINDOW)
    allowed = jnp.logical_and(allowed, own_segment == key_segment)
    total = jnp.zeros((rows, wo_0.shape[0]), jnp.float32)
    for head, wo in enumerate((wo_0, wo_1, wo_2, wo_3)):
        start = 256 * head
        scores = contract(query[:, 128 * head : 128 * head + 128], expanded[:, start : start + 128], 1, 1)
        scores += contract(head_lanes(query[:, 512:640], head), key_rope[:, :128], 1, 1)
        scores += contract(head_lanes(query[:, 640:768], head), key_rope[:, 128:], 1, 1)
        scores = jnp.where(allowed, scores * SCALE, masked_score)
        exponent = jnp.exp(scores - jnp.max(scores, 1, keepdims=True))
        share = exponent / jnp.sum(exponent, 1, keepdims=True)
        probs[head] = share
        mixed = contract(share.astype(low), expanded[:, start + 128 : start + 256], 1, 0).astype(low)
        attended[:, 128 * head : 128 * head + 128] = mixed
        total += contract(mixed, wo[...], 1, 1)
    held[...] = in_groups(total).astype(low)
    hear(peers)
    line = Line(held, landed, *scratch)
    line.scatter()
    line.add()
    line.gather()
    line.finish()
    out[...] = landed[...]


def route_kernel(hidden, attention, gain, router, routes, token_out, middle_out, gates_out):
    low = jnp.bfloat16
    middle = hidden[...].astype(jnp.float32) + attention[...].astype(jnp.float32)
    middle_out[...] = middle
    normed = rms_forward(middle, gain[...])[0].astype(low)
    width = normed.shape[1]
    token_out[:, :width] = normed
    logits = contract(normed, router[...], 1, 0)
    lane = lanes(logits.shape).astype(jnp.float32)
    named = [column(routes[r : r + 1, :]) for r in range(6)]
    chosen = [
        jnp.sum(jnp.where(lane == number + 64, logits, 0.0), 1, keepdims=True) for number in named
    ]
    most = functools.reduce(jnp.maximum, chosen)
    exponents = [jnp.exp(value - most) for value in chosen]
    total = functools.reduce(jnp.add, exponents)
    extra = jnp.where(jnp.logical_or(lane == 6, lane == 7), 128.0, 0.0)
    gates = jnp.zeros(logits.shape, jnp.float32)
    for r in range(6):
        weight = exponents[r] / total
        high = weight.astype(low).astype(jnp.float32)
        extra += jnp.where(lane == r, named[r], 0.0)
        extra += jnp.where(lane == 8 + r, high, 0.0)
        extra += jnp.where(lane == 16 + r, weight - high, 0.0)
        gates += jnp.where(lane == r, weight, 0.0)
    token_out[:, width:] = extra.astype(low)
    gates_out[...] = gates


def shared_kernel(normed, cotangent, weights, part_out, back_out, grads_out):
    low = jnp.bfloat16
    gate = contract(normed[...], weights[:, :768], 1, 0)
    up = contract(normed[...], weights[:, 768:1536], 1, 0)
    sigmoid = 1.0 / (1.0 + jnp.exp(-gate))
    on = gate * sigmoid
    hidden = (on * up).astype(low)
    part_out[...] = contract(hidden, weights[:, 1536:], 1, 1)
    change = contract(cotangent[...], weights[:, 1536:], 1, 0)
    grad_gate = (change * up * (sigmoid * (1.0 + gate * (1.0 - sigmoid)))).astype(low)
    grad_up = (change * on).astype(low)
    width = normed.shape[1]
    back_out[:, :width] = contract(grad_gate, weights[:, :768], 1, 1) + contract(
        grad_up, weights[:, 768:1536], 1, 1
    )
    back_out[:, width:] = jnp.zeros((normed.shape[0], 128), jnp.float32)

    def grads(i, carry):
        part = pl.ds(pl.multiple_of(i * 256, 256), 256)
        rows = normed[:, part]
        grads_out[part, :768] = contract(rows, grad_gate, 0, 0).astype(low)
        grads_out[part, 768:1536] = contract(rows, grad_up, 0, 0).astype(low)
        grads_out[part, 1536:] = contract(cotangent[:, part], hidden, 0, 0).astype(low)
        return carry

    lax.fori_loop(0, grads_out.shape[0] // 256, grads, 0)


def attend_back_kernel(
    back,
    middle,
    gain,
    gates,
    routes,
    router,
    cotangent,
    wo_0,
    wo_1,
    wo_2,
    wo_3,
    probs,
    expanded,
    key_rope,
    query,
    keys,
    expand,
    query_w,
    cosine,
    sine_tab,
    normed,
    attended,
    middle_out,
    attention_out,
    gain_out,
    logits_out,
    own_out,
    query_sum_out,
    latent_sum_out,
    changes,
    ropes,
    query_out,
    back_out,
    keys_out,
    grads_out,
    held,
    near_in,
    far_in,
    ssem,
    rsem,
    pssem,
    prsem,
    latent,
    landed_one,
    landed_two,
    *scratch,
):
    low = jnp.bfloat16
    t, x, z, c = place()
    peers = plane_peers() + line_peers() + [(chip_at(x, z, c, k), t) for k in (1, 2, 3, 4)]
    call(peers)
    width = middle.shape[1]
    rows = middle.shape[0]
    lane = lanes((rows, 128)).astype(jnp.float32)
    sums = back[:, width:].astype(jnp.float32)
    named = [column(routes[r : r + 1, :]) for r in range(6)]
    weight = [gates[:, r : r + 1] for r in range(6)]
    change = [
        jnp.sum(jnp.where(lane == number + 64, sums, 0.0), 1, keepdims=True) for number in named
    ]
    inner = functools.reduce(jnp.add, [w * c for w, c in zip(weight, change)])
    logits = jnp.zeros((rows, 128), jnp.float32)
    for r in range(6):
        logits += jnp.where(lane == named[r] + 64, weight[r] * (change[r] - inner), 0.0)
    logits_low = logits.astype(low)
    logits_out[...] = logits_low
    grad_normed = back[:, :width].astype(jnp.float32) + contract(logits_low, router[...], 1, 1)
    values = middle[...]
    inverse = lax.rsqrt(jnp.mean(values * values, 1, keepdims=True) + epsilon)
    weighted = grad_normed * gain[...]
    aligned = jnp.mean(values * weighted, 1, keepdims=True)
    gain_out[...] = jnp.sum(grad_normed * values * inverse, 0, keepdims=True)
    grad_middle = (
        cotangent[...].astype(jnp.float32)
        + inverse * weighted
        - values * (inverse * inverse * inverse) * aligned
    )
    middle_out[...] = grad_middle
    grad_attn = grad_middle.astype(low)
    attention_out[...] = grad_attn
    first = jnp.zeros((rows, 128), jnp.float32)
    second = jnp.zeros((rows, 128), jnp.float32)
    for head, wo in enumerate((wo_0, wo_1, wo_2, wo_3)):
        start = 256 * head
        nope, value = slice(start, start + 128), slice(start + 128, start + 256)
        own = slice(128 * head, 128 * head + 128)
        grad_mixed = contract(grad_attn, wo[...], 1, 0).astype(low)
        share = probs[head]
        changes[:, value] = contract(share.astype(low), grad_mixed, 0, 0).astype(low)
        grad_share = contract(grad_mixed, expanded[:, value], 1, 1)
        grad_scores = share * (grad_share - jnp.sum(share * grad_share, 1, keepdims=True))
        grad_scores = grad_scores.astype(low)
        query_out[:, own] = (contract(grad_scores, expanded[:, nope], 1, 0) * SCALE).astype(low)
        both = contract(grad_scores, key_rope[...], 1, 0) * SCALE
        first += head_lanes(both[:, :128], head)
        second += head_lanes(both[:, 128:], head)
        changes[:, nope] = (contract(grad_scores, query[:, own], 0, 0) * SCALE).astype(low)
        from_first = contract(grad_scores, head_lanes(query[:, 512:640], head), 0, 0) * SCALE
        from_second = contract(grad_scores, head_lanes(query[:, 640:768], head), 0, 0) * SCALE
        if head == 0:
            ropes[:, :128] = from_first
            ropes[:, 128:] = from_second
        else:
            ropes[:, :128] += from_first
            ropes[:, 128:] += from_second
    cos, sin = cosine[...], sine_tab[...]
    query_out[:, 512:640] = (first * cos + second * sin).astype(low)
    query_out[:, 640:768] = (second * cos - first * sin).astype(low)
    for j in range(4):
        grad_expand = contract(keys[:, :RANK], changes[:, 256 * j : 256 * j + 256], 0, 0)
        grads_out[:, 2 * j : 2 * j + 2, :, 1280:] = grad_expand.reshape(32, 2, 8, 256).astype(low)

    def grads(i, carry):
        part = pl.ds(pl.multiple_of(i * 256, 256), 256)
        some = pl.ds(i * 4, 4)
        of_query = contract(normed[:, part], query_out[...], 0, 0)
        grads_out[some, :, :, :768] = of_query.reshape(4, 8, 8, 768).astype(low)
        of_output = contract(attention_out[:, part], attended[...], 0, 0)
        grads_out[some, :, :, 768:1280] = of_output.reshape(4, 8, 8, 512).astype(low)
        return carry

    lax.fori_loop(0, width // 256, grads, 0)

    def emit(i, total):
        own_out[i] = total

    hear(peers)
    plane = plane_sum_steps(grads_out, emit, scratch[6:])
    advance(plane, 1)
    fold = fold_matrix()

    def key_rows(i, carry):
        part = pl.ds(pl.multiple_of(i * rows, rows), rows)
        compressed = contract(changes[part, :], expand[...], 1, 1)
        keys_out[i, :, :, :RANK] = in_groups(compressed).astype(low)
        rope = contract(ropes[part, :].astype(low), fold, 1, 1)
        keys_out[i, :, :, RANK:] = in_groups(rope).astype(low)
        return carry

    lax.fori_loop(0, keys.shape[0] // rows, key_rows, 0)
    back = send_back_steps(keys_out, latent, held, near_in, far_in, ssem, rsem, pssem, prsem)
    advance(back, 1)
    advance(plane, 2)
    back_out[...] = in_groups(contract(query_out[...], query_w[...], 1, 1)).astype(low)
    line_one = Line(back_out, landed_one, *scratch[:3])
    line_two = Line(latent, landed_two, *scratch[3:6])
    line_one.scatter()
    advance(back, 1)
    advance(plane, 6)
    line_one.add()
    line_one.gather()
    advance(plane, 4)
    advance(back, 1)
    line_two.scatter()
    advance(plane, 8)
    line_two.add()
    line_two.gather()
    advance(plane, PLANE_STEPS - 21)
    line_one.finish()
    query_sum_out[...] = landed_one[...]
    line_two.finish()
    latent_sum_out[...] = landed_two[...]
    advance(back, 1)
    advance(plane, 1)


def finish_kernel(
    query_sum,
    latent_sum,
    latent,
    gain_latent,
    cosine,
    sine_tab,
    wl_0,
    wl_1,
    wl_2,
    wl_3,
    wl_4,
    hidden,
    gain,
    grad_middle,
    normed,
    normed_two,
    grad_logits,
    gain_two_grad,
    layer,
    input_out,
    own_out,
    layer_out,
    changes,
    grads_out,
    landed,
    *scratch,
):
    low = jnp.bfloat16
    greet(plane_peers() + line_peers())
    line = Line(layer, landed, *scratch[:3])
    line.scatter()
    grad_latent = latent_sum[:, :RANK].astype(jnp.float32)
    rope = latent_sum[:, RANK:].astype(jnp.float32)
    values = latent[...]
    inverse = lax.rsqrt(jnp.mean(values * values, 1, keepdims=True) + epsilon)
    weighted = grad_latent * gain_latent[...]
    aligned = jnp.mean(values * weighted, 1, keepdims=True)
    gain_latent_grad = jnp.sum(grad_latent * values * inverse, 0, keepdims=True)
    changes[:, :RANK] = (
        inverse * weighted - values * (inverse * inverse * inverse) * aligned
    ).astype(low)
    kept, crossed = turn_tables(cosine[...], sine_tab[...])
    changes[:, RANK:] = (rope * kept - exchange_halves(rope) * crossed).astype(low)
    grad_normed = query_sum[...].astype(jnp.float32)
    width = hidden.shape[1]
    for j, wl in enumerate((wl_0, wl_1, wl_2, wl_3, wl_4)):
        grad_normed += contract(changes[:, 128 * j : 128 * j + 128], wl[...], 1, 1)
    values = hidden[...].astype(jnp.float32)
    inverse = lax.rsqrt(jnp.mean(values * values, 1, keepdims=True) + epsilon)
    weighted = grad_normed * gain[...]
    aligned = jnp.mean(values * weighted, 1, keepdims=True)
    gain_grad = jnp.sum(grad_normed * values * inverse, 0, keepdims=True)
    input_out[...] = (
        grad_middle[...] + inverse * weighted - values * (inverse * inverse * inverse) * aligned
    ).astype(low)

    def grads(i, carry):
        part = pl.ds(pl.multiple_of(i * 256, 256), 256)
        some = pl.ds(i * 4, 4)
        rows = normed[:, part]
        of_latent = contract(rows, changes[:, :RANK], 0, 0)
        grads_out[some, :, :, :RANK] = of_latent.reshape(4, 8, 8, RANK).astype(low)
        mixed = contract(rows, changes[:, RANK:], 0, 0)
        mixed += contract(normed_two[:, part], grad_logits[...], 0, 0)
        grads_out[some, :, :, RANK : RANK + 128] = mixed.reshape(4, 8, 8, 128).astype(low)
        return carry

    lax.fori_loop(0, width // 256, grads, 0)
    grads_out[:, 1:, :, RANK + 128 :] = jnp.zeros((32, 7, 8, 128), low)
    line_number = lax.broadcasted_iota(jnp.int32, (8, 128), 0)
    gain_two = gain_two_grad[...]
    for e in range(32):
        block = jnp.zeros((8, 128), jnp.float32)
        for row, (values, size) in enumerate(
            ((gain_grad, 64), (gain_two, 64), (gain_latent_grad, 16))
        ):
            piece = values[:, size * e : size * e + size]
            piece = jnp.concatenate([piece, jnp.zeros((1, 128 - size), jnp.float32)], 1)
            block = jnp.where(line_number == row, piece, block)
        grads_out[e, 0, :, RANK + 128 :] = block.astype(low)

    def emit(i, total):
        own_out[i] = total

    plane = plane_sum_steps(grads_out, emit, scratch[3:])
    advance(plane, 1)
    line.add()
    line.gather()
    advance(plane, PLANE_STEPS)
    line.finish()
    layer_out[...] = landed[...]


def unpack_kernel(
    own,
    last,
    ffn,
    middle,
    layer,
    grad_in,
    layer_out,
    grad_in_out,
    query_out,
    latent_out,
    router_out,
    output_out,
    gains_out,
    expand_out,
    gate_out,
    up_out,
    down_out,
):
    layer_out[...] = (middle[...] + layer[...].astype(jnp.float32)).astype(layer_out.dtype)
    grad_in_out[...] = grad_in[...]
    for head in range(HEADS):
        query_out[:, 192 * head : 192 * head + 128] = own[:, 128 * head : 128 * head + 128]
        for half in (0, 1):
            to, start = 192 * head + 128 + 32 * half, 512 + 128 * half + 32 * head
            query_out[:, to : to + 32] = own[:, start : start + 32]
    latent_out[...] = last[:, :576]
    router_out[...] = last[:, 576:640]
    output_out[...] = own[:, 768:1280]
    gains_out[...] = last[0:8, 640:768]
    for j in range(4):
        expand_out[:, 256 * j : 256 * j + 256] = own[16 * j : 16 * j + 16, 1280:1536]
    gate_out[...] = ffn[:, :704].astype(jnp.float32)
    up_out[...] = ffn[:, 768:1472].astype(jnp.float32)
    down_out[...] = ffn[:, 1536:2240].astype(jnp.float32)


def local_call(kernel, name, operands, out_shapes, scratch=()):
    arrays, specs = [], []
    for operand in operands:
        if isinstance(operand, tuple):
            array, block, index = operand
            specs.append(pl.BlockSpec(block, lambda i, index=index: index))
        else:
            array = operand
            zeros = (0,) * array.ndim
            specs.append(pl.BlockSpec(array.shape, lambda i, zeros=zeros: zeros))
        arrays.append(array)
    shapes = [jax.ShapeDtypeStruct(shape, dtype) for shape, dtype in out_shapes]
    return pl.pallas_call(
        kernel,
        grid=(1,),
        out_shape=shapes,
        in_specs=specs,
        out_specs=[
            pl.BlockSpec(shape.shape, lambda i, zeros=(0,) * len(shape.shape): zeros)
            for shape in shapes
        ],
        scratch_shapes=[pltpu.VMEM(shape, dtype) for shape, dtype in scratch],
        compiler_params=pltpu.CompilerParams(vmem_limit_bytes=60 * 2**20),
        name=name,
    )(*arrays)


def joint_call(kernel, collective_id, name, operands, out_shapes, scratch, moved):
    arrays, specs = [], []
    for operand in operands:
        if isinstance(operand, tuple):
            array, block, index = operand
        else:
            array, block, index = operand, operand.shape, (0,) * operand.ndim
        specs.append(
            pl.BlockSpec(block, lambda i, index=index: index, pipeline_mode=pl.Buffered(1))
        )
        arrays.append(array)
    return pl.pallas_call(
        kernel,
        grid=(1,),
        out_shape=[jax.ShapeDtypeStruct(shape, dtype) for shape, dtype in out_shapes],
        in_specs=specs,
        out_specs=[
            pl.BlockSpec(
                shape,
                lambda i, zeros=(0,) * len(shape): zeros,
                pipeline_mode=pl.Buffered(1),
            )
            for shape, _ in out_shapes
        ],
        scratch_shapes=scratch,
        compiler_params=pltpu.CompilerParams(
            collective_id=collective_id, has_side_effects=True, vmem_limit_bytes=60 * 2**20
        ),
        cost_estimate=pl.CostEstimate(flops=0, bytes_accessed=moved, transcendentals=0),
        name=name,
    )(*arrays)


def column_blocks(array, first, number):
    return [(array, (array.shape[0], 128), (0, first + j)) for j in range(number)]


def body(
    hidden_in,
    cotangent,
    segments,
    routes,
    attn_norm,
    w_query,
    w_latent,
    latent_norm,
    w_expand,
    w_output,
    ffn_norm,
    w_router,
    shared_gate,
    shared_up,
    shared_down,
    expert_gate,
    routed_expert_up,
    expert_down,
):
    tokens, model_width = hidden_in.shape
    devices = lax.axis_size("expert")
    low = jnp.bfloat16
    full = jnp.float32
    shard = w_query.shape[0]

    attention_shard, ffn_shard = local_call(
        pack_kernel,
        "pack",
        (
            w_query,
            w_latent,
            attn_norm[None],
            ffn_norm[None],
            latent_norm[None],
            w_output.T,
            w_expand,
            shared_gate,
            w_router,
            shared_up,
            shared_down.T,
        ),
        (((shard, 2176), low), ((shard, 2304), low)),
    )
    ffn_all = lax.all_gather(ffn_shard, "expert", axis=0, tiled=True)
    grad_rows = lax.all_gather(cotangent, "expert", axis=0)
    attention_all = plane_gather(attention_shard, 1, "gather_attention")
    output_blocks = column_blocks(attention_all, 11, 4)
    latent_blocks = column_blocks(attention_all, 6, 5)
    router_block = column_blocks(ffn_all, 5, 1)[0]

    segment_rows = segments.reshape(devices, tokens)
    half_dim = ROPE // 2
    frequencies = rope_base ** (-jnp.arange(half_dim, dtype=full) / half_dim)
    frequencies = jnp.tile(frequencies, HEADS)[None]
    key_count = 9 * tokens
    (
        normed,
        queries,
        latent,
        keys_all,
        cosine,
        sine_tab,
        gain_one,
        gain_two,
        gain_latent,
    ) = joint_call(
        project_kernel,
        2,
        "project",
        (
            hidden_in,
            (attention_all, (model_width, 1408), (0, 0)),
            segment_rows,
            frequencies,
        ),
        (
            ((tokens, model_width), low),
            ((tokens, 768), low),
            ((tokens, RANK), full),
            ((9, tokens // 8, 8, 640), low),
            ((tokens, 128), full),
            ((tokens, 128), full),
            ((1, model_width), full),
            ((1, model_width), full),
            ((1, RANK), full),
        ),
        [
            pltpu.VMEM((tokens // 8, 8, 640), low),
            pltpu.VMEM((9, tokens // 8, 8, 640), low),
            pltpu.SemaphoreType.DMA,
            pltpu.SemaphoreType.DMA((4,)),
            pltpu.SemaphoreType.DMA((4,)),
            pltpu.SemaphoreType.DMA((4,)),
            pltpu.SemaphoreType.DMA((4,)),
        ],
        2**25,
    )
    keys_all = keys_all.reshape(key_count, 640)
    attn_out, attended, probs, expanded, key_rope, expand_w = joint_call(
        attend_kernel,
        3,
        "attend",
        (
            keys_all,
            *column_blocks(attention_all, 15, 2),
            queries,
            segment_rows,
            *output_blocks,
        ),
        (
            ((tokens // 8, 8, model_width), low),
            ((tokens, HEADS * VH), low),
            ((HEADS, tokens, key_count), full),
            ((key_count, HEADS * (NOPE + VH)), low),
            ((key_count, 256), low),
            ((RANK, HEADS * (NOPE + VH)), low),
        ),
        [pltpu.VMEM((tokens // 8, 8, model_width), low)] * 2
        + line_scratch(tokens // 8, model_width),
        2**25,
    )
    attn_out = attn_out.reshape(tokens, model_width)

    route_rows = routes.T
    token_row, middle, gates = local_call(
        route_kernel,
        "route",
        (hidden_in, attn_out, gain_two, router_block, route_rows),
        (
            ((tokens, model_width + 128), low),
            ((tokens, model_width), full),
            ((tokens, 128), full),
        ),
    )
    normed_two = (token_row, (tokens, model_width), (0, 0))

    shared_part, shared_back, ffn_grads = local_call(
        shared_kernel,
        "shared",
        (normed_two, cotangent, ffn_all),
        (
            ((tokens, model_width), full),
            ((tokens, model_width + 128), full),
            (ffn_all.shape, low),
        ),
    )
    own_ffn = lax.psum_scatter(ffn_grads, "expert", scatter_dimension=0, tiled=True)
    token_row, _ = lax.optimization_barrier((token_row, ffn_grads))
    token_rows = plane_gather(token_row, 4, "gather_tokens")

    routed_part, back_part, out_egate, out_eup, out_edown = experts(
        token_rows.reshape(devices // 2, 2 * tokens, -1),
        grad_rows.reshape(devices // 2, 2 * tokens, -1),
        expert_gate.swapaxes(1, 2),
        routed_expert_up.swapaxes(1, 2),
        expert_down,
    )
    out_egate, out_eup = out_egate.swapaxes(1, 2), out_eup.swapaxes(1, 2)
    routed_part, own_ffn = lax.optimization_barrier((routed_part, own_ffn))
    routed_own = lax.psum_scatter(
        routed_part.reshape(-1, model_width), "expert", scatter_dimension=0, tiled=True
    )
    layer_part = (routed_own.astype(full) + shared_part).astype(low)
    back_all = sum_tokens(back_part.reshape(devices * tokens, -1), shared_back, 5)

    (
        grad_middle,
        grad_attn,
        grad_gain_two,
        grad_logits,
        own,
        query_sum,
        latent_sum,
    ) = joint_call(
        attend_back_kernel,
        7,
        "attend_back",
        (
            back_all,
            middle,
            gain_two,
            gates,
            route_rows,
            router_block,
            cotangent,
            *output_blocks,
            probs,
            expanded,
            key_rope,
            queries,
            keys_all,
            expand_w,
            (attention_all, (model_width, 768), (0, 0)),
            cosine,
            sine_tab,
            normed,
            attended,
        ),
        (
            ((tokens, model_width), full),
            ((tokens, model_width), low),
            ((1, model_width), full),
            ((tokens, 128), low),
            ((shard // 8, 8, 1536), full),
            ((tokens // 8, 8, model_width), low),
            ((tokens // 8, 8, 640), low),
        ),
        [
            pltpu.VMEM((key_count, HEADS * (NOPE + VH)), low),
            pltpu.VMEM((key_count, 256), full),
            pltpu.VMEM((tokens, 768), low),
            pltpu.VMEM((tokens // 8, 8, model_width), low),
            pltpu.VMEM((9, tokens // 8, 8, 640), low),
            pltpu.VMEM((devices, shard // 8, 8, 1536), low),
            pltpu.VMEM((5, tokens // 8, 8, 640), low),
            pltpu.VMEM((4, tokens // 8, 8, 640), low),
            pltpu.VMEM((4, tokens // 8, 8, 640), low),
            pltpu.SemaphoreType.DMA((4,)),
            pltpu.SemaphoreType.DMA((4,)),
            pltpu.SemaphoreType.DMA((4,)),
            pltpu.SemaphoreType.DMA((4,)),
            pltpu.VMEM((tokens // 8, 8, 640), low),
            pltpu.VMEM((tokens // 8, 8, model_width), low),
            pltpu.VMEM((tokens // 8, 8, 640), low),
        ]
        + line_scratch(tokens // 8, model_width)
        + line_scratch(tokens // 8, 640)
        + plane_scratch(shard // 8, 1536),
        2**26,
    )
    own = own.reshape(shard, 1536)
    query_sum = query_sum.reshape(tokens, model_width)
    latent_sum = latent_sum.reshape(tokens, 640)
    grad_input, own_last, layer_sum = joint_call(
        finish_kernel,
        9,
        "finish",
        (
            query_sum,
            latent_sum,
            latent,
            gain_latent,
            cosine,
            sine_tab,
            *latent_blocks,
            hidden_in,
            gain_one,
            grad_middle,
            normed,
            normed_two,
            grad_logits,
            grad_gain_two,
            layer_part.reshape(tokens // 8, 8, model_width),
        ),
        (
            ((tokens, model_width), low),
            ((shard // 8, 8, 768), full),
            ((tokens // 8, 8, model_width), low),
        ),
        [
            pltpu.VMEM((tokens, 640), low),
            pltpu.VMEM((devices, shard // 8, 8, 768), low),
            pltpu.VMEM((tokens // 8, 8, model_width), low),
        ]
        + line_scratch(tokens // 8, model_width)
        + plane_scratch(shard // 8, 768),
        2**25,
    )
    own_last = own_last.reshape(shard, 768)
    layer_sum = layer_sum.reshape(tokens, model_width)
    (
        layer_out,
        grad_input,
        out_query,
        out_latent,
        out_router,
        out_output,
        out_gains,
        out_expand,
        out_sgate,
        out_sup,
        out_sdown,
    ) = local_call(
        unpack_kernel,
        "unpack",
        (own, own_last, own_ffn, middle, layer_sum, grad_input),
        (
            ((tokens, model_width), low),
            ((tokens, model_width), low),
            (w_query.shape, full),
            (w_latent.shape, full),
            (w_router.shape, full),
            ((shard, w_output.shape[0]), full),
            ((8, 128), full),
            (w_expand.shape, full),
            (shared_gate.shape, full),
            (shared_up.shape, full),
            ((shard, shared_down.shape[0]), full),
        ),
    )
    return (
        layer_out,
        grad_input,
        out_gains[0, :shard],
        out_query,
        out_latent,
        out_gains[2, : latent_norm.shape[0]],
        out_expand,
        out_output.T,
        out_gains[1, :shard],
        out_router,
        out_sgate,
        out_sup,
        out_sdown.T,
        out_egate,
        out_eup,
        out_edown,
    )


def solution(mesh):
    in_specs = (
        P("expert", None),
        P("expert", None),
        P(),
        P("expert", None),
        P("expert"),
        P("expert", "tensor"),
        P("expert", None),
        P("expert"),
        P("expert", "tensor"),
        P("tensor", "expert"),
        P("expert"),
        P("expert", None),
        P("expert", "tensor"),
        P("expert", "tensor"),
        P("tensor", "expert"),
        P("expert", None, "tensor"),
        P("expert", None, "tensor"),
        P("expert", "tensor", None),
    )
    out_specs = (
        P("expert", None),
        P("expert", None),
        P("expert"),
        P("expert", "tensor"),
        P("expert", None),
        P("expert"),
        P("expert", "tensor"),
        P("tensor", "expert"),
        P("expert"),
        P("expert", None),
        P("expert", "tensor"),
        P("expert", "tensor"),
        P("tensor", "expert"),
        P("expert", None, "tensor"),
        P("expert", None, "tensor"),
        P("expert", "tensor", None),
    )
    return jax.shard_map(body, mesh=mesh, in_specs=in_specs, out_specs=out_specs, check_vma=False)
```

```python
import functools

import jax
import jax.numpy as jnp
from jax import lax
from jax.experimental import pallas as pl
from jax.experimental.pallas import tpu as pltpu
from jax.sharding import PartitionSpec as P

NOPE = 128
ROPE = 64
VH = 128
RANK = 512
WINDOW = 1024


epsilon = 1e-06
masked_score = -1e30
rope_base = 10000.0


MESH = pl.DeviceIdType.MESH
HBM = pl.BlockSpec(memory_space=pltpu.HBM)


def place():
    e = lax.axis_index("expert")
    return lax.axis_index("tensor"), e // 8, lax.rem(e // 2, 4), lax.rem(e, 2)


def at(x, z, c):
    return (x * 4 + z) * 2 + c


def wrap(v):
    return lax.rem(v + 4, 4)


def greet(peers):
    call(peers)
    hear(peers)


def call(peers):
    barrier = pltpu.get_barrier_semaphore()
    for peer in peers:
        pl.semaphore_signal(barrier, inc=1, device_id=peer, device_id_type=MESH)


def hear(peers):
    pl.semaphore_wait(pltpu.get_barrier_semaphore(), len(peers))


def plane_gather_kernel(src, out, ssem, rsem, dssem, drsem, lsem):
    t, x, z, c = place()
    rows = src.shape[0]
    half, quarter = rows // 2, rows // 4
    sibling = (at(x, z, 1 - c), t)
    along_x = [(at(wrap(x - 1), z, c), t), (at(wrap(x + 1), z, c), t)]
    along_z = [(at(x, wrap(z - 1), c), t), (at(x, wrap(z + 1), c), t)]
    greet([sibling] + along_x + along_z)
    own = pltpu.make_async_copy(src, out.at[at(x, z, c)], lsem)
    own.start()
    sent = []

    def piece(h, j1, j2, part=None):
        if h == 0:
            index = at(wrap(x + j2), wrap(z + j1), c)
        else:
            index = at(wrap(x + j1), wrap(z + j2), c)
        if part is None:
            return index, pl.ds(h * half, half)
        return index, pl.ds(h * half + part * quarter, quarter)

    def send(h, slot, which, device, first):
        index, rows_of = which
        return pltpu.make_async_remote_copy(
            src_ref=src.at[rows_of] if first else out.at[index, rows_of],
            dst_ref=out.at[index, rows_of],
            send_sem=ssem.at[h, slot],
            recv_sem=rsem.at[h, slot],
            device_id=device,
            device_id_type=MESH,
        )

    def across(h, j1, j2):
        index, rows_of = piece(h, j1, j2)
        slot = (h * 4 + j1 % 4) * 4 + j2 % 4
        return pltpu.make_async_remote_copy(
            src_ref=src.at[rows_of] if j1 == 0 and j2 == 0 else out.at[index, rows_of],
            dst_ref=out.at[index, rows_of],
            send_sem=dssem.at[slot],
            recv_sem=drsem.at[slot],
            device_id=sibling,
            device_id_type=MESH,
        )

    def ring(h, stage):
        return along_z if (h == 0) == (stage == 1) else along_x

    def stage_one(h, kind):
        left, right = ring(h, 1)
        if kind == 0:
            return send(h, 0, piece(h, 0, 0), right, True)
        if kind == 1:
            return send(h, 1, piece(h, 0, 0), left, True)
        if kind == 2:
            return send(h, 2, piece(h, -1, 0, 0), right, False)
        return send(h, 3, piece(h, 1, 0, 1), left, False)

    def stage_two(h, j1, kind):
        left, right = ring(h, 2)
        slot = 4 + 4 * (j1 % 4) + kind
        if kind == 0:
            return send(h, slot, piece(h, j1, 0), right, j1 == 0)
        if kind == 1:
            return send(h, slot, piece(h, j1, 0), left, j1 == 0)
        if kind == 2:
            return send(h, slot, piece(h, j1, -1, 0), right, False)
        return send(h, slot, piece(h, j1, 1, 1), left, False)

    def go(copy):
        copy.start()
        sent.append(copy)

    for h in (0, 1):
        go(stage_one(h, 0))
        go(stage_one(h, 1))
        go(stage_two(h, 0, 0))
        go(stage_two(h, 0, 1))
        go(across(h, 0, 0))
    for h in (0, 1):
        for kind, j in ((0, -1), (1, 1)):
            stage_one(h, kind).wait_recv()
            go(stage_one(h, 2 + kind))
            go(stage_two(h, j, 0))
            go(stage_two(h, j, 1))
            go(across(h, j, 0))
    for h in (0, 1):
        for kind, j in ((0, -1), (1, 1)):
            stage_two(h, 0, kind).wait_recv()
            go(stage_two(h, 0, 2 + kind))
            go(across(h, 0, j))
    for h in (0, 1):
        stage_one(h, 2).wait_recv()
        stage_one(h, 3).wait_recv()
        go(stage_two(h, 2, 0))
        go(stage_two(h, 2, 1))
        go(across(h, 2, 0))
    for j1 in (-1, 1, 2):
        for h in (0, 1):
            for kind, j in ((0, -1), (1, 1)):
                stage_two(h, j1, kind).wait_recv()
                go(stage_two(h, j1, 2 + kind))
                go(across(h, j1, j))
    for j1 in (0, -1, 1, 2):
        for h in (0, 1):
            stage_two(h, j1, 2).wait_recv()
            stage_two(h, j1, 3).wait_recv()
            go(across(h, j1, 2))
    for h in (0, 1):
        for j1 in (0, -1, 1, 2):
            for j2 in (0, -1, 1, 2):
                across(h, j1, j2).wait_recv()
    for copy in sent:
        copy.wait_send()
    own.wait()


def plane_gather(rows, collective_id, name):
    grouped = rows.reshape(rows.shape[0] // 8, 8, rows.shape[1])
    gathered = pl.pallas_call(
        plane_gather_kernel,
        out_shape=jax.ShapeDtypeStruct((32, *grouped.shape), rows.dtype),
        in_specs=[HBM],
        out_specs=HBM,
        scratch_shapes=[
            pltpu.SemaphoreType.DMA((2, 20)),
            pltpu.SemaphoreType.DMA((2, 20)),
            pltpu.SemaphoreType.DMA((32,)),
            pltpu.SemaphoreType.DMA((32,)),
            pltpu.SemaphoreType.DMA,
        ],
        compiler_params=pltpu.CompilerParams(
            collective_id=collective_id, has_side_effects=True, vmem_limit_bytes=62 * 2**20
        ),
        cost_estimate=pl.CostEstimate(
            flops=0, bytes_accessed=64 * rows.size * rows.dtype.itemsize, transcendentals=0
        ),
        name=name,
    )(grouped)
    return gathered.reshape(32 * rows.shape[0], rows.shape[1])


def line_peers():
    e, t = lax.axis_index("expert"), lax.axis_index("tensor")
    return [(e, lax.rem(t + k, 4)) for k in (1, 2, 3)]


class Line:
    def __init__(self, src, out, taken, ssem, rsem):
        t = lax.axis_index("tensor")
        self.src, self.out, self.taken, self.ssem, self.rsem = src, out, taken, ssem, rsem
        self.share, self.t = src.shape[0] // 4, t
        self.others = line_peers()

    def share_out(self, k):
        device = self.others[k - 1]
        return pltpu.make_async_remote_copy(
            src_ref=self.src.at[pl.ds(device[1] * self.share, self.share)],
            dst_ref=self.taken.at[k - 1],
            send_sem=self.ssem.at[0, k - 1],
            recv_sem=self.rsem.at[0, k - 1],
            device_id=device,
            device_id_type=MESH,
        )

    def pass_on(self, k):
        rows = pl.ds(self.t * self.share, self.share)
        return pltpu.make_async_remote_copy(
            src_ref=self.out.at[rows],
            dst_ref=self.out.at[rows],
            send_sem=self.ssem.at[1, k - 1],
            recv_sem=self.rsem.at[1, k - 1],
            device_id=self.others[k - 1],
            device_id_type=MESH,
        )

    def scatter(self):
        for k in (2, 1, 3):
            self.share_out(k).start()

    def add(self):
        for k in (2, 1, 3):
            self.share_out(k).wait_recv()

        def step(i, carry):
            total = self.src[self.t * self.share + i].astype(jnp.float32)
            for k in range(3):
                total = total + self.taken[k, i].astype(jnp.float32)
            self.out[self.t * self.share + i] = total.astype(self.out.dtype)
            return carry

        lax.fori_loop(0, self.share, step, 0)

    def gather(self):
        for k in (2, 1, 3):
            self.pass_on(k).start()

    def finish(self):
        for k in (2, 1, 3):
            self.pass_on(k).wait_recv()
        for k in (2, 1, 3):
            self.share_out(k).wait_send()
            self.pass_on(k).wait_send()


def line_sum_kernel(src, out, taken, ssem, rsem):
    line = Line(src, out, taken, ssem, rsem)
    greet(line.others)
    line.scatter()
    line.add()
    line.gather()
    line.finish()


PLANE_STEPS = 1 + 8 + 16 + 2 + 4 + 2


def plane_sum_steps(source, emit, scratch):
    mine, peer, one, two, last_one, last_two, lsem, pssem, prsem, ssem, rsem = scratch
    t, x, z, c = place()
    groups = mine.shape[2]
    half, quarter = groups // 2, groups // 4
    sibling = (at(x, z, 1 - c), t)
    along_x = [(at(wrap(x - 1), z, c), t), (at(wrap(x + 1), z, c), t)]
    along_z = [(at(x, wrap(z - 1), c), t), (at(x, wrap(z + 1), c), t)]
    order = (2, 1, 3, 0)
    sent = []

    def view(ref, h, a, b):
        if h == 0:
            return ref.at[a, b, pl.ds(0, half)]
        return ref.at[b, a, pl.ds(half, half)]

    def target(dx, dz, core):
        return at(wrap(x + dx), wrap(z + dz), core)

    def outward(dx, dz):
        return pltpu.make_async_remote_copy(
            src_ref=source.at[target(dx, dz, 1 - c)],
            dst_ref=peer.at[dx, dz],
            send_sem=pssem.at[dx, dz],
            recv_sem=prsem.at[dx, dz],
            device_id=sibling,
            device_id_type=MESH,
        )

    def inward(dx, dz):
        return pltpu.make_async_copy(
            source.at[target(dx, dz, c)], mine.at[dx, dz], lsem.at[dx, dz]
        )

    def hop(h, slot, src, dst, device):
        return pltpu.make_async_remote_copy(
            src_ref=src,
            dst_ref=dst,
            send_sem=ssem.at[h, slot],
            recv_sem=rsem.at[h, slot],
            device_id=device,
            device_id_type=MESH,
        )

    def ring(h, stage):
        return along_x if (h == 0) == (stage == 1) else along_z

    def first(h, b, side):
        return hop(
            h,
            4 * b + side,
            view(mine, h, 2, b).at[pl.ds(side * quarter, quarter)],
            one.at[h, b, side],
            ring(h, 1)[1 - side],
        )

    def second(h, b, side):
        return hop(
            h, 4 * b + 2 + side, view(mine, h, 1 + 2 * side, b), two.at[h, b, side], ring(h, 1)[1 - side]
        )

    def third(h, side):
        return hop(
            h,
            16 + side,
            view(mine, h, 0, 2).at[pl.ds(side * quarter, quarter)],
            last_one.at[h, side],
            ring(h, 2)[1 - side],
        )

    def fourth(h, side):
        return hop(
            h, 18 + side, view(mine, h, 0, 1 + 2 * side), last_two.at[h, side], ring(h, 2)[1 - side]
        )

    def go(copy):
        copy.start()
        sent.append(copy)

    def accumulate(into, sources_of, number):
        def step(i, carry):
            total = into[i].astype(jnp.float32)
            for source in sources_of:
                total = total + source[i].astype(jnp.float32)
            into[i] = total.astype(into.dtype)
            return carry

        lax.fori_loop(0, number, step, 0)

    spots = [(2, 2), (2, 1), (1, 2), (2, 3), (3, 2), (2, 0), (0, 2), (1, 1)]
    spots += [(1, 3), (3, 1), (3, 3), (1, 0), (0, 1), (3, 0), (0, 3), (0, 0)]
    for spot in spots:
        inward(*spot).start()
        go(outward(*spot))
    merged = set()

    yield

    def merge(h, a, b):
        spot = (a, b) if h == 0 else (b, a)
        if spot in merged:
            return
        merged.add(spot)
        inward(*spot).wait()
        outward(*spot).wait_recv()
        accumulate(mine.at[spot[0], spot[1]], [peer.at[spot[0], spot[1]]], groups)

    for b in order:
        for h in (0, 1):
            merge(h, 2, b)
            for side in (0, 1):
                go(first(h, b, side))
            yield
    for side in (0, 1):
        for b in order:
            for h in (0, 1):
                a = 1 + 2 * side
                merge(h, a, b)
                first(h, b, side).wait_recv()
                accumulate(
                    view(mine, h, a, b).at[pl.ds(side * quarter, quarter)],
                    [one.at[h, b, side]],
                    quarter,
                )
                go(second(h, b, side))
                yield

    def gathered_here(h, b):
        merge(h, 0, b)
        for side in (0, 1):
            second(h, b, side).wait_recv()
        accumulate(view(mine, h, 0, b), [two.at[h, b, 0], two.at[h, b, 1]], half)

    for h in (0, 1):
        gathered_here(h, 2)
        for side in (0, 1):
            go(third(h, side))
        yield
    for side in (0, 1):
        b = 1 + 2 * side
        for h in (0, 1):
            gathered_here(h, b)
            third(h, side).wait_recv()
            accumulate(
                view(mine, h, 0, b).at[pl.ds(side * quarter, quarter)],
                [last_one.at[h, side]],
                quarter,
            )
            go(fourth(h, side))
            yield
    for h in (0, 1):
        gathered_here(h, 0)
        for side in (0, 1):
            fourth(h, side).wait_recv()

        def finish(i, carry, h=h):
            total = mine[0, 0, h * half + i].astype(jnp.float32)
            for side in (0, 1):
                total = total + last_two[h, side, i].astype(jnp.float32)
            emit(h * half + i, total)
            return carry

        lax.fori_loop(0, half, finish, 0)
        yield
    for copy in sent:
        copy.wait_send()


def plane_peers():
    t, x, z, c = place()
    return [
        (at(x, z, 1 - c), t),
        (at(wrap(x - 1), z, c), t),
        (at(wrap(x + 1), z, c), t),
        (at(x, wrap(z - 1), c), t),
        (at(x, wrap(z + 1), c), t),
    ]


def plane_scratch(groups, width):
    half, quarter = groups // 2, groups // 4
    low = jnp.bfloat16
    return [
        pltpu.VMEM((4, 4, groups, 8, width), low),
        pltpu.VMEM((4, 4, groups, 8, width), low),
        pltpu.VMEM((2, 4, 2, quarter, 8, width), low),
        pltpu.VMEM((2, 4, 2, half, 8, width), low),
        pltpu.VMEM((2, 2, quarter, 8, width), low),
        pltpu.VMEM((2, 2, half, 8, width), low),
        pltpu.SemaphoreType.DMA((4, 4)),
        pltpu.SemaphoreType.DMA((4, 4)),
        pltpu.SemaphoreType.DMA((4, 4)),
        pltpu.SemaphoreType.DMA((2, 20)),
        pltpu.SemaphoreType.DMA((2, 20)),
    ]


def line_scratch(groups, width):
    return [
        pltpu.VMEM((3, groups // 4, 8, width), jnp.bfloat16),
        pltpu.SemaphoreType.DMA((2, 3)),
        pltpu.SemaphoreType.DMA((2, 3)),
    ]


def advance(task, number):
    for _ in range(number):
        next(task, None)


def by_expert(part, groups):
    return part.reshape(32, groups, 8, part.shape[1])


def by_group(part):
    return part.reshape(part.shape[0] // 8, 8, part.shape[1])


def communicate(kernel, collective_id, name, operands, where, out_shapes, scratch, moved):
    vmem = pl.BlockSpec(memory_space=pltpu.VMEM)
    shapes = [jax.ShapeDtypeStruct(shape, dtype) for shape, dtype in out_shapes]
    return pl.pallas_call(
        kernel,
        out_shape=shapes,
        in_specs=[vmem if inside else HBM for inside in where],
        out_specs=[vmem] * len(shapes),
        scratch_shapes=scratch,
        compiler_params=pltpu.CompilerParams(
            collective_id=collective_id, has_side_effects=True, vmem_limit_bytes=60 * 2**20
        ),
        cost_estimate=pl.CostEstimate(flops=0, bytes_accessed=moved, transcendentals=0),
        name=name,
    )(*operands)


def sum_tokens_kernel(source, shared, out, held, taken, line_ssem, line_rsem, *scratch):
    half = out.shape[0] // 2

    def emit(i, total):
        held[i] = (total + shared[i]).astype(held.dtype)

    greet(plane_peers() + line_peers())
    plane = plane_sum_steps(source, emit, scratch)
    lines = []
    for h in (0, 1):
        rows = pl.ds(h * half, half)
        lines.append(
            Line(held.at[rows], out.at[rows], taken.at[h], line_ssem.at[h], line_rsem.at[h])
        )
    advance(plane, PLANE_STEPS - 1)
    lines[0].scatter()
    advance(plane, 1)
    lines[1].scatter()
    for line in lines:
        line.add()
        line.gather()
    for line in lines:
        line.finish()
    advance(plane, 1)


def sum_tokens(part, shared, collective_id):
    groups, width = part.shape[0] // 256, part.shape[1]
    (summed,) = communicate(
        sum_tokens_kernel,
        collective_id,
        "sum_tokens",
        (by_expert(part, groups), by_group(shared)),
        (False, True),
        (((groups, 8, width), jnp.bfloat16),),
        [
            pltpu.VMEM((groups, 8, width), jnp.bfloat16),
            pltpu.VMEM((2, 3, groups // 8, 8, width), jnp.bfloat16),
            pltpu.SemaphoreType.DMA((2, 2, 3)),
            pltpu.SemaphoreType.DMA((2, 2, 3)),
        ]
        + plane_scratch(groups, width),
        16 * part.size,
    )
    return summed.reshape(8 * groups, width)


def reach_back_peers():
    t, x, z, c = place()
    along = [(at(x, wrap(z - r), c), t) for r in (1, 2, 3)]
    return [(at(x, z, 1 - c), t), (at(wrap(x - 1), z, c), t)] + along


def reach_back_run(src, out, lsem, ssem, rsem, pssem, prsem):
    t, x, z, c = place()
    sibling = (at(x, z, 1 - c), t)
    own = pltpu.make_async_copy(src, out.at[8], lsem)
    own.start()

    def onward():
        return pltpu.make_async_remote_copy(
            src_ref=src,
            dst_ref=out.at[0],
            send_sem=ssem.at[3],
            recv_sem=rsem.at[3],
            device_id=(at(wrap(x + 1), z, c), t),
            device_id_type=MESH,
        )

    def along(r, source):
        return pltpu.make_async_remote_copy(
            src_ref=source,
            dst_ref=out.at[8 - 2 * r],
            send_sem=ssem.at[r - 1],
            recv_sem=rsem.at[r - 1],
            device_id=(at(x, wrap(z + r), c), t),
            device_id_type=MESH,
        )

    def near(i):
        return pltpu.make_async_remote_copy(
            src_ref=out.at[8 - 2 * (i + c)],
            dst_ref=out.at[7 - 2 * i],
            send_sem=pssem.at[i],
            recv_sem=prsem.at[i],
            device_id=sibling,
            device_id_type=MESH,
        )

    onward().start()
    for r in (2, 1, 3):

        @pl.when(z + r < 4)
        def _(r=r):
            along(r, src).start()

    own.wait()
    onward().wait_recv()
    for r in (2, 3, 1):

        @pl.when(z + r >= 4)
        def _(r=r):
            along(r, out.at[0]).start()

    for r in (1, 3, 2):
        along(r, src).wait_recv()
    for i in range(4):
        near(i).start()
    for i in range(4):
        near(i).wait()
    onward().wait_send()
    for r in (1, 2, 3):
        along(r, src).wait_send()


def chip_at(x, z, c, distance):
    place_on = lax.rem(x * 4 + z + 16 + distance, 16)
    return place_on * 2 + c


def send_back_steps(src, out, held, near_in, far_in, ssem, rsem, pssem, prsem):
    t, x, z, c = place()
    groups = out.shape[0]
    sibling = (at(x, z, 1 - c), t)
    behind = [(chip_at(x, z, c, -k), t) for k in (1, 2, 3, 4)]

    def near(i):
        return pltpu.make_async_remote_copy(
            src_ref=src.at[7 - 2 * i],
            dst_ref=near_in.at[i],
            send_sem=pssem.at[i],
            recv_sem=prsem.at[i],
            device_id=sibling,
            device_id_type=MESH,
        )

    def far(k):
        return pltpu.make_async_remote_copy(
            src_ref=held.at[k],
            dst_ref=far_in.at[k - 1],
            send_sem=ssem.at[k - 1],
            recv_sem=rsem.at[k - 1],
            device_id=behind[k - 1],
            device_id_type=MESH,
        )

    for i in (3, 2, 1, 0):
        near(i).start()
    yield
    for i in (3, 2, 1, 0):
        near(i).wait_recv()
    for k in (4, 3, 2, 1, 0):

        def step(i, carry, k=k):
            total = src[8 - 2 * k, i].astype(jnp.float32)
            other = near_in[jnp.clip(k - c, 0, 3), i].astype(jnp.float32)
            covered = jnp.logical_and(k - c >= 0, k - c <= 3)
            total = total + jnp.where(covered, other, jnp.zeros_like(other))
            held[k, i] = total.astype(held.dtype)
            return carry

        lax.fori_loop(0, groups, step, 0)
        if k > 0:
            far(k).start()
    yield
    for k in (1, 2, 3, 4):
        far(k).wait_recv()

    def last(i, carry):
        total = held[0, i].astype(jnp.float32)
        for k in range(4):
            total = total + far_in[k, i].astype(jnp.float32)
        out[i] = total.astype(out.dtype)
        return carry

    lax.fori_loop(0, groups, last, 0)
    yield
    for k in (1, 2, 3, 4):
        far(k).wait_send()
    for i in range(4):
        near(i).wait_send()


def contract(left_side, right_side, left_dim, right_dim):
    return lax.dot_general(
        left_side,
        right_side,
        (((left_dim,), (right_dim,)), ((), ())),
        preferred_element_type=jnp.float32,
    )


def experts_kernel(
    token_rows,
    grad_rows,
    gate_in,
    up_in,
    down_in,
    routed_out,
    back_out,
    gate_out,
    up_out,
    down_out,
    ranks,
    rows_x,
    rows_g,
    weights,
    dots,
    staged,
    gate_up,
    down,
    hidden,
    grads,
    sums_one,
    sums_two,
    in_sem,
    out_sem,
):
    step = pl.program_id(0)
    low = jnp.bfloat16
    units = down_in.shape[1]
    wide = down.shape[0]
    pair_slots = 48
    width = rows_x.shape[2]
    blocks = ranks.shape[0]
    count = rows_x.shape[1]
    part = 256

    def load(k, expert):
        source = (gate_in, up_in, down_in)[k].at[expert]
        return pltpu.make_async_copy(source, staged.at[k], in_sem.at[k])

    def store(k, expert):
        if k == 2:
            source = sums_two.at[pl.ds(0, units)]
        else:
            source = sums_one.at[pl.ds(k * wide, units)]
        target = (gate_out, up_out, down_out)[k].at[expert]
        return pltpu.make_async_copy(source, target, out_sem.at[k])

    def picks(block):
        row = lax.broadcasted_iota(jnp.int32, (pair_slots, 256), 0)
        column = lax.broadcasted_iota(jnp.int32, (pair_slots, 256), 1)
        second = row >= 24
        slot = jnp.where(second, row - 24, row).astype(jnp.float32)
        inside = second == (column >= 128)
        found = []
        for expert in (0, 1):
            rank = ranks[block, expert : expert + 1, :]
            found.append(jnp.logical_and(rank == slot, inside))
        return found

    @pl.when(step == 0)
    def _():
        for k in range(3):
            load(k, 0).start()

    def rank_slots(block):
        square = (128, 128)
        same = lax.broadcasted_iota(jnp.int32, square, 0) == lax.broadcasted_iota(
            jnp.int32, square, 1
        )
        turned = contract(
            jnp.where(same, 1.0, 0.0).astype(low), token_rows[0, :, width:], 1, 1
        )
        first = lax.broadcasted_iota(jnp.int32, (256, 256), 0)
        second = lax.broadcasted_iota(jnp.int32, (256, 256), 1)
        ahead = jnp.logical_and(first < second, (first >= 128) == (second >= 128))
        line = lax.broadcasted_iota(jnp.int32, (8, 256), 0)
        named = jnp.zeros((8, 256), jnp.float32)
        shares = jnp.zeros((8, 256), jnp.float32)
        for expert in (0, 1):
            number = (lax.axis_index("expert") * 2 + expert).astype(jnp.float32)
            match = turned[0:8] == number
            present = jnp.sum(jnp.where(match, 1.0, 0.0), 0, keepdims=True)
            share = jnp.sum(jnp.where(match, turned[8:16] + turned[16:24], 0.0), 0, keepdims=True)
            named = named + jnp.where(line == expert, present, 0.0)
            shares = shares + jnp.where(line == 2 + expert, share, 0.0)
        rank = contract(named.astype(low), jnp.where(ahead, 1.0, 0.0).astype(low), 1, 0)
        rank = jnp.where(named > 0.0, rank, -1.0)
        ranks[block] = jnp.where(line < 2, rank, shares)

    @pl.when(step < blocks)
    def _():
        rank_slots(step)
        found = picks(step)
        pick = jnp.concatenate([jnp.where(f, 1.0, 0.0) for f in found], 0).astype(low)
        from_x = contract(pick, token_rows[0, :, :width], 1, 0).astype(low)
        from_g = contract(pick, grad_rows[0], 1, 0).astype(low)
        here = pl.ds(pl.multiple_of(step * pair_slots, pair_slots), pair_slots)
        for expert in (0, 1):
            lines = slice(expert * pair_slots, (expert + 1) * pair_slots)
            rows_x[expert, here, :] = from_x[lines]
            rows_g[expert, here, :] = from_g[lines]
            shares = ranks[step, 2 + expert : 3 + expert, :]
            weight = jnp.sum(jnp.where(found[expert], shares, 0.0), 1, keepdims=True)
            weights[expert, here, :] = jnp.broadcast_to(weight, (pair_slots, 128))

    for expert in (0, 1):

        @pl.when(step == blocks + expert)
        def _(expert=expert):
            for k in range(3):
                load(k, expert).wait()
            nothing = jnp.zeros((wide - units, width), low)
            gate_up[pl.ds(units, wide - units), :] = nothing
            gate_up[pl.ds(wide + units, wide - units), :] = nothing
            down[pl.ds(units, wide - units), :] = nothing

            def cast(i, carry):
                rows = pl.ds(pl.multiple_of(i * 32, 32), 32)
                gate_up[rows, :] = staged[0, rows, :].astype(low)
                gate_up[pl.ds(pl.multiple_of(wide + i * 32, 32), 32), :] = staged[
                    1, rows, :
                ].astype(low)
                down[rows, :] = staged[2, rows, :].astype(low)
                return carry

            lax.fori_loop(0, units // 32, cast, 0)
            if expert == 0:
                for k in range(3):
                    load(k, 1).start()

            def middle(i, carry):
                rows = pl.ds(pl.multiple_of(i * part, part), part)
                before = contract(rows_x[expert, rows, :], gate_up[...], 1, 1)
                plain = contract(rows_g[expert, rows, :], down[...], 1, 1)
                weight = weights[expert, rows, :][:, 0:1]
                gate, up = before[:, :wide], before[:, wide:]
                sigmoid = 1.0 / (1.0 + jnp.exp(-gate))
                on = gate * sigmoid
                value = on * up
                hidden[rows, :] = (weight * value).astype(low)
                dot = jnp.sum(plain * value, 1, keepdims=True)
                mine = 64 + lax.axis_index("expert") * 2 + expert
                lane = lax.broadcasted_iota(jnp.int32, (part, 128), 1)
                dots[expert, rows, :] = jnp.where(lane == mine, dot, 0.0).astype(low)
                change = weight * plain
                grads[rows, :wide] = (change * up * (sigmoid * (1.0 + gate * (1.0 - sigmoid)))).astype(
                    low
                )
                grads[rows, wide:] = (change * on).astype(low)
                return carry

            lax.fori_loop(0, count // part, middle, 0)
            if expert == 1:
                for k in range(3):
                    store(k, 0).wait()

            def weight_grads(i, carry):
                columns = pl.ds(pl.multiple_of(i * part, part), part)
                sums_one[columns, :] = contract(grads[:, columns], rows_x[expert], 0, 0)
                return carry

            lax.fori_loop(0, 2 * wide // part, weight_grads, 0)
            for i in range(wide // 128):
                columns = pl.ds(i * 128, 128)
                sums_two[columns, :] = contract(hidden[:, columns], rows_g[expert], 0, 0)
            for k in range(3):
                store(k, expert).start()

            def results(i, carry):
                rows = pl.ds(pl.multiple_of(i * part, part), part)
                rows_x[expert, rows, :] = contract(hidden[rows, :], down[...], 1, 0).astype(low)
                rows_g[expert, rows, :] = contract(grads[rows, :], gate_up[...], 1, 0).astype(low)
                return carry

            lax.fori_loop(0, count // part, results, 0)

    @pl.when(step >= blocks + 2)
    def _():
        block = step - blocks - 2
        pick = jnp.concatenate([jnp.where(f, 1.0, 0.0) for f in picks(block)], 0).astype(low)
        here = pl.ds(pl.multiple_of(block * pair_slots, pair_slots), pair_slots)

        def both(ref):
            return jnp.concatenate([ref[0, here, :], ref[1, here, :]], 0)

        routed_out[0] = contract(pick, both(rows_x), 0, 0).astype(low)
        back_out[0, :, :width] = contract(pick, both(rows_g), 0, 0).astype(low)
        back_out[0, :, width:] = contract(pick, both(dots), 0, 0).astype(low)

    @pl.when(step == 2 * blocks + 1)
    def _():
        for k in range(3):
            store(k, 1).wait()


def experts(token_rows, grad_rows, gate, up, down):
    low = jnp.bfloat16
    blocks = token_rows.shape[0]
    local, units, width = down.shape
    wide = (units + 127) // 128 * 128
    count = blocks * 48
    last = blocks - 1

    def entering(i):
        return (jnp.minimum(i, last), 0, 0)

    def leaving(i):
        return (jnp.maximum(i - blocks - 2, 0), 0, 0)

    weight = jax.ShapeDtypeStruct((local, units, width), jnp.float32)
    return pl.pallas_call(
        experts_kernel,
        grid=(2 * blocks + 2,),
        out_shape=(
            jax.ShapeDtypeStruct((blocks, 256, width), low),
            jax.ShapeDtypeStruct((blocks, 256, width + 128), low),
            weight,
            weight,
            weight,
        ),
        in_specs=[
            pl.BlockSpec((1, 256, width + 128), entering),
            pl.BlockSpec((1, 256, width), entering),
            HBM,
            HBM,
            HBM,
        ],
        out_specs=(
            pl.BlockSpec((1, 256, width), leaving),
            pl.BlockSpec((1, 256, width + 128), leaving),
            HBM,
            HBM,
            HBM,
        ),
        scratch_shapes=[
            pltpu.VMEM((blocks, 8, 256), jnp.float32),
            pltpu.VMEM((local, count, width), low),
            pltpu.VMEM((local, count, width), low),
            pltpu.VMEM((local, count, 128), jnp.float32),
            pltpu.VMEM((local, count, 128), low),
            pltpu.VMEM((3, units, width), jnp.float32),
            pltpu.VMEM((2 * wide, width), low),
            pltpu.VMEM((wide, width), low),
            pltpu.VMEM((count, wide), low),
            pltpu.VMEM((count, 2 * wide), low),
            pltpu.VMEM((2 * wide, width), jnp.float32),
            pltpu.VMEM((wide, width), jnp.float32),
            pltpu.SemaphoreType.DMA((3,)),
            pltpu.SemaphoreType.DMA((3,)),
        ],
        compiler_params=pltpu.CompilerParams(
            dimension_semantics=("arbitrary",), vmem_limit_bytes=60 * 2**20
        ),
        cost_estimate=pl.CostEstimate(
            flops=18 * local * count * wide * width,
            bytes_accessed=100 * 2**20,
            transcendentals=local * count * wide,
        ),
        name="experts",
    )(token_rows, grad_rows, gate, up, down)


def rms_forward(values, gains):
    inverse = lax.rsqrt(jnp.mean(values * values, -1, keepdims=True) + epsilon)
    return (values * inverse * gains, inverse)


def rope_tables(positions):
    half_dim = ROPE // 2
    freqs = rope_base ** (-jnp.arange(half_dim, dtype=jnp.float32) / half_dim)
    angles = positions.astype(jnp.float32)[:, None] * freqs[None, :]
    return (jnp.cos(angles), jnp.sin(angles))


HEADS = 4
SCALE = (NOPE + ROPE) ** (-0.5)


def in_groups(values):
    return values.reshape(values.shape[0] // 8, 8, values.shape[1])


def lanes(shape):
    return lax.broadcasted_iota(jnp.int32, shape, 1)


def turn_tables(cosine, sine_tab):
    lane = lanes(cosine.shape)
    kept = jnp.where(lane < 64, cosine, 0.0)
    crossed = jnp.where(lane < 32, -sine_tab, jnp.where(lane < 64, sine_tab, 0.0))
    return kept, crossed


def exchange_halves(values):
    shape = (128, 128)
    to = lanes(shape)
    from_lane = lax.broadcasted_iota(jnp.int32, shape, 0)
    other = jnp.where(to < 32, to + 32, jnp.where(to < 64, to - 32, to))
    swap = jnp.where(from_lane == other, 1.0, 0.0)
    return lax.dot_general(
        values,
        swap,
        (((1,), (0,)), ((), ())),
        precision=lax.Precision.HIGHEST,
        preferred_element_type=jnp.float32,
    )


def fold_matrix():
    shape = (128, 256)
    to = lanes(shape)
    wanted = jnp.where(to >= 128, 32, 0) + lax.rem(to, 32)
    return jnp.where(lax.broadcasted_iota(jnp.int32, shape, 0) == wanted, 1.0, 0.0).astype(
        jnp.bfloat16
    )


def head_lanes(values, head):
    lane = lanes(values.shape)
    inside = jnp.logical_and(lane >= 32 * head, lane < 32 * head + 32)
    return jnp.where(inside, values, jnp.zeros_like(values))


def pack_kernel(
    query,
    latent,
    gain_one,
    gain_two,
    gain_latent,
    output,
    expand,
    gate,
    router,
    up,
    down,
    attention_out,
    ffn_out,
):
    low = jnp.bfloat16
    shard = query.shape[0]
    for head in range(HEADS):
        start = 192 * head
        attention_out[:, 128 * head : 128 * head + 128] = query[:, start : start + 128].astype(low)
    for half in (0, 1):
        starts = [192 * head + 128 + 32 * half for head in range(HEADS)]
        pieces = [query[:, start : start + 32] for start in starts]
        to = 512 + 128 * half
        attention_out[:, to : to + 128] = jnp.concatenate(pieces, 1).astype(low)
    attention_out[:, 768:1280] = latent[:, :RANK].astype(low)
    row = lax.broadcasted_iota(jnp.int32, (shard, shard), 0)
    gains = jnp.where(row == 0, gain_one[...], 0.0)
    gains = jnp.where(row == 1, gain_two[...], gains)
    gains = jnp.where(row == 2, gain_latent[...], gains)
    attention_out[:, 1280:1408] = jnp.concatenate([latent[:, RANK:], gains], 1).astype(low)
    attention_out[:, 1408:1920] = output[...].astype(low)
    for j in range(4):
        attention_out[16 * j : 16 * j + 16, 1920:] = expand[:, 256 * j : 256 * j + 256].astype(low)
    gap = jnp.zeros((shard, 64), jnp.float32)
    for k, (wide, narrow) in enumerate(((gate, router[...]), (up, gap), (down, gap))):
        start = 768 * k
        ffn_out[:, start : start + 640] = wide[:, :640].astype(low)
        ffn_out[:, start + 640 : start + 768] = jnp.concatenate(
            [wide[:, 640:704], narrow], 1
        ).astype(low)


def project_kernel(
    hidden,
    weights,
    gain,
    gain_latent,
    cosine,
    sine_tab,
    normed_out,
    query_out,
    latent_out,
    keys_out,
    key_row,
    landed,
    *scratch,
):
    low = jnp.bfloat16
    peers = reach_back_peers()
    call(peers)
    normed = rms_forward(hidden[...].astype(jnp.float32), gain[...])[0].astype(low)
    normed_out[...] = normed
    query = contract(normed, weights[:, :768], 1, 0)
    first, second = query[:, 512:640], query[:, 640:768]
    cos, sin = cosine[...], sine_tab[...]
    query_out[:, :512] = query[:, :512].astype(low)
    query_out[:, 512:640] = (first * cos - second * sin).astype(low)
    query_out[:, 640:768] = (second * cos + first * sin).astype(low)
    latent = contract(normed, weights[:, 768:1408], 1, 0)
    latent_out[...] = latent[:, :RANK]
    compressed = rms_forward(latent[:, :RANK], gain_latent[...])[0]
    key_row[:, :, :RANK] = in_groups(compressed).astype(low)
    rope = latent[:, RANK:]
    kept, crossed = turn_tables(cos, sin)
    turned = rope * kept + exchange_halves(rope) * crossed
    key_row[:, :, RANK:] = in_groups(turned).astype(low)
    hear(peers)
    reach_back_run(key_row, landed, *scratch)
    keys_out[...] = landed[...]


def attend_kernel(
    keys,
    expand,
    query,
    own_segment,
    key_segment,
    wo_0,
    wo_1,
    wo_2,
    wo_3,
    out,
    attended,
    probs,
    expanded,
    key_rope,
    held,
    landed,
    *scratch,
):
    low = jnp.bfloat16
    peers = line_peers()
    call(peers)
    rows = query.shape[0]
    count = keys.shape[0]
    fold = fold_matrix()

    def expand_rows(i, carry):
        part = pl.ds(pl.multiple_of(i * rows, rows), rows)
        expanded[part, :] = contract(keys[part, :RANK], expand[...], 1, 0).astype(low)
        key_rope[part, :] = contract(keys[part, RANK:], fold, 1, 0).astype(low)
        return carry

    lax.fori_loop(0, count // rows, expand_rows, 0)
    shape = (rows, count)
    distance = lax.broadcasted_iota(jnp.int32, shape, 0) + WINDOW - lanes(shape)
    allowed = jnp.logical_and(distance >= 0, distance < WINDOW)
    allowed = jnp.logical_and(allowed, own_segment[...] == key_segment[...])
    total = jnp.zeros((rows, wo_0.shape[0]), jnp.float32)
    for head, wo in enumerate((wo_0, wo_1, wo_2, wo_3)):
        start = 256 * head
        scores = contract(query[:, 128 * head : 128 * head + 128], expanded[:, start : start + 128], 1, 1)
        scores += contract(head_lanes(query[:, 512:640], head), key_rope[:, :128], 1, 1)
        scores += contract(head_lanes(query[:, 640:768], head), key_rope[:, 128:], 1, 1)
        scores = jnp.where(allowed, scores * SCALE, masked_score)
        exponent = jnp.exp(scores - jnp.max(scores, 1, keepdims=True))
        share = exponent / jnp.sum(exponent, 1, keepdims=True)
        probs[head] = share
        mixed = contract(share.astype(low), expanded[:, start + 128 : start + 256], 1, 0).astype(low)
        attended[:, 128 * head : 128 * head + 128] = mixed
        total += contract(mixed, wo[...], 1, 1)
    held[...] = in_groups(total).astype(low)
    hear(peers)
    line = Line(held, landed, *scratch)
    line.scatter()
    line.add()
    line.gather()
    line.finish()
    out[...] = landed[...]


def route_kernel(hidden, attention, gain, router, routes, token_out, middle_out, gates_out):
    low = jnp.bfloat16
    middle = hidden[...].astype(jnp.float32) + attention[...].astype(jnp.float32)
    middle_out[...] = middle
    normed = rms_forward(middle, gain[...])[0].astype(low)
    width = normed.shape[1]
    token_out[:, :width] = normed
    logits = contract(normed, router[...], 1, 0)
    lane = lanes(logits.shape)
    named = [routes[:, r : r + 1] for r in range(6)]
    chosen = [
        jnp.sum(jnp.where(lane == number + 64, logits, 0.0), 1, keepdims=True) for number in named
    ]
    most = functools.reduce(jnp.maximum, chosen)
    exponents = [jnp.exp(value - most) for value in chosen]
    total = functools.reduce(jnp.add, exponents)
    extra = jnp.where(jnp.logical_or(lane == 6, lane == 7), 128.0, 0.0)
    gates = jnp.zeros(logits.shape, jnp.float32)
    for r in range(6):
        weight = exponents[r] / total
        high = weight.astype(low).astype(jnp.float32)
        extra += jnp.where(lane == r, named[r].astype(jnp.float32), 0.0)
        extra += jnp.where(lane == 8 + r, high, 0.0)
        extra += jnp.where(lane == 16 + r, weight - high, 0.0)
        gates += jnp.where(lane == r, weight, 0.0)
    token_out[:, width:] = extra.astype(low)
    gates_out[...] = gates


def shared_kernel(normed, cotangent, weights, part_out, back_out, grads_out):
    low = jnp.bfloat16
    gate = contract(normed[...], weights[:, :768], 1, 0)
    up = contract(normed[...], weights[:, 768:1536], 1, 0)
    sigmoid = 1.0 / (1.0 + jnp.exp(-gate))
    on = gate * sigmoid
    hidden = (on * up).astype(low)
    part_out[...] = contract(hidden, weights[:, 1536:], 1, 1)
    change = contract(cotangent[...], weights[:, 1536:], 1, 0)
    grad_gate = (change * up * (sigmoid * (1.0 + gate * (1.0 - sigmoid)))).astype(low)
    grad_up = (change * on).astype(low)
    width = normed.shape[1]
    back_out[:, :width] = contract(grad_gate, weights[:, :768], 1, 1) + contract(
        grad_up, weights[:, 768:1536], 1, 1
    )
    back_out[:, width:] = jnp.zeros((normed.shape[0], 128), jnp.float32)

    def grads(i, carry):
        part = pl.ds(pl.multiple_of(i * 256, 256), 256)
        rows = normed[:, part]
        grads_out[part, :768] = contract(rows, grad_gate, 0, 0).astype(low)
        grads_out[part, 768:1536] = contract(rows, grad_up, 0, 0).astype(low)
        grads_out[part, 1536:] = contract(cotangent[:, part], hidden, 0, 0).astype(low)
        return carry

    lax.fori_loop(0, grads_out.shape[0] // 256, grads, 0)


def attend_back_kernel(
    back,
    middle,
    gain,
    gates,
    routes,
    router,
    cotangent,
    wo_0,
    wo_1,
    wo_2,
    wo_3,
    probs,
    expanded,
    key_rope,
    query,
    keys,
    expand,
    query_w,
    cosine,
    sine_tab,
    normed,
    attended,
    middle_out,
    attention_out,
    gain_out,
    logits_out,
    own_out,
    query_sum_out,
    latent_sum_out,
    changes,
    ropes,
    query_out,
    back_out,
    keys_out,
    grads_out,
    held,
    near_in,
    far_in,
    ssem,
    rsem,
    pssem,
    prsem,
    latent,
    landed_one,
    landed_two,
    *scratch,
):
    low = jnp.bfloat16
    t, x, z, c = place()
    peers = plane_peers() + line_peers() + [(chip_at(x, z, c, k), t) for k in (1, 2, 3, 4)]
    call(peers)
    width = middle.shape[1]
    rows = middle.shape[0]
    lane = lanes((rows, 128))
    sums = back[:, width:].astype(jnp.float32)
    named = [routes[:, r : r + 1] for r in range(6)]
    weight = [gates[:, r : r + 1] for r in range(6)]
    change = [
        jnp.sum(jnp.where(lane == number + 64, sums, 0.0), 1, keepdims=True) for number in named
    ]
    inner = functools.reduce(jnp.add, [w * c for w, c in zip(weight, change)])
    logits = jnp.zeros((rows, 128), jnp.float32)
    for r in range(6):
        logits += jnp.where(lane == named[r] + 64, weight[r] * (change[r] - inner), 0.0)
    logits_low = logits.astype(low)
    logits_out[...] = logits_low
    grad_normed = back[:, :width].astype(jnp.float32) + contract(logits_low, router[...], 1, 1)
    values = middle[...]
    inverse = lax.rsqrt(jnp.mean(values * values, 1, keepdims=True) + epsilon)
    weighted = grad_normed * gain[...]
    aligned = jnp.mean(values * weighted, 1, keepdims=True)
    gain_out[...] = jnp.sum(grad_normed * values * inverse, 0, keepdims=True)
    grad_middle = (
        cotangent[...].astype(jnp.float32)
        + inverse * weighted
        - values * (inverse * inverse * inverse) * aligned
    )
    middle_out[...] = grad_middle
    grad_attn = grad_middle.astype(low)
    attention_out[...] = grad_attn
    first = jnp.zeros((rows, 128), jnp.float32)
    second = jnp.zeros((rows, 128), jnp.float32)
    for head, wo in enumerate((wo_0, wo_1, wo_2, wo_3)):
        start = 256 * head
        nope, value = slice(start, start + 128), slice(start + 128, start + 256)
        own = slice(128 * head, 128 * head + 128)
        grad_mixed = contract(grad_attn, wo[...], 1, 0).astype(low)
        share = probs[head]
        changes[:, value] = contract(share.astype(low), grad_mixed, 0, 0).astype(low)
        grad_share = contract(grad_mixed, expanded[:, value], 1, 1)
        grad_scores = share * (grad_share - jnp.sum(share * grad_share, 1, keepdims=True))
        grad_scores = grad_scores.astype(low)
        query_out[:, own] = (contract(grad_scores, expanded[:, nope], 1, 0) * SCALE).astype(low)
        both = contract(grad_scores, key_rope[...], 1, 0) * SCALE
        first += head_lanes(both[:, :128], head)
        second += head_lanes(both[:, 128:], head)
        changes[:, nope] = (contract(grad_scores, query[:, own], 0, 0) * SCALE).astype(low)
        from_first = contract(grad_scores, head_lanes(query[:, 512:640], head), 0, 0) * SCALE
        from_second = contract(grad_scores, head_lanes(query[:, 640:768], head), 0, 0) * SCALE
        if head == 0:
            ropes[:, :128] = from_first
            ropes[:, 128:] = from_second
        else:
            ropes[:, :128] += from_first
            ropes[:, 128:] += from_second
    cos, sin = cosine[...], sine_tab[...]
    query_out[:, 512:640] = (first * cos + second * sin).astype(low)
    query_out[:, 640:768] = (second * cos - first * sin).astype(low)
    back_out[...] = in_groups(contract(query_out[...], query_w[...], 1, 1)).astype(low)
    fold = fold_matrix()

    def key_rows(i, carry):
        part = pl.ds(pl.multiple_of(i * rows, rows), rows)
        compressed = contract(changes[part, :], expand[...], 1, 1)
        keys_out[i, :, :, :RANK] = in_groups(compressed).astype(low)
        rope = contract(ropes[part, :].astype(low), fold, 1, 1)
        keys_out[i, :, :, RANK:] = in_groups(rope).astype(low)
        return carry

    lax.fori_loop(0, keys.shape[0] // rows, key_rows, 0)
    hear(peers)
    back = send_back_steps(keys_out, latent, held, near_in, far_in, ssem, rsem, pssem, prsem)
    advance(back, 1)
    line_one = Line(back_out, landed_one, *scratch[:3])
    line_two = Line(latent, landed_two, *scratch[3:6])
    line_one.scatter()
    advance(back, 1)
    for j in range(4):
        grad_expand = contract(keys[:, :RANK], changes[:, 256 * j : 256 * j + 256], 0, 0)
        grads_out[:, 2 * j : 2 * j + 2, :, 1280:] = grad_expand.reshape(32, 2, 8, 256).astype(low)

    def grads(i, carry):
        part = pl.ds(pl.multiple_of(i * 256, 256), 256)
        some = pl.ds(i * 4, 4)
        of_query = contract(normed[:, part], query_out[...], 0, 0)
        grads_out[some, :, :, :768] = of_query.reshape(4, 8, 8, 768).astype(low)
        of_output = contract(attention_out[:, part], attended[...], 0, 0)
        grads_out[some, :, :, 768:1280] = of_output.reshape(4, 8, 8, 512).astype(low)
        return carry

    lax.fori_loop(0, width // 256, grads, 0)

    def emit(i, total):
        own_out[i] = total

    plane = plane_sum_steps(grads_out, emit, scratch[6:])
    advance(plane, 1)
    line_one.add()
    line_one.gather()
    advance(plane, 4)
    advance(back, 1)
    line_two.scatter()
    advance(plane, 8)
    line_two.add()
    line_two.gather()
    advance(plane, PLANE_STEPS - 13)
    line_one.finish()
    query_sum_out[...] = landed_one[...]
    line_two.finish()
    latent_sum_out[...] = landed_two[...]
    advance(back, 1)
    advance(plane, 1)


def finish_kernel(
    query_sum,
    latent_sum,
    latent,
    gain_latent,
    cosine,
    sine_tab,
    wl_0,
    wl_1,
    wl_2,
    wl_3,
    wl_4,
    hidden,
    gain,
    grad_middle,
    normed,
    normed_two,
    grad_logits,
    gain_two_grad,
    routed,
    shared,
    input_out,
    own_out,
    layer_out,
    changes,
    grads_out,
    landed,
    layer,
    *scratch,
):
    low = jnp.bfloat16
    peers = plane_peers() + line_peers()
    call(peers)
    grad_latent = latent_sum[:, :RANK].astype(jnp.float32)
    rope = latent_sum[:, RANK:].astype(jnp.float32)
    values = latent[...]
    inverse = lax.rsqrt(jnp.mean(values * values, 1, keepdims=True) + epsilon)
    weighted = grad_latent * gain_latent[...]
    aligned = jnp.mean(values * weighted, 1, keepdims=True)
    gain_latent_grad = jnp.sum(grad_latent * values * inverse, 0, keepdims=True)
    changes[:, :RANK] = (
        inverse * weighted - values * (inverse * inverse * inverse) * aligned
    ).astype(low)
    kept, crossed = turn_tables(cosine[...], sine_tab[...])
    changes[:, RANK:] = (rope * kept - exchange_halves(rope) * crossed).astype(low)
    grad_normed = query_sum[...].astype(jnp.float32)
    width = hidden.shape[1]
    for j, wl in enumerate((wl_0, wl_1, wl_2, wl_3, wl_4)):
        grad_normed += contract(changes[:, 128 * j : 128 * j + 128], wl[...], 1, 1)
    values = hidden[...].astype(jnp.float32)
    inverse = lax.rsqrt(jnp.mean(values * values, 1, keepdims=True) + epsilon)
    weighted = grad_normed * gain[...]
    aligned = jnp.mean(values * weighted, 1, keepdims=True)
    gain_grad = jnp.sum(grad_normed * values * inverse, 0, keepdims=True)
    input_out[...] = (
        grad_middle[...] + inverse * weighted - values * (inverse * inverse * inverse) * aligned
    ).astype(low)

    def grads(i, carry):
        part = pl.ds(pl.multiple_of(i * 256, 256), 256)
        some = pl.ds(i * 4, 4)
        rows = normed[:, part]
        of_latent = contract(rows, changes[:, :RANK], 0, 0)
        grads_out[some, :, :, :RANK] = of_latent.reshape(4, 8, 8, RANK).astype(low)
        mixed = contract(rows, changes[:, RANK:], 0, 0)
        mixed += contract(normed_two[:, part], grad_logits[...], 0, 0)
        grads_out[some, :, :, RANK : RANK + 128] = mixed.reshape(4, 8, 8, 128).astype(low)
        return carry

    lax.fori_loop(0, width // 256, grads, 0)
    grads_out[:, 1:, :, RANK + 128 :] = jnp.zeros((32, 7, 8, 128), low)
    line_number = lax.broadcasted_iota(jnp.int32, (8, 128), 0)
    gain_two = gain_two_grad[...]
    for e in range(32):
        block = jnp.zeros((8, 128), jnp.float32)
        for row, (values, size) in enumerate(
            ((gain_grad, 64), (gain_two, 64), (gain_latent_grad, 16))
        ):
            piece = values[:, size * e : size * e + size]
            piece = jnp.concatenate([piece, jnp.zeros((1, 128 - size), jnp.float32)], 1)
            block = jnp.where(line_number == row, piece, block)
        grads_out[e, 0, :, RANK + 128 :] = block.astype(low)
    layer[...] = (routed[...].astype(jnp.float32) + shared[...]).astype(low)
    hear(peers)
    line = Line(layer, landed, *scratch[:3])
    line.scatter()

    def emit(i, total):
        own_out[i] = total

    plane = plane_sum_steps(grads_out, emit, scratch[3:])
    advance(plane, 10)
    line.add()
    line.gather()
    advance(plane, PLANE_STEPS)
    line.finish()
    layer_out[...] = landed[...]


def unpack_kernel(
    own,
    last,
    ffn,
    middle,
    layer,
    grad_in,
    layer_out,
    grad_in_out,
    query_out,
    latent_out,
    router_out,
    output_out,
    gain_one_out,
    gain_two_out,
    gain_latent_out,
    expand_out,
    gate_out,
    up_out,
    down_out,
):
    layer_out[...] = (middle[...] + layer[...].astype(jnp.float32)).astype(layer_out.dtype)
    grad_in_out[...] = grad_in[...]
    for head in range(HEADS):
        query_out[:, 192 * head : 192 * head + 128] = own[:, 128 * head : 128 * head + 128]
        for half in (0, 1):
            to, start = 192 * head + 128 + 32 * half, 512 + 128 * half + 32 * head
            query_out[:, to : to + 32] = own[:, start : start + 32]
    latent_out[...] = last[:, :576]
    router_out[...] = last[:, 576:640]
    output_out[...] = own[:, 768:1280]
    gain_one_out[...] = last[0:1, 640:704]
    gain_two_out[...] = last[1:2, 640:704]
    gain_latent_out[...] = last[2:3, 640:656]
    for j in range(4):
        expand_out[:, 256 * j : 256 * j + 256] = own[16 * j : 16 * j + 16, 1280:1536]
    gate_out[...] = ffn[:, :704].astype(jnp.float32)
    up_out[...] = ffn[:, 768:1472].astype(jnp.float32)
    down_out[...] = ffn[:, 1536:2240].astype(jnp.float32)


def local_call(kernel, name, operands, out_shapes, scratch=()):
    arrays, specs = [], []
    for operand in operands:
        if isinstance(operand, tuple):
            array, block, index = operand
            specs.append(pl.BlockSpec(block, lambda i, index=index: index))
        else:
            array = operand
            zeros = (0,) * array.ndim
            specs.append(pl.BlockSpec(array.shape, lambda i, zeros=zeros: zeros))
        arrays.append(array)
    shapes = [jax.ShapeDtypeStruct(shape, dtype) for shape, dtype in out_shapes]
    return pl.pallas_call(
        kernel,
        grid=(1,),
        out_shape=shapes,
        in_specs=specs,
        out_specs=[
            pl.BlockSpec(shape.shape, lambda i, zeros=(0,) * len(shape.shape): zeros)
            for shape in shapes
        ],
        scratch_shapes=[pltpu.VMEM(shape, dtype) for shape, dtype in scratch],
        compiler_params=pltpu.CompilerParams(vmem_limit_bytes=60 * 2**20),
        name=name,
    )(*arrays)


def joint_call(kernel, collective_id, name, operands, out_shapes, scratch, moved):
    arrays, specs = [], []
    for operand in operands:
        if isinstance(operand, tuple):
            array, block, index = operand
        else:
            array, block, index = operand, operand.shape, (0,) * operand.ndim
        specs.append(
            pl.BlockSpec(block, lambda i, index=index: index, pipeline_mode=pl.Buffered(1))
        )
        arrays.append(array)
    return pl.pallas_call(
        kernel,
        grid=(1,),
        out_shape=[jax.ShapeDtypeStruct(shape, dtype) for shape, dtype in out_shapes],
        in_specs=specs,
        out_specs=[
            pl.BlockSpec(
                shape,
                lambda i, zeros=(0,) * len(shape): zeros,
                pipeline_mode=pl.Buffered(1),
            )
            for shape, _ in out_shapes
        ],
        scratch_shapes=scratch,
        compiler_params=pltpu.CompilerParams(
            collective_id=collective_id, has_side_effects=True, vmem_limit_bytes=60 * 2**20
        ),
        cost_estimate=pl.CostEstimate(flops=0, bytes_accessed=moved, transcendentals=0),
        name=name,
    )(*arrays)


def column_blocks(array, first, number):
    return [(array, (array.shape[0], 128), (0, first + j)) for j in range(number)]


def body(
    hidden_in,
    cotangent,
    segments,
    routes,
    attn_norm,
    w_query,
    w_latent,
    latent_norm,
    w_expand,
    w_output,
    ffn_norm,
    w_router,
    shared_gate,
    shared_up,
    shared_down,
    expert_gate,
    routed_expert_up,
    expert_down,
):
    tokens, model_width = hidden_in.shape
    devices = lax.axis_size("expert")
    own_index = lax.axis_index("expert")
    low = jnp.bfloat16
    full = jnp.float32
    shard = w_query.shape[0]

    attention_shard, ffn_shard = local_call(
        pack_kernel,
        "pack",
        (
            w_query,
            w_latent,
            attn_norm[None],
            ffn_norm[None],
            jnp.pad(latent_norm, (0, shard - latent_norm.shape[0]))[None],
            w_output.T,
            w_expand,
            shared_gate,
            w_router,
            shared_up,
            shared_down.T,
        ),
        (((shard, 2176), low), ((shard, 2304), low)),
    )
    ffn_all = lax.all_gather(ffn_shard, "expert", axis=0, tiled=True)
    grad_rows = lax.all_gather(cotangent, "expert", axis=0)
    attention_all = plane_gather(attention_shard, 1, "gather_attention")
    gains = attention_all.reshape(devices, shard, -1)[:, :8, 1344:1408].astype(full)
    gain_one = gains[:, 0].reshape(1, -1)
    gain_two = gains[:, 1].reshape(1, -1)
    gain_latent = gains[:, 2, : latent_norm.shape[0]].reshape(1, -1)
    expand_w = (
        attention_all[:, 1920:].reshape(devices, 4, 16, 256).swapaxes(1, 2).reshape(RANK, -1)
    )
    output_blocks = column_blocks(attention_all, 11, 4)
    latent_blocks = column_blocks(attention_all, 6, 5)
    router_block = column_blocks(ffn_all, 5, 1)[0]

    first_row = own_index * tokens
    row_index = first_row + jnp.arange(tokens, dtype=jnp.int32)
    own_segments = lax.dynamic_slice_in_dim(segments, first_row, tokens)
    doc_start = jnp.sum((segments[None, :] < own_segments[:, None]).astype(jnp.int32), 1)
    cosine, sine_tab = rope_tables(row_index - doc_start)
    cosine, sine_tab = jnp.tile(cosine, (1, 4)), jnp.tile(sine_tab, (1, 4))
    key_count = 9 * tokens
    normed, queries, latent, keys_all = joint_call(
        project_kernel,
        2,
        "project",
        (
            hidden_in,
            (attention_all, (model_width, 1408), (0, 0)),
            gain_one,
            gain_latent,
            cosine,
            sine_tab,
        ),
        (
            ((tokens, model_width), low),
            ((tokens, 768), low),
            ((tokens, RANK), full),
            ((9, tokens // 8, 8, 640), low),
        ),
        [
            pltpu.VMEM((tokens // 8, 8, 640), low),
            pltpu.VMEM((9, tokens // 8, 8, 640), low),
            pltpu.SemaphoreType.DMA,
            pltpu.SemaphoreType.DMA((4,)),
            pltpu.SemaphoreType.DMA((4,)),
            pltpu.SemaphoreType.DMA((4,)),
            pltpu.SemaphoreType.DMA((4,)),
        ],
        2**25,
    )
    keys_all = keys_all.reshape(key_count, 640)
    key_segments = lax.dynamic_slice_in_dim(
        jnp.pad(segments, (key_count - tokens, 0), constant_values=-1), first_row, key_count
    )
    attn_out, attended, probs, expanded, key_rope = joint_call(
        attend_kernel,
        3,
        "attend",
        (keys_all, expand_w, queries, own_segments[:, None], key_segments[None], *output_blocks),
        (
            ((tokens // 8, 8, model_width), low),
            ((tokens, HEADS * VH), low),
            ((HEADS, tokens, key_count), full),
            ((key_count, HEADS * (NOPE + VH)), low),
            ((key_count, 256), low),
        ),
        [pltpu.VMEM((tokens // 8, 8, model_width), low)] * 2
        + line_scratch(tokens // 8, model_width),
        2**25,
    )
    attn_out = attn_out.reshape(tokens, model_width)

    token_row, middle, gates = local_call(
        route_kernel,
        "route",
        (hidden_in, attn_out, gain_two, router_block, routes),
        (
            ((tokens, model_width + 128), low),
            ((tokens, model_width), full),
            ((tokens, 128), full),
        ),
    )
    normed_two = (token_row, (tokens, model_width), (0, 0))

    shared_part, shared_back, ffn_grads = local_call(
        shared_kernel,
        "shared",
        (normed_two, cotangent, ffn_all),
        (
            ((tokens, model_width), full),
            ((tokens, model_width + 128), full),
            (ffn_all.shape, low),
        ),
    )
    own_ffn = lax.psum_scatter(ffn_grads, "expert", scatter_dimension=0, tiled=True)
    token_row, _ = lax.optimization_barrier((token_row, ffn_grads))
    token_rows = plane_gather(token_row, 4, "gather_tokens")

    routed_part, back_part, out_egate, out_eup, out_edown = experts(
        token_rows.reshape(devices // 2, 2 * tokens, -1),
        grad_rows.reshape(devices // 2, 2 * tokens, -1),
        expert_gate.swapaxes(1, 2),
        routed_expert_up.swapaxes(1, 2),
        expert_down,
    )
    out_egate, out_eup = out_egate.swapaxes(1, 2), out_eup.swapaxes(1, 2)
    routed_part, own_ffn = lax.optimization_barrier((routed_part, own_ffn))
    routed_own = lax.psum_scatter(
        routed_part.reshape(-1, model_width), "expert", scatter_dimension=0, tiled=True
    )
    back_all = sum_tokens(back_part.reshape(devices * tokens, -1), shared_back, 5)

    (
        grad_middle,
        grad_attn,
        grad_gain_two,
        grad_logits,
        own,
        query_sum,
        latent_sum,
    ) = joint_call(
        attend_back_kernel,
        7,
        "attend_back",
        (
            back_all,
            middle,
            gain_two,
            gates,
            routes,
            router_block,
            cotangent,
            *output_blocks,
            probs,
            expanded,
            key_rope,
            queries,
            keys_all,
            expand_w,
            (attention_all, (model_width, 768), (0, 0)),
            cosine,
            sine_tab,
            normed,
            attended,
        ),
        (
            ((tokens, model_width), full),
            ((tokens, model_width), low),
            ((1, model_width), full),
            ((tokens, 128), low),
            ((shard // 8, 8, 1536), full),
            ((tokens // 8, 8, model_width), low),
            ((tokens // 8, 8, 640), low),
        ),
        [
            pltpu.VMEM((key_count, HEADS * (NOPE + VH)), low),
            pltpu.VMEM((key_count, 256), full),
            pltpu.VMEM((tokens, 768), low),
            pltpu.VMEM((tokens // 8, 8, model_width), low),
            pltpu.VMEM((9, tokens // 8, 8, 640), low),
            pltpu.VMEM((devices, shard // 8, 8, 1536), low),
            pltpu.VMEM((5, tokens // 8, 8, 640), low),
            pltpu.VMEM((4, tokens // 8, 8, 640), low),
            pltpu.VMEM((4, tokens // 8, 8, 640), low),
            pltpu.SemaphoreType.DMA((4,)),
            pltpu.SemaphoreType.DMA((4,)),
            pltpu.SemaphoreType.DMA((4,)),
            pltpu.SemaphoreType.DMA((4,)),
            pltpu.VMEM((tokens // 8, 8, 640), low),
            pltpu.VMEM((tokens // 8, 8, model_width), low),
            pltpu.VMEM((tokens // 8, 8, 640), low),
        ]
        + line_scratch(tokens // 8, model_width)
        + line_scratch(tokens // 8, 640)
        + plane_scratch(shard // 8, 1536),
        2**26,
    )
    own = own.reshape(shard, 1536)
    query_sum = query_sum.reshape(tokens, model_width)
    latent_sum = latent_sum.reshape(tokens, 640)
    grad_input, own_last, layer_sum = joint_call(
        finish_kernel,
        9,
        "finish",
        (
            query_sum,
            latent_sum,
            latent,
            gain_latent,
            cosine,
            sine_tab,
            *latent_blocks,
            hidden_in,
            gain_one,
            grad_middle,
            normed,
            normed_two,
            grad_logits,
            grad_gain_two,
            by_group(routed_own),
            by_group(shared_part),
        ),
        (
            ((tokens, model_width), low),
            ((shard // 8, 8, 768), full),
            ((tokens // 8, 8, model_width), low),
        ),
        [
            pltpu.VMEM((tokens, 640), low),
            pltpu.VMEM((devices, shard // 8, 8, 768), low),
            pltpu.VMEM((tokens // 8, 8, model_width), low),
            pltpu.VMEM((tokens // 8, 8, model_width), low),
        ]
        + line_scratch(tokens // 8, model_width)
        + plane_scratch(shard // 8, 768),
        2**25,
    )
    own_last = own_last.reshape(shard, 768)
    layer_sum = layer_sum.reshape(tokens, model_width)
    (
        layer_out,
        grad_input,
        out_query,
        out_latent,
        out_router,
        out_output,
        out_gain_one,
        out_gain_two,
        out_gain_latent,
        out_expand,
        out_sgate,
        out_sup,
        out_sdown,
    ) = local_call(
        unpack_kernel,
        "unpack",
        (own, own_last, own_ffn, middle, layer_sum, grad_input),
        (
            ((tokens, model_width), low),
            ((tokens, model_width), low),
            (w_query.shape, full),
            (w_latent.shape, full),
            (w_router.shape, full),
            ((shard, w_output.shape[0]), full),
            ((1, shard), full),
            ((1, shard), full),
            ((1, latent_norm.shape[0]), full),
            (w_expand.shape, full),
            (shared_gate.shape, full),
            (shared_up.shape, full),
            ((shard, shared_down.shape[0]), full),
        ),
    )
    return (
        layer_out,
        grad_input,
        out_gain_one.reshape(-1),
        out_query,
        out_latent,
        out_gain_latent.reshape(-1),
        out_expand,
        out_output.T,
        out_gain_two.reshape(-1),
        out_router,
        out_sgate,
        out_sup,
        out_sdown.T,
        out_egate,
        out_eup,
        out_edown,
    )


def solution(mesh):
    in_specs = (
        P("expert", None),
        P("expert", None),
        P(),
        P("expert", None),
        P("expert"),
        P("expert", "tensor"),
        P("expert", None),
        P("expert"),
        P("expert", "tensor"),
        P("tensor", "expert"),
        P("expert"),
        P("expert", None),
        P("expert", "tensor"),
        P("expert", "tensor"),
        P("tensor", "expert"),
        P("expert", None, "tensor"),
        P("expert", None, "tensor"),
        P("expert", "tensor", None),
    )
    out_specs = (
        P("expert", None),
        P("expert", None),
        P("expert"),
        P("expert", "tensor"),
        P("expert", None),
        P("expert"),
        P("expert", "tensor"),
        P("tensor", "expert"),
        P("expert"),
        P("expert", None),
        P("expert", "tensor"),
        P("expert", "tensor"),
        P("tensor", "expert"),
        P("expert", None, "tensor"),
        P("expert", None, "tensor"),
        P("expert", "tensor", None),
    )
    return jax.shard_map(body, mesh=mesh, in_specs=in_specs, out_specs=out_specs, check_vma=False)
```

```python
import functools

import jax
import jax.numpy as jnp
from jax import lax
from jax.experimental import pallas as pl
from jax.experimental.pallas import tpu as pltpu
from jax.sharding import PartitionSpec as P

NOPE = 128
ROPE = 64
VH = 128
RANK = 512
WINDOW = 1024


epsilon = 1e-06
masked_score = -1e30
rope_base = 10000.0


MESH = pl.DeviceIdType.MESH
HBM = pl.BlockSpec(memory_space=pltpu.HBM)


def place():
    e = lax.axis_index("expert")
    return lax.axis_index("tensor"), e // 8, lax.rem(e // 2, 4), lax.rem(e, 2)


def at(x, z, c):
    return (x * 4 + z) * 2 + c


def wrap(v):
    return lax.rem(v + 4, 4)


def greet(peers):
    call(peers)
    hear(peers)


def call(peers):
    barrier = pltpu.get_barrier_semaphore()
    for peer in peers:
        pl.semaphore_signal(barrier, inc=1, device_id=peer, device_id_type=MESH)


def hear(peers):
    pl.semaphore_wait(pltpu.get_barrier_semaphore(), len(peers))


def plane_gather_kernel(src, out, ssem, rsem, dssem, drsem, lsem):
    t, x, z, c = place()
    rows = src.shape[0]
    half, quarter = rows // 2, rows // 4
    sibling = (at(x, z, 1 - c), t)
    along_x = [(at(wrap(x - 1), z, c), t), (at(wrap(x + 1), z, c), t)]
    along_z = [(at(x, wrap(z - 1), c), t), (at(x, wrap(z + 1), c), t)]
    greet([sibling] + along_x + along_z)
    own = pltpu.make_async_copy(src, out.at[at(x, z, c)], lsem)
    own.start()
    sent = []

    def piece(h, j1, j2, part=None):
        if h == 0:
            index = at(wrap(x + j2), wrap(z + j1), c)
        else:
            index = at(wrap(x + j1), wrap(z + j2), c)
        if part is None:
            return index, pl.ds(h * half, half)
        return index, pl.ds(h * half + part * quarter, quarter)

    def send(h, slot, which, device, first):
        index, rows_of = which
        return pltpu.make_async_remote_copy(
            src_ref=src.at[rows_of] if first else out.at[index, rows_of],
            dst_ref=out.at[index, rows_of],
            send_sem=ssem.at[h, slot],
            recv_sem=rsem.at[h, slot],
            device_id=device,
            device_id_type=MESH,
        )

    def across(h, j1, j2):
        index, rows_of = piece(h, j1, j2)
        slot = (h * 4 + j1 % 4) * 4 + j2 % 4
        return pltpu.make_async_remote_copy(
            src_ref=src.at[rows_of] if j1 == 0 and j2 == 0 else out.at[index, rows_of],
            dst_ref=out.at[index, rows_of],
            send_sem=dssem.at[slot],
            recv_sem=drsem.at[slot],
            device_id=sibling,
            device_id_type=MESH,
        )

    def ring(h, stage):
        return along_z if (h == 0) == (stage == 1) else along_x

    def stage_one(h, kind):
        left, right = ring(h, 1)
        if kind == 0:
            return send(h, 0, piece(h, 0, 0), right, True)
        if kind == 1:
            return send(h, 1, piece(h, 0, 0), left, True)
        if kind == 2:
            return send(h, 2, piece(h, -1, 0, 0), right, False)
        return send(h, 3, piece(h, 1, 0, 1), left, False)

    def stage_two(h, j1, kind):
        left, right = ring(h, 2)
        slot = 4 + 4 * (j1 % 4) + kind
        if kind == 0:
            return send(h, slot, piece(h, j1, 0), right, j1 == 0)
        if kind == 1:
            return send(h, slot, piece(h, j1, 0), left, j1 == 0)
        if kind == 2:
            return send(h, slot, piece(h, j1, -1, 0), right, False)
        return send(h, slot, piece(h, j1, 1, 1), left, False)

    def go(copy):
        copy.start()
        sent.append(copy)

    for h in (0, 1):
        go(stage_one(h, 0))
        go(stage_one(h, 1))
        go(stage_two(h, 0, 0))
        go(stage_two(h, 0, 1))
        go(across(h, 0, 0))
    for h in (0, 1):
        for kind, j in ((0, -1), (1, 1)):
            stage_one(h, kind).wait_recv()
            go(stage_one(h, 2 + kind))
            go(stage_two(h, j, 0))
            go(stage_two(h, j, 1))
            go(across(h, j, 0))
    for h in (0, 1):
        for kind, j in ((0, -1), (1, 1)):
            stage_two(h, 0, kind).wait_recv()
            go(stage_two(h, 0, 2 + kind))
            go(across(h, 0, j))
    for h in (0, 1):
        stage_one(h, 2).wait_recv()
        stage_one(h, 3).wait_recv()
        go(stage_two(h, 2, 0))
        go(stage_two(h, 2, 1))
        go(across(h, 2, 0))
    for j1 in (-1, 1, 2):
        for h in (0, 1):
            for kind, j in ((0, -1), (1, 1)):
                stage_two(h, j1, kind).wait_recv()
                go(stage_two(h, j1, 2 + kind))
                go(across(h, j1, j))
    for j1 in (0, -1, 1, 2):
        for h in (0, 1):
            stage_two(h, j1, 2).wait_recv()
            stage_two(h, j1, 3).wait_recv()
            go(across(h, j1, 2))
    for h in (0, 1):
        for j1 in (0, -1, 1, 2):
            for j2 in (0, -1, 1, 2):
                across(h, j1, j2).wait_recv()
    for copy in sent:
        copy.wait_send()
    own.wait()


def plane_gather(rows, collective_id, name):
    grouped = rows.reshape(rows.shape[0] // 8, 8, rows.shape[1])
    gathered = pl.pallas_call(
        plane_gather_kernel,
        out_shape=jax.ShapeDtypeStruct((32, *grouped.shape), rows.dtype),
        in_specs=[HBM],
        out_specs=HBM,
        scratch_shapes=[
            pltpu.SemaphoreType.DMA((2, 20)),
            pltpu.SemaphoreType.DMA((2, 20)),
            pltpu.SemaphoreType.DMA((32,)),
            pltpu.SemaphoreType.DMA((32,)),
            pltpu.SemaphoreType.DMA,
        ],
        compiler_params=pltpu.CompilerParams(
            collective_id=collective_id, has_side_effects=True, vmem_limit_bytes=62 * 2**20
        ),
        cost_estimate=pl.CostEstimate(
            flops=0, bytes_accessed=64 * rows.size * rows.dtype.itemsize, transcendentals=0
        ),
        name=name,
    )(grouped)
    return gathered.reshape(32 * rows.shape[0], rows.shape[1])


def line_peers():
    e, t = lax.axis_index("expert"), lax.axis_index("tensor")
    return [(e, lax.rem(t + k, 4)) for k in (1, 2, 3)]


class Line:
    def __init__(self, src, out, taken, ssem, rsem):
        t = lax.axis_index("tensor")
        self.src, self.out, self.taken, self.ssem, self.rsem = src, out, taken, ssem, rsem
        self.share, self.t = src.shape[0] // 4, t
        self.others = line_peers()

    def share_out(self, k):
        device = self.others[k - 1]
        return pltpu.make_async_remote_copy(
            src_ref=self.src.at[pl.ds(device[1] * self.share, self.share)],
            dst_ref=self.taken.at[k - 1],
            send_sem=self.ssem.at[0, k - 1],
            recv_sem=self.rsem.at[0, k - 1],
            device_id=device,
            device_id_type=MESH,
        )

    def pass_on(self, k):
        rows = pl.ds(self.t * self.share, self.share)
        return pltpu.make_async_remote_copy(
            src_ref=self.out.at[rows],
            dst_ref=self.out.at[rows],
            send_sem=self.ssem.at[1, k - 1],
            recv_sem=self.rsem.at[1, k - 1],
            device_id=self.others[k - 1],
            device_id_type=MESH,
        )

    def scatter(self):
        for k in (2, 1, 3):
            self.share_out(k).start()

    def add(self):
        for k in (2, 1, 3):
            self.share_out(k).wait_recv()

        def step(i, carry):
            total = self.src[self.t * self.share + i].astype(jnp.float32)
            for k in range(3):
                total = total + self.taken[k, i].astype(jnp.float32)
            self.out[self.t * self.share + i] = total.astype(self.out.dtype)
            return carry

        lax.fori_loop(0, self.share, step, 0)

    def gather(self):
        for k in (2, 1, 3):
            self.pass_on(k).start()

    def finish(self):
        for k in (2, 1, 3):
            self.pass_on(k).wait_recv()
        for k in (2, 1, 3):
            self.share_out(k).wait_send()
            self.pass_on(k).wait_send()


def line_sum_kernel(src, out, taken, ssem, rsem):
    line = Line(src, out, taken, ssem, rsem)
    greet(line.others)
    line.scatter()
    line.add()
    line.gather()
    line.finish()


PLANE_STEPS = 1 + 8 + 16 + 2 + 4 + 2


def plane_sum_steps(source, emit, scratch):
    mine, peer, one, two, last_one, last_two, lsem, pssem, prsem, ssem, rsem = scratch
    t, x, z, c = place()
    groups = mine.shape[2]
    half, quarter = groups // 2, groups // 4
    sibling = (at(x, z, 1 - c), t)
    along_x = [(at(wrap(x - 1), z, c), t), (at(wrap(x + 1), z, c), t)]
    along_z = [(at(x, wrap(z - 1), c), t), (at(x, wrap(z + 1), c), t)]
    order = (2, 1, 3, 0)
    sent = []

    def view(ref, h, a, b):
        if h == 0:
            return ref.at[a, b, pl.ds(0, half)]
        return ref.at[b, a, pl.ds(half, half)]

    def target(dx, dz, core):
        return at(wrap(x + dx), wrap(z + dz), core)

    def outward(dx, dz):
        return pltpu.make_async_remote_copy(
            src_ref=source.at[target(dx, dz, 1 - c)],
            dst_ref=peer.at[dx, dz],
            send_sem=pssem.at[dx, dz],
            recv_sem=prsem.at[dx, dz],
            device_id=sibling,
            device_id_type=MESH,
        )

    def inward(dx, dz):
        return pltpu.make_async_copy(
            source.at[target(dx, dz, c)], mine.at[dx, dz], lsem.at[dx, dz]
        )

    def hop(h, slot, src, dst, device):
        return pltpu.make_async_remote_copy(
            src_ref=src,
            dst_ref=dst,
            send_sem=ssem.at[h, slot],
            recv_sem=rsem.at[h, slot],
            device_id=device,
            device_id_type=MESH,
        )

    def ring(h, stage):
        return along_x if (h == 0) == (stage == 1) else along_z

    def first(h, b, side):
        return hop(
            h,
            4 * b + side,
            view(mine, h, 2, b).at[pl.ds(side * quarter, quarter)],
            one.at[h, b, side],
            ring(h, 1)[1 - side],
        )

    def second(h, b, side):
        return hop(
            h, 4 * b + 2 + side, view(mine, h, 1 + 2 * side, b), two.at[h, b, side], ring(h, 1)[1 - side]
        )

    def third(h, side):
        return hop(
            h,
            16 + side,
            view(mine, h, 0, 2).at[pl.ds(side * quarter, quarter)],
            last_one.at[h, side],
            ring(h, 2)[1 - side],
        )

    def fourth(h, side):
        return hop(
            h, 18 + side, view(mine, h, 0, 1 + 2 * side), last_two.at[h, side], ring(h, 2)[1 - side]
        )

    def go(copy):
        copy.start()
        sent.append(copy)

    def accumulate(into, sources_of, number):
        def step(i, carry):
            total = into[i].astype(jnp.float32)
            for source in sources_of:
                total = total + source[i].astype(jnp.float32)
            into[i] = total.astype(into.dtype)
            return carry

        lax.fori_loop(0, number, step, 0)

    spots = [(2, 2), (2, 1), (1, 2), (2, 3), (3, 2), (2, 0), (0, 2), (1, 1)]
    spots += [(1, 3), (3, 1), (3, 3), (1, 0), (0, 1), (3, 0), (0, 3), (0, 0)]
    for spot in spots:
        inward(*spot).start()
        go(outward(*spot))
    merged = set()

    yield

    def merge(h, a, b):
        spot = (a, b) if h == 0 else (b, a)
        if spot in merged:
            return
        merged.add(spot)
        inward(*spot).wait()
        outward(*spot).wait_recv()
        accumulate(mine.at[spot[0], spot[1]], [peer.at[spot[0], spot[1]]], groups)

    for b in order:
        for h in (0, 1):
            merge(h, 2, b)
            for side in (0, 1):
                go(first(h, b, side))
            yield
    for side in (0, 1):
        for b in order:
            for h in (0, 1):
                a = 1 + 2 * side
                merge(h, a, b)
                first(h, b, side).wait_recv()
                accumulate(
                    view(mine, h, a, b).at[pl.ds(side * quarter, quarter)],
                    [one.at[h, b, side]],
                    quarter,
                )
                go(second(h, b, side))
                yield

    def gathered_here(h, b):
        merge(h, 0, b)
        for side in (0, 1):
            second(h, b, side).wait_recv()
        accumulate(view(mine, h, 0, b), [two.at[h, b, 0], two.at[h, b, 1]], half)

    for h in (0, 1):
        gathered_here(h, 2)
        for side in (0, 1):
            go(third(h, side))
        yield
    for side in (0, 1):
        b = 1 + 2 * side
        for h in (0, 1):
            gathered_here(h, b)
            third(h, side).wait_recv()
            accumulate(
                view(mine, h, 0, b).at[pl.ds(side * quarter, quarter)],
                [last_one.at[h, side]],
                quarter,
            )
            go(fourth(h, side))
            yield
    for h in (0, 1):
        gathered_here(h, 0)
        for side in (0, 1):
            fourth(h, side).wait_recv()

        def finish(i, carry, h=h):
            total = mine[0, 0, h * half + i].astype(jnp.float32)
            for side in (0, 1):
                total = total + last_two[h, side, i].astype(jnp.float32)
            emit(h * half + i, total)
            return carry

        lax.fori_loop(0, half, finish, 0)
        yield
    for copy in sent:
        copy.wait_send()


def plane_peers():
    t, x, z, c = place()
    return [
        (at(x, z, 1 - c), t),
        (at(wrap(x - 1), z, c), t),
        (at(wrap(x + 1), z, c), t),
        (at(x, wrap(z - 1), c), t),
        (at(x, wrap(z + 1), c), t),
    ]


def plane_scratch(groups, width):
    half, quarter = groups // 2, groups // 4
    low = jnp.bfloat16
    return [
        pltpu.VMEM((4, 4, groups, 8, width), low),
        pltpu.VMEM((4, 4, groups, 8, width), low),
        pltpu.VMEM((2, 4, 2, quarter, 8, width), low),
        pltpu.VMEM((2, 4, 2, half, 8, width), low),
        pltpu.VMEM((2, 2, quarter, 8, width), low),
        pltpu.VMEM((2, 2, half, 8, width), low),
        pltpu.SemaphoreType.DMA((4, 4)),
        pltpu.SemaphoreType.DMA((4, 4)),
        pltpu.SemaphoreType.DMA((4, 4)),
        pltpu.SemaphoreType.DMA((2, 20)),
        pltpu.SemaphoreType.DMA((2, 20)),
    ]


def line_scratch(groups, width):
    return [
        pltpu.VMEM((3, groups // 4, 8, width), jnp.bfloat16),
        pltpu.SemaphoreType.DMA((2, 3)),
        pltpu.SemaphoreType.DMA((2, 3)),
    ]


def advance(task, number):
    for _ in range(number):
        next(task, None)


def by_expert(part, groups):
    return part.reshape(32, groups, 8, part.shape[1])


def by_group(part):
    return part.reshape(part.shape[0] // 8, 8, part.shape[1])


def communicate(kernel, collective_id, name, operands, where, out_shapes, scratch, moved):
    vmem = pl.BlockSpec(memory_space=pltpu.VMEM)
    shapes = [jax.ShapeDtypeStruct(shape, dtype) for shape, dtype in out_shapes]
    return pl.pallas_call(
        kernel,
        out_shape=shapes,
        in_specs=[vmem if inside else HBM for inside in where],
        out_specs=[vmem] * len(shapes),
        scratch_shapes=scratch,
        compiler_params=pltpu.CompilerParams(
            collective_id=collective_id, has_side_effects=True, vmem_limit_bytes=60 * 2**20
        ),
        cost_estimate=pl.CostEstimate(flops=0, bytes_accessed=moved, transcendentals=0),
        name=name,
    )(*operands)


def sum_tokens_kernel(source, shared, out, held, taken, line_ssem, line_rsem, *scratch):
    half = out.shape[0] // 2

    def emit(i, total):
        held[i] = (total + shared[i]).astype(held.dtype)

    greet(plane_peers() + line_peers())
    plane = plane_sum_steps(source, emit, scratch)
    lines = []
    for h in (0, 1):
        rows = pl.ds(h * half, half)
        lines.append(
            Line(held.at[rows], out.at[rows], taken.at[h], line_ssem.at[h], line_rsem.at[h])
        )
    advance(plane, PLANE_STEPS - 1)
    lines[0].scatter()
    advance(plane, 1)
    lines[1].scatter()
    for line in lines:
        line.add()
        line.gather()
    for line in lines:
        line.finish()
    advance(plane, 1)


def sum_tokens(part, shared, collective_id):
    groups, width = part.shape[0] // 256, part.shape[1]
    (summed,) = communicate(
        sum_tokens_kernel,
        collective_id,
        "sum_tokens",
        (by_expert(part, groups), by_group(shared)),
        (False, True),
        (((groups, 8, width), jnp.bfloat16),),
        [
            pltpu.VMEM((groups, 8, width), jnp.bfloat16),
            pltpu.VMEM((2, 3, groups // 8, 8, width), jnp.bfloat16),
            pltpu.SemaphoreType.DMA((2, 2, 3)),
            pltpu.SemaphoreType.DMA((2, 2, 3)),
        ]
        + plane_scratch(groups, width),
        16 * part.size,
    )
    return summed.reshape(8 * groups, width)


def reach_back_peers():
    t, x, z, c = place()
    along = [(at(x, wrap(z - r), c), t) for r in (1, 2, 3)]
    return [(at(x, z, 1 - c), t), (at(wrap(x - 1), z, c), t)] + along


def reach_back_run(src, out, lsem, ssem, rsem, pssem, prsem):
    t, x, z, c = place()
    sibling = (at(x, z, 1 - c), t)
    own = pltpu.make_async_copy(src, out.at[8], lsem)
    own.start()

    def onward():
        return pltpu.make_async_remote_copy(
            src_ref=src,
            dst_ref=out.at[0],
            send_sem=ssem.at[3],
            recv_sem=rsem.at[3],
            device_id=(at(wrap(x + 1), z, c), t),
            device_id_type=MESH,
        )

    def along(r, source):
        return pltpu.make_async_remote_copy(
            src_ref=source,
            dst_ref=out.at[8 - 2 * r],
            send_sem=ssem.at[r - 1],
            recv_sem=rsem.at[r - 1],
            device_id=(at(x, wrap(z + r), c), t),
            device_id_type=MESH,
        )

    def near(i):
        return pltpu.make_async_remote_copy(
            src_ref=out.at[8 - 2 * (i + c)],
            dst_ref=out.at[7 - 2 * i],
            send_sem=pssem.at[i],
            recv_sem=prsem.at[i],
            device_id=sibling,
            device_id_type=MESH,
        )

    onward().start()
    for r in (2, 1, 3):

        @pl.when(z + r < 4)
        def _(r=r):
            along(r, src).start()

    own.wait()
    onward().wait_recv()
    for r in (2, 3, 1):

        @pl.when(z + r >= 4)
        def _(r=r):
            along(r, out.at[0]).start()

    for r in (1, 3, 2):
        along(r, src).wait_recv()
    for i in range(4):
        near(i).start()
    for i in range(4):
        near(i).wait()
    onward().wait_send()
    for r in (1, 2, 3):
        along(r, src).wait_send()


def chip_at(x, z, c, distance):
    place_on = lax.rem(x * 4 + z + 16 + distance, 16)
    return place_on * 2 + c


def send_back_steps(src, out, held, near_in, far_in, ssem, rsem, pssem, prsem):
    t, x, z, c = place()
    groups = out.shape[0]
    sibling = (at(x, z, 1 - c), t)
    behind = [(chip_at(x, z, c, -k), t) for k in (1, 2, 3, 4)]

    def near(i):
        return pltpu.make_async_remote_copy(
            src_ref=src.at[7 - 2 * i],
            dst_ref=near_in.at[i],
            send_sem=pssem.at[i],
            recv_sem=prsem.at[i],
            device_id=sibling,
            device_id_type=MESH,
        )

    def far(k):
        return pltpu.make_async_remote_copy(
            src_ref=held.at[k],
            dst_ref=far_in.at[k - 1],
            send_sem=ssem.at[k - 1],
            recv_sem=rsem.at[k - 1],
            device_id=behind[k - 1],
            device_id_type=MESH,
        )

    for i in (3, 2, 1, 0):
        near(i).start()
    yield
    for i in (3, 2, 1, 0):
        near(i).wait_recv()
    for k in (4, 3, 2, 1, 0):

        def step(i, carry, k=k):
            total = src[8 - 2 * k, i].astype(jnp.float32)
            other = near_in[jnp.clip(k - c, 0, 3), i].astype(jnp.float32)
            covered = jnp.logical_and(k - c >= 0, k - c <= 3)
            total = total + jnp.where(covered, other, jnp.zeros_like(other))
            held[k, i] = total.astype(held.dtype)
            return carry

        lax.fori_loop(0, groups, step, 0)
        if k > 0:
            far(k).start()
    yield
    for k in (1, 2, 3, 4):
        far(k).wait_recv()

    def last(i, carry):
        total = held[0, i].astype(jnp.float32)
        for k in range(4):
            total = total + far_in[k, i].astype(jnp.float32)
        out[i] = total.astype(out.dtype)
        return carry

    lax.fori_loop(0, groups, last, 0)
    yield
    for k in (1, 2, 3, 4):
        far(k).wait_send()
    for i in range(4):
        near(i).wait_send()


def contract(left_side, right_side, left_dim, right_dim):
    return lax.dot_general(
        left_side,
        right_side,
        (((left_dim,), (right_dim,)), ((), ())),
        preferred_element_type=jnp.float32,
    )


def experts_kernel(
    token_rows,
    grad_rows,
    gate_in,
    up_in,
    down_in,
    routed_out,
    back_out,
    gate_out,
    up_out,
    down_out,
    ranks,
    rows_x,
    rows_g,
    weights,
    dots,
    staged,
    gate_up,
    down,
    hidden,
    grads,
    sums_one,
    sums_two,
    in_sem,
    out_sem,
):
    step = pl.program_id(0)
    low = jnp.bfloat16
    units = down_in.shape[1]
    wide = down.shape[0]
    pair_slots = 48
    width = rows_x.shape[2]
    blocks = ranks.shape[0]
    count = rows_x.shape[1]
    part = 256

    def load(k, expert):
        source = (gate_in, up_in, down_in)[k].at[expert]
        return pltpu.make_async_copy(source, staged.at[k], in_sem.at[k])

    def store(k, expert):
        if k == 2:
            source = sums_two.at[pl.ds(0, units)]
        else:
            source = sums_one.at[pl.ds(k * wide, units)]
        target = (gate_out, up_out, down_out)[k].at[expert]
        return pltpu.make_async_copy(source, target, out_sem.at[k])

    def picks(block):
        row = lax.broadcasted_iota(jnp.int32, (pair_slots, 256), 0)
        column = lax.broadcasted_iota(jnp.int32, (pair_slots, 256), 1)
        second = row >= 24
        slot = jnp.where(second, row - 24, row).astype(jnp.float32)
        inside = second == (column >= 128)
        found = []
        for expert in (0, 1):
            rank = ranks[block, expert : expert + 1, :]
            found.append(jnp.logical_and(rank == slot, inside))
        return found

    @pl.when(step == 0)
    def _():
        for k in range(3):
            load(k, 0).start()

    def rank_slots(block):
        square = (128, 128)
        same = lax.broadcasted_iota(jnp.int32, square, 0) == lax.broadcasted_iota(
            jnp.int32, square, 1
        )
        turned = contract(
            jnp.where(same, 1.0, 0.0).astype(low), token_rows[0, :, width:], 1, 1
        )
        first = lax.broadcasted_iota(jnp.int32, (256, 256), 0)
        second = lax.broadcasted_iota(jnp.int32, (256, 256), 1)
        ahead = jnp.logical_and(first < second, (first >= 128) == (second >= 128))
        line = lax.broadcasted_iota(jnp.int32, (8, 256), 0)
        named = jnp.zeros((8, 256), jnp.float32)
        shares = jnp.zeros((8, 256), jnp.float32)
        for expert in (0, 1):
            number = (lax.axis_index("expert") * 2 + expert).astype(jnp.float32)
            match = turned[0:8] == number
            present = jnp.sum(jnp.where(match, 1.0, 0.0), 0, keepdims=True)
            share = jnp.sum(jnp.where(match, turned[8:16] + turned[16:24], 0.0), 0, keepdims=True)
            named = named + jnp.where(line == expert, present, 0.0)
            shares = shares + jnp.where(line == 2 + expert, share, 0.0)
        rank = contract(named.astype(low), jnp.where(ahead, 1.0, 0.0).astype(low), 1, 0)
        rank = jnp.where(named > 0.0, rank, -1.0)
        ranks[block] = jnp.where(line < 2, rank, shares)

    @pl.when(step < blocks)
    def _():
        rank_slots(step)
        found = picks(step)
        pick = jnp.concatenate([jnp.where(f, 1.0, 0.0) for f in found], 0).astype(low)
        from_x = contract(pick, token_rows[0, :, :width], 1, 0).astype(low)
        from_g = contract(pick, grad_rows[0], 1, 0).astype(low)
        here = pl.ds(pl.multiple_of(step * pair_slots, pair_slots), pair_slots)
        for expert in (0, 1):
            lines = slice(expert * pair_slots, (expert + 1) * pair_slots)
            rows_x[expert, here, :] = from_x[lines]
            rows_g[expert, here, :] = from_g[lines]
            shares = ranks[step, 2 + expert : 3 + expert, :]
            weight = jnp.sum(jnp.where(found[expert], shares, 0.0), 1, keepdims=True)
            weights[expert, here, :] = jnp.broadcast_to(weight, (pair_slots, 128))

    for expert in (0, 1):

        @pl.when(step == blocks + expert)
        def _(expert=expert):
            for k in range(3):
                load(k, expert).wait()
            nothing = jnp.zeros((wide - units, width), low)
            gate_up[pl.ds(units, wide - units), :] = nothing
            gate_up[pl.ds(wide + units, wide - units), :] = nothing
            down[pl.ds(units, wide - units), :] = nothing

            def cast(i, carry):
                rows = pl.ds(pl.multiple_of(i * 32, 32), 32)
                gate_up[rows, :] = staged[0, rows, :].astype(low)
                gate_up[pl.ds(pl.multiple_of(wide + i * 32, 32), 32), :] = staged[
                    1, rows, :
                ].astype(low)
                down[rows, :] = staged[2, rows, :].astype(low)
                return carry

            lax.fori_loop(0, units // 32, cast, 0)
            if expert == 0:
                for k in range(3):
                    load(k, 1).start()

            def middle(i, carry):
                rows = pl.ds(pl.multiple_of(i * part, part), part)
                before = contract(rows_x[expert, rows, :], gate_up[...], 1, 1)
                plain = contract(rows_g[expert, rows, :], down[...], 1, 1)
                weight = weights[expert, rows, :][:, 0:1]
                gate, up = before[:, :wide], before[:, wide:]
                sigmoid = 1.0 / (1.0 + jnp.exp(-gate))
                on = gate * sigmoid
                value = on * up
                hidden[rows, :] = (weight * value).astype(low)
                dot = jnp.sum(plain * value, 1, keepdims=True)
                mine = 64 + lax.axis_index("expert") * 2 + expert
                lane = lax.broadcasted_iota(jnp.int32, (part, 128), 1)
                dots[expert, rows, :] = jnp.where(lane == mine, dot, 0.0).astype(low)
                change = weight * plain
                grads[rows, :wide] = (change * up * (sigmoid * (1.0 + gate * (1.0 - sigmoid)))).astype(
                    low
                )
                grads[rows, wide:] = (change * on).astype(low)
                return carry

            lax.fori_loop(0, count // part, middle, 0)
            if expert == 1:
                for k in range(3):
                    store(k, 0).wait()

            def weight_grads(i, carry):
                columns = pl.ds(pl.multiple_of(i * part, part), part)
                sums_one[columns, :] = contract(grads[:, columns], rows_x[expert], 0, 0)
                return carry

            lax.fori_loop(0, 2 * wide // part, weight_grads, 0)
            for i in range(wide // 128):
                columns = pl.ds(i * 128, 128)
                sums_two[columns, :] = contract(hidden[:, columns], rows_g[expert], 0, 0)
            for k in range(3):
                store(k, expert).start()

            def results(i, carry):
                rows = pl.ds(pl.multiple_of(i * part, part), part)
                rows_x[expert, rows, :] = contract(hidden[rows, :], down[...], 1, 0).astype(low)
                rows_g[expert, rows, :] = contract(grads[rows, :], gate_up[...], 1, 0).astype(low)
                return carry

            lax.fori_loop(0, count // part, results, 0)

    @pl.when(step >= blocks + 2)
    def _():
        block = step - blocks - 2
        pick = jnp.concatenate([jnp.where(f, 1.0, 0.0) for f in picks(block)], 0).astype(low)
        here = pl.ds(pl.multiple_of(block * pair_slots, pair_slots), pair_slots)

        def both(ref):
            return jnp.concatenate([ref[0, here, :], ref[1, here, :]], 0)

        routed_out[0] = contract(pick, both(rows_x), 0, 0).astype(low)
        back_out[0, :, :width] = contract(pick, both(rows_g), 0, 0).astype(low)
        back_out[0, :, width:] = contract(pick, both(dots), 0, 0).astype(low)

    @pl.when(step == 2 * blocks + 1)
    def _():
        for k in range(3):
            store(k, 1).wait()


def experts(token_rows, grad_rows, gate, up, down):
    low = jnp.bfloat16
    blocks = token_rows.shape[0]
    local, units, width = down.shape
    wide = (units + 127) // 128 * 128
    count = blocks * 48
    last = blocks - 1

    def entering(i):
        return (jnp.minimum(i, last), 0, 0)

    def leaving(i):
        return (jnp.maximum(i - blocks - 2, 0), 0, 0)

    weight = jax.ShapeDtypeStruct((local, units, width), jnp.float32)
    return pl.pallas_call(
        experts_kernel,
        grid=(2 * blocks + 2,),
        out_shape=(
            jax.ShapeDtypeStruct((blocks, 256, width), low),
            jax.ShapeDtypeStruct((blocks, 256, width + 128), low),
            weight,
            weight,
            weight,
        ),
        in_specs=[
            pl.BlockSpec((1, 256, width + 128), entering),
            pl.BlockSpec((1, 256, width), entering),
            HBM,
            HBM,
            HBM,
        ],
        out_specs=(
            pl.BlockSpec((1, 256, width), leaving),
            pl.BlockSpec((1, 256, width + 128), leaving),
            HBM,
            HBM,
            HBM,
        ),
        scratch_shapes=[
            pltpu.VMEM((blocks, 8, 256), jnp.float32),
            pltpu.VMEM((local, count, width), low),
            pltpu.VMEM((local, count, width), low),
            pltpu.VMEM((local, count, 128), jnp.float32),
            pltpu.VMEM((local, count, 128), low),
            pltpu.VMEM((3, units, width), jnp.float32),
            pltpu.VMEM((2 * wide, width), low),
            pltpu.VMEM((wide, width), low),
            pltpu.VMEM((count, wide), low),
            pltpu.VMEM((count, 2 * wide), low),
            pltpu.VMEM((2 * wide, width), jnp.float32),
            pltpu.VMEM((wide, width), jnp.float32),
            pltpu.SemaphoreType.DMA((3,)),
            pltpu.SemaphoreType.DMA((3,)),
        ],
        compiler_params=pltpu.CompilerParams(
            dimension_semantics=("arbitrary",), vmem_limit_bytes=60 * 2**20
        ),
        cost_estimate=pl.CostEstimate(
            flops=18 * local * count * wide * width,
            bytes_accessed=100 * 2**20,
            transcendentals=local * count * wide,
        ),
        name="experts",
    )(token_rows, grad_rows, gate, up, down)


def rms_forward(values, gains):
    inverse = lax.rsqrt(jnp.mean(values * values, -1, keepdims=True) + epsilon)
    return (values * inverse * gains, inverse)


def rope_tables(positions):
    half_dim = ROPE // 2
    freqs = rope_base ** (-jnp.arange(half_dim, dtype=jnp.float32) / half_dim)
    angles = positions.astype(jnp.float32)[:, None] * freqs[None, :]
    return (jnp.cos(angles), jnp.sin(angles))


HEADS = 4
SCALE = (NOPE + ROPE) ** (-0.5)


def column(row):
    shape = (128, 128)
    same = lax.broadcasted_iota(jnp.int32, shape, 0) == lanes(shape)
    return jnp.sum(jnp.where(same, row.astype(jnp.float32), 0.0), 1, keepdims=True)


def in_groups(values):
    return values.reshape(values.shape[0] // 8, 8, values.shape[1])


def lanes(shape):
    return lax.broadcasted_iota(jnp.int32, shape, 1)


def turn_tables(cosine, sine_tab):
    lane = lanes(cosine.shape)
    kept = jnp.where(lane < 64, cosine, 0.0)
    crossed = jnp.where(lane < 32, -sine_tab, jnp.where(lane < 64, sine_tab, 0.0))
    return kept, crossed


def exchange_halves(values):
    shape = (128, 128)
    to = lanes(shape)
    from_lane = lax.broadcasted_iota(jnp.int32, shape, 0)
    other = jnp.where(to < 32, to + 32, jnp.where(to < 64, to - 32, to))
    swap = jnp.where(from_lane == other, 1.0, 0.0)
    return lax.dot_general(
        values,
        swap,
        (((1,), (0,)), ((), ())),
        precision=lax.Precision.HIGHEST,
        preferred_element_type=jnp.float32,
    )


def fold_matrix():
    shape = (128, 256)
    to = lanes(shape)
    wanted = jnp.where(to >= 128, 32, 0) + lax.rem(to, 32)
    return jnp.where(lax.broadcasted_iota(jnp.int32, shape, 0) == wanted, 1.0, 0.0).astype(
        jnp.bfloat16
    )


def head_lanes(values, head):
    lane = lanes(values.shape)
    inside = jnp.logical_and(lane >= 32 * head, lane < 32 * head + 32)
    return jnp.where(inside, values, jnp.zeros_like(values))


def pack_kernel(
    query,
    latent,
    gain_one,
    gain_two,
    gain_latent,
    output,
    expand,
    gate,
    router,
    up,
    down,
    attention_out,
    ffn_out,
):
    low = jnp.bfloat16
    shard = query.shape[0]
    for head in range(HEADS):
        start = 192 * head
        attention_out[:, 128 * head : 128 * head + 128] = query[:, start : start + 128].astype(low)
    for half in (0, 1):
        starts = [192 * head + 128 + 32 * half for head in range(HEADS)]
        pieces = [query[:, start : start + 32] for start in starts]
        to = 512 + 128 * half
        attention_out[:, to : to + 128] = jnp.concatenate(pieces, 1).astype(low)
    attention_out[:, 768:1280] = latent[:, :RANK].astype(low)
    row = lax.broadcasted_iota(jnp.int32, (shard, shard), 0)
    gains = jnp.where(row == 0, gain_one[...], 0.0)
    gains = jnp.where(row == 1, gain_two[...], gains)
    rest = jnp.zeros((1, shard - gain_latent.shape[1]), jnp.float32)
    gains = jnp.where(row == 2, jnp.concatenate([gain_latent[...], rest], 1), gains)
    attention_out[:, 1280:1408] = jnp.concatenate([latent[:, RANK:], gains], 1).astype(low)
    attention_out[:, 1408:1920] = output[...].astype(low)
    for j in range(4):
        attention_out[16 * j : 16 * j + 16, 1920:] = expand[:, 256 * j : 256 * j + 256].astype(low)
    gap = jnp.zeros((shard, 64), jnp.float32)
    for k, (wide, narrow) in enumerate(((gate, router[...]), (up, gap), (down, gap))):
        start = 768 * k
        ffn_out[:, start : start + 640] = wide[:, :640].astype(low)
        ffn_out[:, start + 640 : start + 768] = jnp.concatenate(
            [wide[:, 640:704], narrow], 1
        ).astype(low)


def project_kernel(
    hidden,
    weights,
    gain,
    gain_latent,
    cosine,
    sine_tab,
    normed_out,
    query_out,
    latent_out,
    keys_out,
    key_row,
    landed,
    *scratch,
):
    low = jnp.bfloat16
    peers = reach_back_peers()
    call(peers)
    normed = rms_forward(hidden[...].astype(jnp.float32), gain[...])[0].astype(low)
    normed_out[...] = normed
    query = contract(normed, weights[:, :768], 1, 0)
    first, second = query[:, 512:640], query[:, 640:768]
    cos, sin = cosine[...], sine_tab[...]
    query_out[:, :512] = query[:, :512].astype(low)
    query_out[:, 512:640] = (first * cos - second * sin).astype(low)
    query_out[:, 640:768] = (second * cos + first * sin).astype(low)
    latent = contract(normed, weights[:, 768:1408], 1, 0)
    latent_out[...] = latent[:, :RANK]
    compressed = rms_forward(latent[:, :RANK], gain_latent[...])[0]
    key_row[:, :, :RANK] = in_groups(compressed).astype(low)
    rope = latent[:, RANK:]
    kept, crossed = turn_tables(cos, sin)
    turned = rope * kept + exchange_halves(rope) * crossed
    key_row[:, :, RANK:] = in_groups(turned).astype(low)
    hear(peers)
    reach_back_run(key_row, landed, *scratch)
    keys_out[...] = landed[...]


def attend_kernel(
    keys,
    expand_0,
    expand_1,
    query,
    own_segment,
    key_segment,
    wo_0,
    wo_1,
    wo_2,
    wo_3,
    out,
    attended,
    probs,
    expanded,
    key_rope,
    expand,
    held,
    landed,
    *scratch,
):
    low = jnp.bfloat16
    peers = line_peers()
    call(peers)
    rows = query.shape[0]
    count = keys.shape[0]
    fold = fold_matrix()
    for k, block in enumerate((expand_0, expand_1)):
        for j in range(4):
            part = block[...].reshape(32, 64, 128)[:, 16 * j : 16 * j + 16, :]
            expand[:, 256 * j + 128 * k : 256 * j + 128 * k + 128] = part.reshape(RANK, 128)

    def expand_rows(i, carry):
        part = pl.ds(pl.multiple_of(i * rows, rows), rows)
        expanded[part, :] = contract(keys[part, :RANK], expand[...], 1, 0).astype(low)
        key_rope[part, :] = contract(keys[part, RANK:], fold, 1, 0).astype(low)
        return carry

    lax.fori_loop(0, count // rows, expand_rows, 0)
    shape = (rows, count)
    distance = lax.broadcasted_iota(jnp.int32, shape, 0) + WINDOW - lanes(shape)
    allowed = jnp.logical_and(distance >= 0, distance < WINDOW)
    allowed = jnp.logical_and(allowed, own_segment[...] == key_segment[...])
    total = jnp.zeros((rows, wo_0.shape[0]), jnp.float32)
    for head, wo in enumerate((wo_0, wo_1, wo_2, wo_3)):
        start = 256 * head
        scores = contract(query[:, 128 * head : 128 * head + 128], expanded[:, start : start + 128], 1, 1)
        scores += contract(head_lanes(query[:, 512:640], head), key_rope[:, :128], 1, 1)
        scores += contract(head_lanes(query[:, 640:768], head), key_rope[:, 128:], 1, 1)
        scores = jnp.where(allowed, scores * SCALE, masked_score)
        exponent = jnp.exp(scores - jnp.max(scores, 1, keepdims=True))
        share = exponent / jnp.sum(exponent, 1, keepdims=True)
        probs[head] = share
        mixed = contract(share.astype(low), expanded[:, start + 128 : start + 256], 1, 0).astype(low)
        attended[:, 128 * head : 128 * head + 128] = mixed
        total += contract(mixed, wo[...], 1, 1)
    held[...] = in_groups(total).astype(low)
    hear(peers)
    line = Line(held, landed, *scratch)
    line.scatter()
    line.add()
    line.gather()
    line.finish()
    out[...] = landed[...]


def route_kernel(hidden, attention, gain, router, routes, token_out, middle_out, gates_out):
    low = jnp.bfloat16
    middle = hidden[...].astype(jnp.float32) + attention[...].astype(jnp.float32)
    middle_out[...] = middle
    normed = rms_forward(middle, gain[...])[0].astype(low)
    width = normed.shape[1]
    token_out[:, :width] = normed
    logits = contract(normed, router[...], 1, 0)
    lane = lanes(logits.shape).astype(jnp.float32)
    named = [column(routes[r : r + 1, :]) for r in range(6)]
    chosen = [
        jnp.sum(jnp.where(lane == number + 64, logits, 0.0), 1, keepdims=True) for number in named
    ]
    most = functools.reduce(jnp.maximum, chosen)
    exponents = [jnp.exp(value - most) for value in chosen]
    total = functools.reduce(jnp.add, exponents)
    extra = jnp.where(jnp.logical_or(lane == 6, lane == 7), 128.0, 0.0)
    gates = jnp.zeros(logits.shape, jnp.float32)
    for r in range(6):
        weight = exponents[r] / total
        high = weight.astype(low).astype(jnp.float32)
        extra += jnp.where(lane == r, named[r], 0.0)
        extra += jnp.where(lane == 8 + r, high, 0.0)
        extra += jnp.where(lane == 16 + r, weight - high, 0.0)
        gates += jnp.where(lane == r, weight, 0.0)
    token_out[:, width:] = extra.astype(low)
    gates_out[...] = gates


def shared_kernel(normed, cotangent, weights, part_out, back_out, grads_out):
    low = jnp.bfloat16
    gate = contract(normed[...], weights[:, :768], 1, 0)
    up = contract(normed[...], weights[:, 768:1536], 1, 0)
    sigmoid = 1.0 / (1.0 + jnp.exp(-gate))
    on = gate * sigmoid
    hidden = (on * up).astype(low)
    part_out[...] = contract(hidden, weights[:, 1536:], 1, 1)
    change = contract(cotangent[...], weights[:, 1536:], 1, 0)
    grad_gate = (change * up * (sigmoid * (1.0 + gate * (1.0 - sigmoid)))).astype(low)
    grad_up = (change * on).astype(low)
    width = normed.shape[1]
    back_out[:, :width] = contract(grad_gate, weights[:, :768], 1, 1) + contract(
        grad_up, weights[:, 768:1536], 1, 1
    )
    back_out[:, width:] = jnp.zeros((normed.shape[0], 128), jnp.float32)

    def grads(i, carry):
        part = pl.ds(pl.multiple_of(i * 256, 256), 256)
        rows = normed[:, part]
        grads_out[part, :768] = contract(rows, grad_gate, 0, 0).astype(low)
        grads_out[part, 768:1536] = contract(rows, grad_up, 0, 0).astype(low)
        grads_out[part, 1536:] = contract(cotangent[:, part], hidden, 0, 0).astype(low)
        return carry

    lax.fori_loop(0, grads_out.shape[0] // 256, grads, 0)


def attend_back_kernel(
    back,
    middle,
    gain,
    gates,
    routes,
    router,
    cotangent,
    wo_0,
    wo_1,
    wo_2,
    wo_3,
    probs,
    expanded,
    key_rope,
    query,
    keys,
    expand,
    query_w,
    cosine,
    sine_tab,
    normed,
    attended,
    middle_out,
    attention_out,
    gain_out,
    logits_out,
    own_out,
    query_sum_out,
    latent_sum_out,
    changes,
    ropes,
    query_out,
    back_out,
    keys_out,
    grads_out,
    held,
    near_in,
    far_in,
    ssem,
    rsem,
    pssem,
    prsem,
    latent,
    landed_one,
    landed_two,
    *scratch,
):
    low = jnp.bfloat16
    t, x, z, c = place()
    peers = plane_peers() + line_peers() + [(chip_at(x, z, c, k), t) for k in (1, 2, 3, 4)]
    call(peers)
    width = middle.shape[1]
    rows = middle.shape[0]
    lane = lanes((rows, 128)).astype(jnp.float32)
    sums = back[:, width:].astype(jnp.float32)
    named = [column(routes[r : r + 1, :]) for r in range(6)]
    weight = [gates[:, r : r + 1] for r in range(6)]
    change = [
        jnp.sum(jnp.where(lane == number + 64, sums, 0.0), 1, keepdims=True) for number in named
    ]
    inner = functools.reduce(jnp.add, [w * c for w, c in zip(weight, change)])
    logits = jnp.zeros((rows, 128), jnp.float32)
    for r in range(6):
        logits += jnp.where(lane == named[r] + 64, weight[r] * (change[r] - inner), 0.0)
    logits_low = logits.astype(low)
    logits_out[...] = logits_low
    grad_normed = back[:, :width].astype(jnp.float32) + contract(logits_low, router[...], 1, 1)
    values = middle[...]
    inverse = lax.rsqrt(jnp.mean(values * values, 1, keepdims=True) + epsilon)
    weighted = grad_normed * gain[...]
    aligned = jnp.mean(values * weighted, 1, keepdims=True)
    gain_out[...] = jnp.sum(grad_normed * values * inverse, 0, keepdims=True)
    grad_middle = (
        cotangent[...].astype(jnp.float32)
        + inverse * weighted
        - values * (inverse * inverse * inverse) * aligned
    )
    middle_out[...] = grad_middle
    grad_attn = grad_middle.astype(low)
    attention_out[...] = grad_attn
    first = jnp.zeros((rows, 128), jnp.float32)
    second = jnp.zeros((rows, 128), jnp.float32)
    for head, wo in enumerate((wo_0, wo_1, wo_2, wo_3)):
        start = 256 * head
        nope, value = slice(start, start + 128), slice(start + 128, start + 256)
        own = slice(128 * head, 128 * head + 128)
        grad_mixed = contract(grad_attn, wo[...], 1, 0).astype(low)
        share = probs[head]
        changes[:, value] = contract(share.astype(low), grad_mixed, 0, 0).astype(low)
        grad_share = contract(grad_mixed, expanded[:, value], 1, 1)
        grad_scores = share * (grad_share - jnp.sum(share * grad_share, 1, keepdims=True))
        grad_scores = grad_scores.astype(low)
        query_out[:, own] = (contract(grad_scores, expanded[:, nope], 1, 0) * SCALE).astype(low)
        both = contract(grad_scores, key_rope[...], 1, 0) * SCALE
        first += head_lanes(both[:, :128], head)
        second += head_lanes(both[:, 128:], head)
        changes[:, nope] = (contract(grad_scores, query[:, own], 0, 0) * SCALE).astype(low)
        from_first = contract(grad_scores, head_lanes(query[:, 512:640], head), 0, 0) * SCALE
        from_second = contract(grad_scores, head_lanes(query[:, 640:768], head), 0, 0) * SCALE
        if head == 0:
            ropes[:, :128] = from_first
            ropes[:, 128:] = from_second
        else:
            ropes[:, :128] += from_first
            ropes[:, 128:] += from_second
    cos, sin = cosine[...], sine_tab[...]
    query_out[:, 512:640] = (first * cos + second * sin).astype(low)
    query_out[:, 640:768] = (second * cos - first * sin).astype(low)
    back_out[...] = in_groups(contract(query_out[...], query_w[...], 1, 1)).astype(low)
    fold = fold_matrix()

    def key_rows(i, carry):
        part = pl.ds(pl.multiple_of(i * rows, rows), rows)
        compressed = contract(changes[part, :], expand[...], 1, 1)
        keys_out[i, :, :, :RANK] = in_groups(compressed).astype(low)
        rope = contract(ropes[part, :].astype(low), fold, 1, 1)
        keys_out[i, :, :, RANK:] = in_groups(rope).astype(low)
        return carry

    lax.fori_loop(0, keys.shape[0] // rows, key_rows, 0)
    hear(peers)
    back = send_back_steps(keys_out, latent, held, near_in, far_in, ssem, rsem, pssem, prsem)
    advance(back, 1)
    line_one = Line(back_out, landed_one, *scratch[:3])
    line_two = Line(latent, landed_two, *scratch[3:6])
    line_one.scatter()
    advance(back, 1)
    for j in range(4):
        grad_expand = contract(keys[:, :RANK], changes[:, 256 * j : 256 * j + 256], 0, 0)
        grads_out[:, 2 * j : 2 * j + 2, :, 1280:] = grad_expand.reshape(32, 2, 8, 256).astype(low)

    def grads(i, carry):
        part = pl.ds(pl.multiple_of(i * 256, 256), 256)
        some = pl.ds(i * 4, 4)
        of_query = contract(normed[:, part], query_out[...], 0, 0)
        grads_out[some, :, :, :768] = of_query.reshape(4, 8, 8, 768).astype(low)
        of_output = contract(attention_out[:, part], attended[...], 0, 0)
        grads_out[some, :, :, 768:1280] = of_output.reshape(4, 8, 8, 512).astype(low)
        return carry

    lax.fori_loop(0, width // 256, grads, 0)

    def emit(i, total):
        own_out[i] = total

    plane = plane_sum_steps(grads_out, emit, scratch[6:])
    advance(plane, 1)
    line_one.add()
    line_one.gather()
    advance(plane, 4)
    advance(back, 1)
    line_two.scatter()
    advance(plane, 8)
    line_two.add()
    line_two.gather()
    advance(plane, PLANE_STEPS - 13)
    line_one.finish()
    query_sum_out[...] = landed_one[...]
    line_two.finish()
    latent_sum_out[...] = landed_two[...]
    advance(back, 1)
    advance(plane, 1)


def finish_kernel(
    query_sum,
    latent_sum,
    latent,
    gain_latent,
    cosine,
    sine_tab,
    wl_0,
    wl_1,
    wl_2,
    wl_3,
    wl_4,
    hidden,
    gain,
    grad_middle,
    normed,
    normed_two,
    grad_logits,
    gain_two_grad,
    routed,
    shared,
    input_out,
    own_out,
    layer_out,
    changes,
    grads_out,
    landed,
    layer,
    *scratch,
):
    low = jnp.bfloat16
    peers = plane_peers() + line_peers()
    call(peers)
    grad_latent = latent_sum[:, :RANK].astype(jnp.float32)
    rope = latent_sum[:, RANK:].astype(jnp.float32)
    values = latent[...]
    inverse = lax.rsqrt(jnp.mean(values * values, 1, keepdims=True) + epsilon)
    weighted = grad_latent * gain_latent[...]
    aligned = jnp.mean(values * weighted, 1, keepdims=True)
    gain_latent_grad = jnp.sum(grad_latent * values * inverse, 0, keepdims=True)
    changes[:, :RANK] = (
        inverse * weighted - values * (inverse * inverse * inverse) * aligned
    ).astype(low)
    kept, crossed = turn_tables(cosine[...], sine_tab[...])
    changes[:, RANK:] = (rope * kept - exchange_halves(rope) * crossed).astype(low)
    grad_normed = query_sum[...].astype(jnp.float32)
    width = hidden.shape[1]
    for j, wl in enumerate((wl_0, wl_1, wl_2, wl_3, wl_4)):
        grad_normed += contract(changes[:, 128 * j : 128 * j + 128], wl[...], 1, 1)
    values = hidden[...].astype(jnp.float32)
    inverse = lax.rsqrt(jnp.mean(values * values, 1, keepdims=True) + epsilon)
    weighted = grad_normed * gain[...]
    aligned = jnp.mean(values * weighted, 1, keepdims=True)
    gain_grad = jnp.sum(grad_normed * values * inverse, 0, keepdims=True)
    input_out[...] = (
        grad_middle[...] + inverse * weighted - values * (inverse * inverse * inverse) * aligned
    ).astype(low)

    def grads(i, carry):
        part = pl.ds(pl.multiple_of(i * 256, 256), 256)
        some = pl.ds(i * 4, 4)
        rows = normed[:, part]
        of_latent = contract(rows, changes[:, :RANK], 0, 0)
        grads_out[some, :, :, :RANK] = of_latent.reshape(4, 8, 8, RANK).astype(low)
        mixed = contract(rows, changes[:, RANK:], 0, 0)
        mixed += contract(normed_two[:, part], grad_logits[...], 0, 0)
        grads_out[some, :, :, RANK : RANK + 128] = mixed.reshape(4, 8, 8, 128).astype(low)
        return carry

    lax.fori_loop(0, width // 256, grads, 0)
    grads_out[:, 1:, :, RANK + 128 :] = jnp.zeros((32, 7, 8, 128), low)
    line_number = lax.broadcasted_iota(jnp.int32, (8, 128), 0)
    gain_two = gain_two_grad[...]
    for e in range(32):
        block = jnp.zeros((8, 128), jnp.float32)
        for row, (values, size) in enumerate(
            ((gain_grad, 64), (gain_two, 64), (gain_latent_grad, 16))
        ):
            piece = values[:, size * e : size * e + size]
            piece = jnp.concatenate([piece, jnp.zeros((1, 128 - size), jnp.float32)], 1)
            block = jnp.where(line_number == row, piece, block)
        grads_out[e, 0, :, RANK + 128 :] = block.astype(low)
    layer[...] = (routed[...].astype(jnp.float32) + shared[...]).astype(low)
    hear(peers)
    line = Line(layer, landed, *scratch[:3])
    line.scatter()

    def emit(i, total):
        own_out[i] = total

    plane = plane_sum_steps(grads_out, emit, scratch[3:])
    advance(plane, 10)
    line.add()
    line.gather()
    advance(plane, PLANE_STEPS)
    line.finish()
    layer_out[...] = landed[...]


def unpack_kernel(
    own,
    last,
    ffn,
    middle,
    layer,
    grad_in,
    layer_out,
    grad_in_out,
    query_out,
    latent_out,
    router_out,
    output_out,
    gain_one_out,
    gain_two_out,
    gain_latent_out,
    expand_out,
    gate_out,
    up_out,
    down_out,
):
    layer_out[...] = (middle[...] + layer[...].astype(jnp.float32)).astype(layer_out.dtype)
    grad_in_out[...] = grad_in[...]
    for head in range(HEADS):
        query_out[:, 192 * head : 192 * head + 128] = own[:, 128 * head : 128 * head + 128]
        for half in (0, 1):
            to, start = 192 * head + 128 + 32 * half, 512 + 128 * half + 32 * head
            query_out[:, to : to + 32] = own[:, start : start + 32]
    latent_out[...] = last[:, :576]
    router_out[...] = last[:, 576:640]
    output_out[...] = own[:, 768:1280]
    gain_one_out[...] = last[0:1, 640:704]
    gain_two_out[...] = last[1:2, 640:704]
    gain_latent_out[...] = last[2:3, 640:656]
    for j in range(4):
        expand_out[:, 256 * j : 256 * j + 256] = own[16 * j : 16 * j + 16, 1280:1536]
    gate_out[...] = ffn[:, :704].astype(jnp.float32)
    up_out[...] = ffn[:, 768:1472].astype(jnp.float32)
    down_out[...] = ffn[:, 1536:2240].astype(jnp.float32)


def local_call(kernel, name, operands, out_shapes, scratch=()):
    arrays, specs = [], []
    for operand in operands:
        if isinstance(operand, tuple):
            array, block, index = operand
            specs.append(pl.BlockSpec(block, lambda i, index=index: index))
        else:
            array = operand
            zeros = (0,) * array.ndim
            specs.append(pl.BlockSpec(array.shape, lambda i, zeros=zeros: zeros))
        arrays.append(array)
    shapes = [jax.ShapeDtypeStruct(shape, dtype) for shape, dtype in out_shapes]
    return pl.pallas_call(
        kernel,
        grid=(1,),
        out_shape=shapes,
        in_specs=specs,
        out_specs=[
            pl.BlockSpec(shape.shape, lambda i, zeros=(0,) * len(shape.shape): zeros)
            for shape in shapes
        ],
        scratch_shapes=[pltpu.VMEM(shape, dtype) for shape, dtype in scratch],
        compiler_params=pltpu.CompilerParams(vmem_limit_bytes=60 * 2**20),
        name=name,
    )(*arrays)


def joint_call(kernel, collective_id, name, operands, out_shapes, scratch, moved):
    arrays, specs = [], []
    for operand in operands:
        if isinstance(operand, tuple):
            array, block, index = operand
        else:
            array, block, index = operand, operand.shape, (0,) * operand.ndim
        specs.append(
            pl.BlockSpec(block, lambda i, index=index: index, pipeline_mode=pl.Buffered(1))
        )
        arrays.append(array)
    return pl.pallas_call(
        kernel,
        grid=(1,),
        out_shape=[jax.ShapeDtypeStruct(shape, dtype) for shape, dtype in out_shapes],
        in_specs=specs,
        out_specs=[
            pl.BlockSpec(
                shape,
                lambda i, zeros=(0,) * len(shape): zeros,
                pipeline_mode=pl.Buffered(1),
            )
            for shape, _ in out_shapes
        ],
        scratch_shapes=scratch,
        compiler_params=pltpu.CompilerParams(
            collective_id=collective_id, has_side_effects=True, vmem_limit_bytes=60 * 2**20
        ),
        cost_estimate=pl.CostEstimate(flops=0, bytes_accessed=moved, transcendentals=0),
        name=name,
    )(*arrays)


def column_blocks(array, first, number):
    return [(array, (array.shape[0], 128), (0, first + j)) for j in range(number)]


def body(
    hidden_in,
    cotangent,
    segments,
    routes,
    attn_norm,
    w_query,
    w_latent,
    latent_norm,
    w_expand,
    w_output,
    ffn_norm,
    w_router,
    shared_gate,
    shared_up,
    shared_down,
    expert_gate,
    routed_expert_up,
    expert_down,
):
    tokens, model_width = hidden_in.shape
    devices = lax.axis_size("expert")
    own_index = lax.axis_index("expert")
    low = jnp.bfloat16
    full = jnp.float32
    shard = w_query.shape[0]

    attention_shard, ffn_shard = local_call(
        pack_kernel,
        "pack",
        (
            w_query,
            w_latent,
            attn_norm[None],
            ffn_norm[None],
            latent_norm[None],
            w_output.T,
            w_expand,
            shared_gate,
            w_router,
            shared_up,
            shared_down.T,
        ),
        (((shard, 2176), low), ((shard, 2304), low)),
    )
    ffn_all = lax.all_gather(ffn_shard, "expert", axis=0, tiled=True)
    grad_rows = lax.all_gather(cotangent, "expert", axis=0)
    attention_all = plane_gather(attention_shard, 1, "gather_attention")
    gains = attention_all.reshape(devices, shard, -1)[:, :8, 1344:1408].astype(full)
    gain_one = gains[:, 0].reshape(1, -1)
    gain_two = gains[:, 1].reshape(1, -1)
    gain_latent = gains[:, 2, : latent_norm.shape[0]].reshape(1, -1)
    output_blocks = column_blocks(attention_all, 11, 4)
    latent_blocks = column_blocks(attention_all, 6, 5)
    router_block = column_blocks(ffn_all, 5, 1)[0]

    first_row = own_index * tokens
    row_index = first_row + jnp.arange(tokens, dtype=jnp.int32)
    own_segments = lax.dynamic_slice_in_dim(segments, first_row, tokens)
    doc_start = jnp.sum((segments[None, :] < own_segments[:, None]).astype(jnp.int32), 1)
    cosine, sine_tab = rope_tables(row_index - doc_start)
    cosine, sine_tab = jnp.tile(cosine, (1, 4)), jnp.tile(sine_tab, (1, 4))
    key_count = 9 * tokens
    normed, queries, latent, keys_all = joint_call(
        project_kernel,
        2,
        "project",
        (
            hidden_in,
            (attention_all, (model_width, 1408), (0, 0)),
            gain_one,
            gain_latent,
            cosine,
            sine_tab,
        ),
        (
            ((tokens, model_width), low),
            ((tokens, 768), low),
            ((tokens, RANK), full),
            ((9, tokens // 8, 8, 640), low),
        ),
        [
            pltpu.VMEM((tokens // 8, 8, 640), low),
            pltpu.VMEM((9, tokens // 8, 8, 640), low),
            pltpu.SemaphoreType.DMA,
            pltpu.SemaphoreType.DMA((4,)),
            pltpu.SemaphoreType.DMA((4,)),
            pltpu.SemaphoreType.DMA((4,)),
            pltpu.SemaphoreType.DMA((4,)),
        ],
        2**25,
    )
    keys_all = keys_all.reshape(key_count, 640)
    key_segments = lax.dynamic_slice_in_dim(
        jnp.pad(segments, (key_count - tokens, 0), constant_values=-1), first_row, key_count
    )
    attn_out, attended, probs, expanded, key_rope, expand_w = joint_call(
        attend_kernel,
        3,
        "attend",
        (
            keys_all,
            *column_blocks(attention_all, 15, 2),
            queries,
            own_segments[:, None],
            key_segments[None],
            *output_blocks,
        ),
        (
            ((tokens // 8, 8, model_width), low),
            ((tokens, HEADS * VH), low),
            ((HEADS, tokens, key_count), full),
            ((key_count, HEADS * (NOPE + VH)), low),
            ((key_count, 256), low),
            ((RANK, HEADS * (NOPE + VH)), low),
        ),
        [pltpu.VMEM((tokens // 8, 8, model_width), low)] * 2
        + line_scratch(tokens // 8, model_width),
        2**25,
    )
    attn_out = attn_out.reshape(tokens, model_width)

    route_rows = routes.T
    token_row, middle, gates = local_call(
        route_kernel,
        "route",
        (hidden_in, attn_out, gain_two, router_block, route_rows),
        (
            ((tokens, model_width + 128), low),
            ((tokens, model_width), full),
            ((tokens, 128), full),
        ),
    )
    normed_two = (token_row, (tokens, model_width), (0, 0))

    shared_part, shared_back, ffn_grads = local_call(
        shared_kernel,
        "shared",
        (normed_two, cotangent, ffn_all),
        (
            ((tokens, model_width), full),
            ((tokens, model_width + 128), full),
            (ffn_all.shape, low),
        ),
    )
    own_ffn = lax.psum_scatter(ffn_grads, "expert", scatter_dimension=0, tiled=True)
    token_row, _ = lax.optimization_barrier((token_row, ffn_grads))
    token_rows = plane_gather(token_row, 4, "gather_tokens")

    routed_part, back_part, out_egate, out_eup, out_edown = experts(
        token_rows.reshape(devices // 2, 2 * tokens, -1),
        grad_rows.reshape(devices // 2, 2 * tokens, -1),
        expert_gate.swapaxes(1, 2),
        routed_expert_up.swapaxes(1, 2),
        expert_down,
    )
    out_egate, out_eup = out_egate.swapaxes(1, 2), out_eup.swapaxes(1, 2)
    routed_part, own_ffn = lax.optimization_barrier((routed_part, own_ffn))
    routed_own = lax.psum_scatter(
        routed_part.reshape(-1, model_width), "expert", scatter_dimension=0, tiled=True
    )
    back_all = sum_tokens(back_part.reshape(devices * tokens, -1), shared_back, 5)

    (
        grad_middle,
        grad_attn,
        grad_gain_two,
        grad_logits,
        own,
        query_sum,
        latent_sum,
    ) = joint_call(
        attend_back_kernel,
        7,
        "attend_back",
        (
            back_all,
            middle,
            gain_two,
            gates,
            route_rows,
            router_block,
            cotangent,
            *output_blocks,
            probs,
            expanded,
            key_rope,
            queries,
            keys_all,
            expand_w,
            (attention_all, (model_width, 768), (0, 0)),
            cosine,
            sine_tab,
            normed,
            attended,
        ),
        (
            ((tokens, model_width), full),
            ((tokens, model_width), low),
            ((1, model_width), full),
            ((tokens, 128), low),
            ((shard // 8, 8, 1536), full),
            ((tokens // 8, 8, model_width), low),
            ((tokens // 8, 8, 640), low),
        ),
        [
            pltpu.VMEM((key_count, HEADS * (NOPE + VH)), low),
            pltpu.VMEM((key_count, 256), full),
            pltpu.VMEM((tokens, 768), low),
            pltpu.VMEM((tokens // 8, 8, model_width), low),
            pltpu.VMEM((9, tokens // 8, 8, 640), low),
            pltpu.VMEM((devices, shard // 8, 8, 1536), low),
            pltpu.VMEM((5, tokens // 8, 8, 640), low),
            pltpu.VMEM((4, tokens // 8, 8, 640), low),
            pltpu.VMEM((4, tokens // 8, 8, 640), low),
            pltpu.SemaphoreType.DMA((4,)),
            pltpu.SemaphoreType.DMA((4,)),
            pltpu.SemaphoreType.DMA((4,)),
            pltpu.SemaphoreType.DMA((4,)),
            pltpu.VMEM((tokens // 8, 8, 640), low),
            pltpu.VMEM((tokens // 8, 8, model_width), low),
            pltpu.VMEM((tokens // 8, 8, 640), low),
        ]
        + line_scratch(tokens // 8, model_width)
        + line_scratch(tokens // 8, 640)
        + plane_scratch(shard // 8, 1536),
        2**26,
    )
    own = own.reshape(shard, 1536)
    query_sum = query_sum.reshape(tokens, model_width)
    latent_sum = latent_sum.reshape(tokens, 640)
    grad_input, own_last, layer_sum = joint_call(
        finish_kernel,
        9,
        "finish",
        (
            query_sum,
            latent_sum,
            latent,
            gain_latent,
            cosine,
            sine_tab,
            *latent_blocks,
            hidden_in,
            gain_one,
            grad_middle,
            normed,
            normed_two,
            grad_logits,
            grad_gain_two,
            by_group(routed_own),
            by_group(shared_part),
        ),
        (
            ((tokens, model_width), low),
            ((shard // 8, 8, 768), full),
            ((tokens // 8, 8, model_width), low),
        ),
        [
            pltpu.VMEM((tokens, 640), low),
            pltpu.VMEM((devices, shard // 8, 8, 768), low),
            pltpu.VMEM((tokens // 8, 8, model_width), low),
            pltpu.VMEM((tokens // 8, 8, model_width), low),
        ]
        + line_scratch(tokens // 8, model_width)
        + plane_scratch(shard // 8, 768),
        2**25,
    )
    own_last = own_last.reshape(shard, 768)
    layer_sum = layer_sum.reshape(tokens, model_width)
    (
        layer_out,
        grad_input,
        out_query,
        out_latent,
        out_router,
        out_output,
        out_gain_one,
        out_gain_two,
        out_gain_latent,
        out_expand,
        out_sgate,
        out_sup,
        out_sdown,
    ) = local_call(
        unpack_kernel,
        "unpack",
        (own, own_last, own_ffn, middle, layer_sum, grad_input),
        (
            ((tokens, model_width), low),
            ((tokens, model_width), low),
            (w_query.shape, full),
            (w_latent.shape, full),
            (w_router.shape, full),
            ((shard, w_output.shape[0]), full),
            ((1, shard), full),
            ((1, shard), full),
            ((1, latent_norm.shape[0]), full),
            (w_expand.shape, full),
            (shared_gate.shape, full),
            (shared_up.shape, full),
            ((shard, shared_down.shape[0]), full),
        ),
    )
    return (
        layer_out,
        grad_input,
        out_gain_one.reshape(-1),
        out_query,
        out_latent,
        out_gain_latent.reshape(-1),
        out_expand,
        out_output.T,
        out_gain_two.reshape(-1),
        out_router,
        out_sgate,
        out_sup,
        out_sdown.T,
        out_egate,
        out_eup,
        out_edown,
    )


def solution(mesh):
    in_specs = (
        P("expert", None),
        P("expert", None),
        P(),
        P("expert", None),
        P("expert"),
        P("expert", "tensor"),
        P("expert", None),
        P("expert"),
        P("expert", "tensor"),
        P("tensor", "expert"),
        P("expert"),
        P("expert", None),
        P("expert", "tensor"),
        P("expert", "tensor"),
        P("tensor", "expert"),
        P("expert", None, "tensor"),
        P("expert", None, "tensor"),
        P("expert", "tensor", None),
    )
    out_specs = (
        P("expert", None),
        P("expert", None),
        P("expert"),
        P("expert", "tensor"),
        P("expert", None),
        P("expert"),
        P("expert", "tensor"),
        P("tensor", "expert"),
        P("expert"),
        P("expert", None),
        P("expert", "tensor"),
        P("expert", "tensor"),
        P("tensor", "expert"),
        P("expert", None, "tensor"),
        P("expert", None, "tensor"),
        P("expert", "tensor", None),
    )
    return jax.shard_map(body, mesh=mesh, in_specs=in_specs, out_specs=out_specs, check_vma=False)
```
